128 devices in a mesh: ty: 8 (over x_lo, y), tx: 8 (over z, x_hi), slide: 2 (over core).
Axes of the slice: x: 4 (x_hi: 2, x_lo: 2; x = x_hi * 2 + x_lo), y: 4, z: 4, core: 2. Of those that a mesh axis runs over, the one named last changes fastest.
Arguments:
- tokens: bfloat16 [16, 8, 192, 768], P(('slide', 'ty'), 'tx'), parts along dimension 0, may hold values from -6 to 6
- summary: bfloat16 [2048, 768], P(('slide', 'ty', 'tx')), parts along dimension 0, may hold values from -6 to 6
- counts: int32 [16, 8], P('slide'), parts along dimension 0, may hold values from 1 to 192, as said below
- tile_pattern: int32 [16, 8, 9], P('slide'), parts along dimension 0, may hold values from 0 to 1, as said below
- summary_pattern: int32 [16, 8, 8], P(('slide', 'ty'), 'tx'), parts along dimension 0, may hold values 0 or 1
- norm_gain: float32 [768], replicated, may hold values from 0.1 to 1.9
- projections: bfloat16 [4, 768, 768], replicated, may hold values from -4 to 4
- cotangent: bfloat16 [16, 8, 192, 768], P(('slide', 'ty'), 'tx'), parts along dimension 0, may hold values from -6 to 6
Outputs:
- updated: bfloat16 [16, 8, 192, 768], P(('slide', 'ty'), 'tx'), parts along dimension 0
- grad_tokens: bfloat16 [16, 8, 192, 768], P(('slide', 'ty'), 'tx'), parts along dimension 0
- grad_summary: bfloat16 [2048, 768], P(('slide', 'ty', 'tx')), parts along dimension 0
- grad_proj: float32 [8, 768, 768], P('slide'), parts along dimension 0
- grad_gain: float32 [1536], P('slide'), parts along dimension 0
The draws below stay inside these ranges and needn't reach their ends.
There are 2 independent parts, one for each index of `slide`. The reference program is written for one: setup_inputs(seed, part) draws one part's arguments, and reference() takes and returns one part's arrays. A program takes and returns all parts, laid end to end along the dimension named above; an argument that names none is the same for every part. Nothing has to cross between parts.
Inputs may be any that keep to these rules, and one draw needn't show every extreme that they name: `counts`: some tile holds exactly 192 tokens and some tile exactly 1 in every draw. `tile_pattern`: entry 4, the tile itself, is always 1.
All inputs are finite; a program needn't handle non-finite values. No bound on the sum of `summary_pattern` on one device may be relied on, other than what follows from the above.
Results may differ from the reference program's by a relative error of at most 0.011.
Values may be sent and summed in bfloat16 or wider, within the bound.
A program may use at most 128 MiB of HBM per device.

```python
import math
import jax
import jax.numpy as jnp
from jax import lax

D = 768
HEADS = 12
TILE = 192
SBLK = 128
SUMMARIES = 1024
SUM_BLOCKS = 8
N_TY = 8
N_TX = 8


def draw_counts(key, part):
    draw_one, draw_two, draw_three, draw_four = jax.random.split(jax.random.fold_in(key, 11), 4)
    dense_count = jax.random.randint(draw_one, (N_TY * N_TX,), 1, TILE + 1)
    sparse_count = jax.random.randint(draw_two, (N_TY * N_TX,), 1, TILE // 8 + 1)
    selector = jax.random.randint(draw_three, (N_TY * N_TX,), 0, 4)
    values = jnp.where(selector == 0, sparse_count, dense_count)
    position = jax.random.randint(draw_four, (), 0, N_TY * N_TX)
    values = values.at[position].set(TILE)
    values = values.at[(position + 1) % (N_TY * N_TX)].set(1)
    return values.reshape(N_TY, N_TX).astype(jnp.int32)


def draw_tile_pattern(key, part):
    raw_draws = jax.random.randint(jax.random.fold_in(key, 23), (N_TY, N_TX, 9), 0, 4)
    pattern = (raw_draws > 0).astype(jnp.int32)
    return pattern.at[:, :, 4].set(1)


def draw_projections(key, part):
    draw_one = jax.random.fold_in(jax.random.fold_in(key, 37), 0)
    weights = jax.random.normal(draw_one, (4, D, D), jnp.float32) * D ** (-0.5)
    return jnp.clip(weights, -4.0, 4.0).astype(jnp.bfloat16)


def touch_ends(drawn, rng, smallest, top_value):
    longest = drawn.shape.index(max(drawn.shape))
    spots = []
    for shift in (0, 1):
        where = [jax.random.randint(jax.random.fold_in(rng, axis), (), 0, length) for axis, length in enumerate(drawn.shape)]
        where[longest] = (where[longest] + shift) % drawn.shape[longest]
        spots.append(tuple(where))
    return drawn.at[spots[0]].set(smallest).at[spots[1]].set(top_value)


def steps_of(own_key, dims, cuts, low, high):
    level = 1.0
    for dim, shards_of in cuts:
        draws = jax.random.uniform(jax.random.fold_in(jax.random.fold_in(own_key, 6), dim), (shards_of,), jnp.float32, low / len(cuts), high / len(cuts))
        level = level * jnp.repeat(jnp.exp(draws), dims[dim] // shards_of).reshape((-1,) + (1,) * (len(dims) - 1 - dim))
    return level


def scatter_about(rng, extent, scale, reach, cuts=(), kind=jnp.bfloat16):
    values = jax.random.normal(rng, extent, jnp.float32) * scale
    if len(cuts) > 0:
        values = steps_of(rng, extent, cuts, -0.22, 0.18) * values
    return jnp.clip(values, min=-reach, max=reach).astype(kind)


def setup_inputs(seed: int = 0, part: int = 0) -> dict:
    streams_of = jax.random.split(jax.random.key(seed), 9)
    part_splits = jax.random.split(jax.random.fold_in(streams_of[8], part), 9)
    tokens = scatter_about(part_splits[0], (N_TY, N_TX, TILE, D), 1.0, 6.0, ((0, 8), (1, 8)))
    summary = scatter_about(part_splits[1], (SUMMARIES, D), 1.0, 6.0, ((0, 64),))
    counts = draw_counts(jax.random.fold_in(jax.random.fold_in(streams_of[8], part), 71), part)
    tile_pattern = draw_tile_pattern(jax.random.fold_in(jax.random.fold_in(streams_of[8], part), 71), part)
    summary_pattern = touch_ends((jax.random.randint(part_splits[4], (N_TY, N_TX, SUM_BLOCKS), 0, 4) < 3).astype(jnp.int32), jax.random.fold_in(part_splits[4], 1), 0, 1)
    norm_gain = jnp.clip(1.0 + 0.18 * jax.random.normal(streams_of[5], (D,), jnp.float32), 0.1, 1.9)
    projections = draw_projections(jax.random.fold_in(streams_of[8], 71), part)
    cotangent = scatter_about(part_splits[7], (N_TY, N_TX, TILE, D), 1.0, 6.0, ((0, 8), (1, 8)))
    return dict(tokens=tokens, summary=summary, counts=counts, tile_pattern=tile_pattern, summary_pattern=summary_pattern, norm_gain=norm_gain, projections=projections, cotangent=cotangent)


epsilon = 1e-05

def rounded(values):
    return lax.optimization_barrier(values.astype(jnp.bfloat16)).astype(jnp.float32)

def normalize(rows, gain):
    values = rows.astype(jnp.float32)
    scale = lax.rsqrt(lax.optimization_barrier(jnp.mean(values * values, axis=-1, keepdims=True)) + epsilon)
    return ((values * scale * gain).astype(jnp.bfloat16), scale)

def norm_back(rows, scale, gain, grad_norm):
    values = rows.astype(jnp.float32)
    scaled = gain * grad_norm
    return scale * scaled - values * scale ** 3 * lax.optimization_barrier(jnp.mean(values * scaled, axis=-1, keepdims=True))

def project(rows, weight):
    return jnp.dot(rows, weight, preferred_element_type=jnp.float32).astype(jnp.bfloat16)

def back_project(rows, weight):
    return jnp.dot(rows, weight.T, preferred_element_type=jnp.float32)

def exact_back(rows, weight):
    return jnp.dot(rows, weight.astype(jnp.float32).T, precision=lax.Precision.HIGHEST)

def contract_rows(left, right):
    return lax.dot_general(left, right, (((0,), (0,)), ((), ())), preferred_element_type=jnp.float32)

def exact_rows(left, right):
    return lax.dot_general(left.astype(jnp.float32), right, (((0,), (0,)), ((), ())), precision=lax.Precision.HIGHEST)

def reference(tokens, summary, counts, tile_pattern, summary_pattern, norm_gain, projections, cotangent):
    head_size = D // HEADS
    factor = 1.0 / math.sqrt(head_size)
    near_rows = 9 * TILE
    total_keys = near_rows + SUMMARIES
    token_rows = tokens.reshape(-1, D)
    hidden, row_scale = normalize(token_rows, norm_gain)
    summary_hidden, summary_scale = normalize(summary, norm_gain)
    w_query, w_key, w_value, w_out = (projections[0], projections[1], projections[2], projections[3])
    grid_shape = (N_TY, N_TX, TILE, D)
    queries = project(hidden, w_query).reshape(grid_shape)
    keys = project(hidden, w_key).reshape(grid_shape)
    values = project(hidden, w_value).reshape(grid_shape)
    summary_keys = project(summary_hidden, w_key)
    summary_values = project(summary_hidden, w_value)
    grid_pad = ((1, 1), (1, 1), (0, 0), (0, 0))
    key_pad = jnp.pad(keys, grid_pad)
    value_pad = jnp.pad(values, grid_pad)
    count_pad = jnp.pad(counts, 1)
    positions = jnp.arange(TILE, dtype=jnp.int32)

    def visit_tile(running, tile_index):
        grid_kgrad, grid_vgrad, summ_kgrad, summ_vgrad, out_grad = running
        zero = jnp.zeros((), jnp.int32)
        grid_row = (tile_index // N_TX).astype(jnp.int32)
        grid_col = (tile_index % N_TX).astype(jnp.int32)
        corner = (grid_row, grid_col, zero, zero)
        near_keys = lax.dynamic_slice(key_pad, corner, (3, 3, TILE, D)).reshape(near_rows, D)
        near_values = lax.dynamic_slice(value_pad, corner, (3, 3, TILE, D)).reshape(near_rows, D)
        near_counts = lax.dynamic_slice(count_pad, (grid_row, grid_col), (3, 3)).reshape(9)
        tile_flags = lax.dynamic_slice(tile_pattern, (grid_row, grid_col, zero), (1, 1, 9)).reshape(9)
        tile_ok = ((positions[None, :] < near_counts[:, None]) & (tile_flags[:, None] == 1)).reshape(near_rows)
        summ_flags = lax.dynamic_slice(summary_pattern, (grid_row, grid_col, zero), (1, 1, SUMMARIES // SBLK)).reshape(-1)
        summ_ok = jnp.repeat(summ_flags == 1, SBLK)
        allowed = jnp.concatenate([tile_ok, summ_ok])
        all_keys = jnp.concatenate([near_keys, summary_keys]).astype(jnp.float32).reshape(total_keys, HEADS, head_size)
        all_values = jnp.concatenate([near_values, summary_values]).astype(jnp.float32).reshape(total_keys, HEADS, head_size)
        query_here = lax.dynamic_slice(queries, corner, (1, 1, TILE, D)).reshape(TILE, HEADS, head_size).astype(jnp.float32)
        scores = jnp.einsum('qhd,khd->hqk', query_here, all_keys) * factor
        scores = jnp.where(allowed[None, None, :], scores, -jnp.inf)
        largest = lax.optimization_barrier(jnp.max(scores, axis=-1, keepdims=True))
        exponent = jnp.exp(scores - largest)
        denominator = lax.optimization_barrier(jnp.sum(exponent, axis=-1, keepdims=True))
        weights_full = exponent / denominator
        weights_half = rounded(weights_full)
        attended = jnp.einsum('hqk,khd->qhd', weights_half, all_values).reshape(TILE, D).astype(jnp.bfloat16)
        own_count = near_counts[4]
        row_mask = (positions < own_count).astype(jnp.float32)[:, None]
        rows_here = lax.dynamic_slice(tokens, corner, (1, 1, TILE, D)).reshape(TILE, D)
        updated = (rows_here.astype(jnp.float32) + row_mask * jnp.dot(attended, w_out, preferred_element_type=jnp.float32)).astype(jnp.bfloat16)
        grads_here = lax.dynamic_slice(cotangent, corner, (1, 1, TILE, D)).reshape(TILE, D)
        masked = (grads_here.astype(jnp.float32) * row_mask).astype(jnp.bfloat16)
        out_grad = out_grad + contract_rows(attended, masked)
        attended_grad = rounded(back_project(masked, w_out)).reshape(TILE, HEADS, head_size)
        grad_weights = jnp.einsum('qhd,khd->hqk', attended_grad, all_values)
        row_delta = lax.optimization_barrier(jnp.sum(weights_full * grad_weights, axis=-1, keepdims=True))
        grad_scores = rounded(weights_full * (grad_weights - row_delta))
        query_grad = (jnp.einsum('hqk,khd->qhd', grad_scores, all_keys) * factor).reshape(TILE, D).astype(jnp.bfloat16)
        key_grads = (jnp.einsum('hqk,qhd->khd', grad_scores, query_here) * factor).reshape(total_keys, D)
        value_grads = jnp.einsum('hqk,qhd->khd', weights_half, attended_grad).reshape(total_keys, D)
        grid_kgrad = lax.dynamic_update_slice(grid_kgrad, lax.dynamic_slice(grid_kgrad, corner, (3, 3, TILE, D)) + key_grads[:near_rows].reshape(3, 3, TILE, D), corner)
        grid_vgrad = lax.dynamic_update_slice(grid_vgrad, lax.dynamic_slice(grid_vgrad, corner, (3, 3, TILE, D)) + value_grads[:near_rows].reshape(3, 3, TILE, D), corner)
        summ_kgrad = summ_kgrad + key_grads[near_rows:]
        summ_vgrad = summ_vgrad + value_grads[near_rows:]
        return ((grid_kgrad, grid_vgrad, summ_kgrad, summ_vgrad, out_grad), (updated, query_grad))
    start_state = (jnp.zeros((N_TY + 2, N_TX + 2, TILE, D), jnp.float32), jnp.zeros((N_TY + 2, N_TX + 2, TILE, D), jnp.float32), jnp.zeros((SUMMARIES, D), jnp.float32), jnp.zeros((SUMMARIES, D), jnp.float32), jnp.zeros((D, D), jnp.float32))
    final_state, stacked = lax.scan(visit_tile, start_state, jnp.arange(N_TY * N_TX, dtype=jnp.int32))
    grid_kgrad, grid_vgrad, summ_kgrad, summ_vgrad, out_grad = final_state
    updated = stacked[0].reshape(tokens.shape)
    query_grad = stacked[1].reshape(-1, D)
    key_grad = grid_kgrad[1:-1, 1:-1].reshape(-1, D).astype(jnp.bfloat16)
    value_grad = grid_vgrad[1:-1, 1:-1].reshape(-1, D).astype(jnp.bfloat16)
    summary_key_grad = summ_kgrad
    summary_value_grad = summ_vgrad
    hidden_grad = back_project(query_grad, w_query) + back_project(key_grad, w_key) + back_project(value_grad, w_value)
    summary_hidden_grad = exact_back(summary_key_grad, w_key) + exact_back(summary_value_grad, w_value)
    grad_proj = jnp.stack([contract_rows(hidden, query_grad), contract_rows(hidden, key_grad) + exact_rows(summary_hidden, summary_key_grad), contract_rows(hidden, value_grad) + exact_rows(summary_hidden, summary_value_grad), out_grad])
    grad_gain = lax.optimization_barrier(jnp.sum(hidden_grad * token_rows.astype(jnp.float32) * row_scale, axis=0)) + lax.optimization_barrier(jnp.sum(summary_hidden_grad * summary.astype(jnp.float32) * summary_scale, axis=0))
    grad_tokens = (cotangent.reshape(-1, D).astype(jnp.float32) + norm_back(token_rows, row_scale, norm_gain, hidden_grad)).astype(jnp.bfloat16).reshape(tokens.shape)
    grad_summary = norm_back(summary, summary_scale, norm_gain, summary_hidden_grad).astype(jnp.bfloat16)
    return (updated, grad_tokens, grad_summary, grad_proj, grad_gain)
```

```python
import math

import jax
import jax.numpy as jnp
from jax import lax
from jax.experimental import pallas as pl
from jax.experimental.pallas import tpu as pltpu
from jax.sharding import Mesh
from jax.sharding import PartitionSpec as P

HEADS = 12
SBLK = 128
QUAD = 4
CHUNK = 256
PACK = 16
NEAR = 9
TY = ("ty_0", "ty_1")
TX = ("tx_0", "tx_1")
TY_TX = ("ty_0", "ty_1", "tx_0", "tx_1")
SLIDE_TY = ("slide", "ty_0", "ty_1")
SLIDE_TY_TX = ("slide", "ty_0", "ty_1", "tx_0", "tx_1")
F32 = jnp.float32
BF16 = jnp.bfloat16

epsilon = 1e-05


def with_halo(cells, sides, width):
    for axis, dim in sides:
        count = lax.axis_size(axis)
        ends = count - 1
        head = lax.slice_in_dim(cells, 0, width, axis=dim)
        tail = lax.slice_in_dim(cells, cells.shape[dim] - width, cells.shape[dim], axis=dim)
        cells = jnp.concatenate(
            [
                lax.ppermute(tail, axis, [(i, (i + 1) % count) for i in range(ends)]),
                cells,
                lax.ppermute(head, axis, [((i + 1) % count, i) for i in range(ends)]),
            ],
            axis=dim,
        )
    return cells


def passed_along(array, axis, by):
    peers = lax.axis_size(axis)
    pairs = [(i, i + by) for i in range(peers) if 0 <= i + by < peers]
    return lax.ppermute(array, axis, pairs)


def own_block(pieces, axes, turns):
    lengths = [lax.axis_size(a) for a in axes]
    pieces = pieces.reshape(*lengths, *pieces.shape[1:])
    pieces = pieces.transpose(*turns, *range(len(axes), pieces.ndim))
    pieces = pieces.reshape(-1, *pieces.shape[len(axes) :])
    for k in turns:
        pieces = lax.psum_scatter(pieces, axes[k], scatter_dimension=0, tiled=True)
    return pieces[0]


def normalize(rows, gain):
    values = rows.astype(F32)
    scale = lax.rsqrt(jnp.mean(values * values, axis=-1, keepdims=True) + epsilon)
    return ((values * scale * gain).astype(BF16), scale)


def norm_back(rows, scale, gain, grad_norm):
    values = rows.astype(F32)
    scaled = gain * grad_norm
    return scale * scaled - values * scale**3 * jnp.mean(values * scaled, axis=-1, keepdims=True)


def dot(a, b, ca, cb):
    return lax.dot_general(a, b, (((ca,), (cb,)), ((), ())), preferred_element_type=F32)


def layer_kernel(
    meta, near, summ, w, tok, cot,
    updated, near_grad, own_grad, sum_grad, w_part, gain_part,
    xp, kp, vp, dkt, dvt, scores, probs, bias, qs, gs, qst, gst, acc, m_ref, l_ref, d_ref,
    q_all, g_all, o_all, dq_all,
):
    rows = tok.shape[0]
    width = tok.shape[1]
    quads = width // CHUNK
    head_size = width // HEADS
    stack = QUAD * rows
    factor = 1.0 / math.sqrt(head_size)
    n_blocks = summ.shape[0] // SBLK
    yp = kp
    zk = scores.at[:, 0:width]
    zv = scores.at[:, width : 2 * width]

    block_at = []
    total = jnp.int32(0)
    for b in range(n_blocks):
        block_at.append(total)
        flag = meta[NEAR + b]

        @pl.when(flag == 1)
        def _(b=b, total=total):
            xp[pl.ds(pl.multiple_of(total, SBLK), SBLK), :] = summ[b * SBLK : (b + 1) * SBLK, :]

        total = total + SBLK * flag
    summ_end = total
    tile_at = []
    for t in range(NEAR):
        tile_at.append(total)
        n = meta[t]

        @pl.when(n > 0)
        def _(t=t, total=total):
            xp[pl.ds(pl.multiple_of(total, PACK), rows), :] = near[t]

        total = total + ((n + (PACK - 1)) // PACK) * PACK
    xp[pl.ds(pl.multiple_of(total, PACK), CHUNK), :] = jnp.zeros((CHUNK, width), BF16)
    chunks = (total + (CHUNK - 1)) // CHUNK

    place = lax.broadcasted_iota(jnp.int32, bias.shape, 1)
    live = place < summ_end
    for t in range(NEAR):
        live = live | ((place >= tile_at[t]) & (place < tile_at[t] + meta[t]))
    bias[...] = jnp.where(live, 0.0, -1e30)

    own = near[NEAR // 2]
    valid = lax.broadcasted_iota(jnp.int32, (rows, width), 0) < meta[NEAR + n_blocks]
    masked = jnp.where(valid, cot[...].astype(F32), 0.0).astype(BF16)
    q_all[...] = (dot(own, w[0], 1, 0).astype(BF16).astype(F32) * factor).astype(BF16)
    g_all[...] = dot(masked, w[3], 1, 1).astype(BF16)

    def project(c, carry):
        at = pl.ds(pl.multiple_of(c * CHUNK, CHUNK), CHUNK)
        x = xp[at, :]
        kp[at, :] = dot(x, w[1], 1, 0).astype(BF16)
        vp[at, :] = dot(x, w[2], 1, 0).astype(BF16)
        return carry

    lax.fori_loop(0, chunks, project, 0)

    lane_head = lax.broadcasted_iota(jnp.int32, (rows, CHUNK), 1) // head_size
    low, high = slice(0, 128), slice(128, 256)

    for j in range(quads):
        cols = slice(j * CHUNK, (j + 1) * CHUNK)
        q_part = q_all[:, cols].astype(F32)
        g_part = g_all[:, cols].astype(F32)
        for i in range(QUAD):
            here = slice(i * rows, (i + 1) * rows)
            qs[here, :] = jnp.where(lane_head == i, q_part, 0.0).astype(BF16)
            gs[here, :] = jnp.where(lane_head == i, g_part, 0.0).astype(BF16)
        m_ref[...] = jnp.full(m_ref.shape, -3e38, F32)

        def score(c, carry):
            at = pl.ds(pl.multiple_of(c * CHUNK, CHUNK), CHUNK)
            s = dot(qs[...], kp[at, cols], 1, 1) + bias[0:1, at]
            scores[:, at] = s
            m_ref[...] = jnp.maximum(m_ref[...], jnp.maximum(s[:, low], s[:, high]))
            return carry

        lax.fori_loop(0, chunks, score, 0)
        m_ref[...] = jnp.broadcast_to(jnp.max(m_ref[...], axis=1, keepdims=True), m_ref.shape)
        l_ref[...] = jnp.zeros(l_ref.shape, F32)
        acc[...] = jnp.zeros(acc.shape, F32)

        def mix(c, carry):
            at = pl.ds(pl.multiple_of(c * CHUNK, CHUNK), CHUNK)
            s = scores[:, at]
            m = m_ref[...]
            e0 = jnp.exp(s[:, low] - m)
            e1 = jnp.exp(s[:, high] - m)
            l_ref[...] += e0 + e1
            e = jnp.concatenate([e0, e1], axis=1).astype(BF16)
            probs[:, at] = e
            acc[...] += dot(e, vp[at, cols], 1, 0)
            return carry

        lax.fori_loop(0, chunks, mix, 0)
        inv = 1.0 / jnp.sum(l_ref[...], axis=1, keepdims=True)
        out = acc[...] * inv
        d_ref[...] = jnp.broadcast_to(
            jnp.sum(out * gs[...].astype(F32), axis=1, keepdims=True), d_ref.shape
        )
        picked = jnp.zeros((rows, CHUNK), F32)
        for i in range(QUAD):
            here = slice(i * rows, (i + 1) * rows)
            picked = jnp.where(lane_head == i, out[here], picked)
        o_all[:, cols] = picked.astype(BF16)
        qst[...] = (qs[...].astype(F32) * inv).astype(BF16).T
        gst[...] = (gs[...].astype(F32) * inv).astype(BF16).T
        l_ref[...] = jnp.broadcast_to(inv, l_ref.shape)
        acc[...] = jnp.zeros(acc.shape, F32)

        def back(c, carry):
            at = pl.ds(pl.multiple_of(c * CHUNK, CHUNK), CHUNK)
            e = probs[:, at]
            dp = dot(gs[...], vp[at, cols], 1, 1)
            d = d_ref[...]
            delta = jnp.concatenate([dp[:, low] - d, dp[:, high] - d], axis=1)
            ds = (e.astype(F32) * delta).astype(BF16)
            acc[...] += dot(ds, kp[at, cols], 1, 0)
            dkt[cols, at] = dot(qst[...], ds, 1, 0).astype(BF16)
            dvt[cols, at] = dot(gst[...], e, 1, 0).astype(BF16)
            return carry

        lax.fori_loop(0, chunks, back, 0)
        inv2 = l_ref[...] * factor
        dq = acc[...] * jnp.concatenate([inv2, inv2], axis=1)
        picked = jnp.zeros((rows, CHUNK), F32)
        for i in range(QUAD):
            here = slice(i * rows, (i + 1) * rows)
            picked = jnp.where(lane_head == i, dq[here], picked)
        dq_all[:, cols] = picked.astype(BF16)

    zk[...] = jnp.zeros(zk.shape, F32)
    zv[...] = jnp.zeros(zv.shape, F32)
    own_part = dot(dq_all[...], w[0], 1, 1)
    gain_part[...] = jnp.sum(
        (own_part * own.astype(F32)).reshape(rows // 8, 8, width), axis=0
    )

    def finish(c, carry):
        at = pl.ds(pl.multiple_of(c * CHUNK, CHUNK), CHUNK)
        x = xp[at, :]
        dk = dkt[:, at]
        dv = dvt[:, at]
        zk[...] += dot(dk, x, 1, 0)
        zv[...] += dot(dv, x, 1, 0)
        yt = dot(w[1], dk, 1, 0) + dot(w[2], dv, 1, 0)
        y = yt.astype(BF16).T
        yp[at, :] = y
        gain_part[...] += jnp.sum(
            (y.astype(F32) * x.astype(F32)).reshape(CHUNK // 8, 8, width), axis=0
        )
        return carry

    lax.fori_loop(0, chunks, finish, 0)

    w_part[0] = dot(own, dq_all[...], 0, 0).astype(BF16)
    w_part[1] = zk[...].astype(BF16).T
    w_part[2] = zv[...].astype(BF16).T
    w_part[3] = dot(o_all[...], masked, 0, 0).astype(BF16)

    row_at = lax.broadcasted_iota(jnp.int32, (rows, width), 0)
    for t in range(NEAR):
        y = yp[pl.ds(pl.multiple_of(tile_at[t], PACK), rows), :].astype(F32)
        y = jnp.where(row_at < meta[t], y, 0.0)
        if t == NEAR // 2:
            own_grad[...] = y + own_part
            near_grad[t] = jnp.zeros((rows, width), BF16)
        else:
            near_grad[t] = y.astype(BF16)
    for b in range(n_blocks):
        y = yp[pl.ds(pl.multiple_of(block_at[b], SBLK), SBLK), :].astype(F32)
        keep = jnp.zeros((SBLK, width), jnp.int32) + meta[NEAR + b]
        sum_grad[b * SBLK : (b + 1) * SBLK, :] = jnp.where(keep == 1, y, 0.0).astype(BF16)

    mixed = dot(o_all[...], w[3], 1, 0)
    updated[...] = (tok[...].astype(F32) + jnp.where(valid, mixed, 0.0)).astype(BF16)


def layer(meta, near, summ, w, tok, cot):
    rows, width = tok.shape
    most = (NEAR * rows + summ.shape[0] + CHUNK - 1) // CHUNK * CHUNK
    stack = QUAD * rows
    vm = pl.BlockSpec(memory_space=pltpu.VMEM)
    return pl.pallas_call(
        layer_kernel,
        out_shape=(
            jax.ShapeDtypeStruct((rows, width), BF16),
            jax.ShapeDtypeStruct((NEAR, rows, width), BF16),
            jax.ShapeDtypeStruct((rows, width), F32),
            jax.ShapeDtypeStruct(summ.shape, BF16),
            jax.ShapeDtypeStruct((4, width, width), BF16),
            jax.ShapeDtypeStruct((8, width), F32),
        ),
        in_specs=[pl.BlockSpec(memory_space=pltpu.SMEM)] + [vm] * 5,
        out_specs=(vm,) * 6,
        scratch_shapes=[
            pltpu.VMEM((most + CHUNK, width), BF16),
            pltpu.VMEM((most + CHUNK, width), BF16),
            pltpu.VMEM((most, width), BF16),
            pltpu.VMEM((width, most), BF16),
            pltpu.VMEM((width, most), BF16),
            pltpu.VMEM((stack, most), F32),
            pltpu.VMEM((stack, most), BF16),
            pltpu.VMEM((8, most), F32),
            pltpu.VMEM((stack, CHUNK), BF16),
            pltpu.VMEM((stack, CHUNK), BF16),
            pltpu.VMEM((CHUNK, stack), BF16),
            pltpu.VMEM((CHUNK, stack), BF16),
            pltpu.VMEM((stack, CHUNK), F32),
            pltpu.VMEM((stack, 128), F32),
            pltpu.VMEM((stack, 128), F32),
            pltpu.VMEM((stack, 128), F32),
            pltpu.VMEM((rows, width), BF16),
            pltpu.VMEM((rows, width), BF16),
            pltpu.VMEM((rows, width), BF16),
            pltpu.VMEM((rows, width), BF16),
        ],
        compiler_params=pltpu.CompilerParams(vmem_limit_bytes=63 * 1024 * 1024),
        name="layer",
    )(meta, near, summ, w, tok, cot)


def local(
    tokens, summary, counts, tile_pattern, summary_pattern, norm_gain, projections, cotangent
):
    rows, width = tokens.shape[2:]
    zero = jnp.zeros((), jnp.int32)
    grid_row = lax.axis_index(TY)
    grid_col = lax.axis_index(TX)
    token_rows = tokens[0, 0]
    grads_in = cotangent[0, 0]
    hidden, row_scale = normalize(token_rows, norm_gain)
    summary_hidden, summary_scale = normalize(summary, norm_gain)
    every = lax.all_gather(summary_hidden, TY_TX, axis=0, tiled=True)
    near = with_halo(hidden.reshape(1, 1, rows, width), ((TX, 1), (TY, 0)), 1)
    near = near.reshape(NEAR, rows, width)
    count_pad = jnp.pad(counts, 1)
    near_counts = lax.dynamic_slice(count_pad, (grid_row, grid_col), (3, 3)).reshape(NEAR)
    flags = lax.dynamic_slice(tile_pattern, (grid_row, grid_col, zero), (1, 1, NEAR)).reshape(NEAR)
    meta = jnp.concatenate(
        [
            jnp.where(flags == 1, near_counts, 0),
            (summary_pattern[0, 0] == 1).astype(jnp.int32),
            near_counts[NEAR // 2 : NEAR // 2 + 1],
        ]
    )
    updated, near_grad, own_grad, sum_grad, w_part, gain_part = layer(
        meta, near, every, projections, token_rows, grads_in
    )
    near_grad = near_grad.reshape(3, 3, rows, width)
    row_lower = passed_along(near_grad[2], TY, 1).astype(F32)
    row_upper = passed_along(near_grad[0], TY, -1).astype(F32)
    row_sum = near_grad[1].astype(F32) + row_lower + row_upper
    from_lower = passed_along(row_sum[2].astype(BF16), TX, 1).astype(F32)
    from_upper = passed_along(row_sum[0].astype(BF16), TX, -1).astype(F32)
    hidden_grad = own_grad + row_sum[1] + from_lower + from_upper
    pieces = sum_grad.reshape(-1, summary.shape[0], width)
    summary_hidden_grad = own_block(pieces, TY_TX, (1, 2, 0, 3)).astype(F32)
    grad_proj = lax.psum(w_part, TY_TX).astype(F32)
    grad_gain = lax.psum(jnp.sum(gain_part, axis=0), TY_TX)
    grad_gain = grad_gain / norm_gain
    grad_tokens = (
        grads_in.astype(F32) + norm_back(token_rows, row_scale, norm_gain, hidden_grad)
    ).astype(BF16)
    grad_summary = norm_back(summary, summary_scale, norm_gain, summary_hidden_grad).astype(BF16)
    return (
        updated.reshape(tokens.shape),
        grad_tokens.reshape(tokens.shape),
        grad_summary,
        grad_proj,
        grad_gain,
    )


def solution(mesh):
    finer = Mesh(
        mesh.devices.reshape(2, 4, 4, 2, mesh.shape["slide"]),
        ("ty_0", "ty_1", "tx_0", "tx_1", "slide"),
    )
    return jax.shard_map(
        local,
        mesh=finer,
        in_specs=(
            P(SLIDE_TY, TX, None, None),
            P(SLIDE_TY_TX, None),
            P("slide", None),
            P("slide", None, None),
            P(SLIDE_TY, TX, None),
            P(),
            P(),
            P(SLIDE_TY, TX, None, None),
        ),
        out_specs=(
            P(SLIDE_TY, TX, None, None),
            P(SLIDE_TY, TX, None, None),
            P(SLIDE_TY_TX, None),
            P("slide", None, None),
            P("slide"),
        ),
        check_vma=False,
    )
```

```python
import math

import jax
import jax.numpy as jnp
from jax import lax
from jax.experimental import pallas as pl
from jax.experimental.pallas import tpu as pltpu
from jax.sharding import Mesh
from jax.sharding import PartitionSpec as P

HEADS = 12
SBLK = 128
QUAD = 4
CHUNK = 256
PACK = 16
NEAR = 9
TY = ("ty_0", "ty_1")
TX = ("tx_0", "tx_1")
TY_TX = ("ty_0", "ty_1", "tx_0", "tx_1")
SLIDE_TY = ("slide", "ty_0", "ty_1")
SLIDE_TY_TX = ("slide", "ty_0", "ty_1", "tx_0", "tx_1")
F32 = jnp.float32
BF16 = jnp.bfloat16
MESH = pl.DeviceIdType.MESH

epsilon = 1e-05


def places():
    return (
        2 * lax.axis_index("tx_1") + lax.axis_index("ty_0"),
        lax.axis_index("ty_1"),
        lax.axis_index("tx_0"),
    )


def peer(axis, at, by):
    there = lax.rem(at[axis] + (by + 4), 4)
    if axis == 0:
        return {"tx_1": there // 2, "ty_0": lax.rem(there, 2)}
    return {"ty_1": there} if axis == 1 else {"tx_0": there}


def row_peer(at, by):
    there = lax.rem(lax.axis_index("ty_0") * 4 + at[1] + (by + 8), 8)
    return {"ty_0": there // 4, "ty_1": lax.rem(there, 4)}


def greet(at):
    barrier = pltpu.get_barrier_semaphore()
    others = [peer(axis, at, by) for axis in range(3) for by in (1, 2, 3)]
    others += [row_peer(at, 1), row_peer(at, -1)]
    for other in others:
        pl.semaphore_signal(barrier, inc=1, device_id=other, device_id_type=MESH)
    pl.semaphore_wait(barrier, len(others))


class Sender:
    def __init__(self, send_sems, recv_sems):
        self.send_sems, self.recv_sems = send_sems, recv_sems
        self.copies = []

    def send(self, src, dst, device):
        k = len(self.copies)
        copy = pltpu.make_async_remote_copy(
            src_ref=src,
            dst_ref=dst,
            send_sem=self.send_sems.at[k],
            recv_sem=self.recv_sems.at[k],
            device_id=device,
            device_id_type=MESH,
        )
        copy.start()
        self.copies.append(copy)
        return copy

    def drain(self):
        for copy in self.copies:
            copy.wait_send()


def take_turns(tasks):
    tasks = list(tasks)
    while tasks:
        tasks = [task for task in tasks if next(task, "end") != "end"]


def added(*refs):
    total = refs[0][...].astype(F32)
    for ref in refs[1:]:
        total = total + ref[...].astype(F32)
    return total


def scatter_ring(link, axis, at, piece, relay, direct, out):
    c = at[axis]
    right, left, across = [lax.rem(c + k, 4) for k in (1, 3, 2)]
    to_right, to_left = peer(axis, at, 1), peer(axis, at, -1)
    far_a = link.send(piece(across, 0), relay.at[0, 0], to_right)
    far_b = link.send(piece(across, 1), relay.at[0, 1], to_left)
    near_b = link.send(piece(right, 1), direct.at[0, 1], to_right)
    near_a = link.send(piece(left, 0), direct.at[1, 0], to_left)
    yield
    far_a.wait_recv()
    relay[1, 0] = added(relay.at[0, 0], piece(right, 0)).astype(BF16)
    sum_a = link.send(relay.at[1, 0], direct.at[0, 0], to_right)
    yield
    far_b.wait_recv()
    relay[1, 1] = added(relay.at[0, 1], piece(left, 1)).astype(BF16)
    sum_b = link.send(relay.at[1, 1], direct.at[1, 1], to_left)
    yield
    for copy in (near_b, near_a, sum_a, sum_b):
        copy.wait_recv()
    for half in range(2):
        out[half] = added(piece(c, half), direct.at[0, half], direct.at[1, half]).astype(BF16)


def scatter_direct(link, axis, at, piece, slots, out):
    copies = [
        link.send(piece(lax.rem(at[axis] + k, 4)), slots.at[k - 1], peer(axis, at, k))
        for k in (1, 3, 2)
    ]
    yield
    for copy in copies:
        copy.wait_recv()
    total = added(piece(at[axis]), slots.at[0], slots.at[1], slots.at[2])
    out[...] = total.astype(out.dtype)


def gather_direct(link, axis, at, place):
    mine = place(at[axis])
    copies = [link.send(mine, mine, peer(axis, at, k)) for k in (1, 3, 2)]
    yield
    for copy in copies:
        copy.wait_recv()


def gather_ring(link, axis, at, place, half_place):
    c = at[axis]
    right, left = lax.rem(c + 1, 4), lax.rem(c + 3, 4)
    to_right, to_left = peer(axis, at, 1), peer(axis, at, -1)
    mine = place(c)
    one = link.send(mine, mine, to_right)
    two = link.send(mine, mine, to_left)
    yield
    one.wait_recv()
    half = half_place(left, 0)
    three = link.send(half, half, to_right)
    yield
    two.wait_recv()
    half = half_place(right, 1)
    four = link.send(half, half, to_left)
    yield
    three.wait_recv()
    four.wait_recv()


def gather_kernel(hidden, summ, near, every, send_sems, recv_sems):
    at = places()
    x, y, z = at
    x_hi, x_lo = lax.axis_index("tx_1"), lax.axis_index("ty_0")
    near[1, 1] = hidden[...]
    every[x_lo, y, z, x_hi] = summ[...]
    greet(at)
    link = Sender(send_sems, recv_sems)
    from_x, from_z = 2 - 2 * x_hi, 2 * x_hi

    def halo():
        beside = link.send(hidden, near.at[1, 2 * x_hi], {"tx_1": 1 - x_hi})
        rows = [
            link.send(hidden, near.at[0, 1], row_peer(at, 1)),
            link.send(hidden, near.at[2, 1], row_peer(at, -1)),
        ]
        yield
        beside.wait_recv()
        there = {"tx_0": lax.rem(z + (5 - 2 * x_hi), 4)}
        beyond = link.send(near.at[1, from_x], near.at[1, from_z], there)
        rows.append(link.send(near.at[1, from_x], near.at[0, from_x], row_peer(at, 1)))
        rows.append(link.send(near.at[1, from_x], near.at[2, from_x], row_peer(at, -1)))
        yield
        beyond.wait_recv()
        rows.append(link.send(near.at[1, from_z], near.at[0, from_z], row_peer(at, 1)))
        rows.append(link.send(near.at[1, from_z], near.at[2, from_z], row_peer(at, -1)))
        yield
        yield
        yield
        for copy in rows:
            copy.wait_recv()

    def summaries():
        yield from gather_direct(link, 1, at, lambda d: every.at[x_lo, d, z, x_hi])
        yield from gather_direct(
            link, 0, at, lambda d: every.at[lax.rem(d, 2), :, z, d // 2]
        )
        yield from gather_ring(
            link, 2, at, lambda d: every.at[:, :, d], lambda d, half: every.at[half, :, d]
        )

    take_turns([summaries(), halo()])
    link.drain()


def gather(hidden, summary_hidden):
    rows, width = hidden.shape
    block = summary_hidden.shape[0]
    vm = pl.BlockSpec(memory_space=pltpu.VMEM)
    sends = 3 + 3 + 4 + 3 + 3 + 2
    near, every = pl.pallas_call(
        gather_kernel,
        out_shape=(
            jax.ShapeDtypeStruct((3, 3, rows, width), BF16),
            jax.ShapeDtypeStruct((2, 4, 4, 2, block, width), BF16),
        ),
        in_specs=[vm] * 2,
        out_specs=(vm,) * 2,
        scratch_shapes=[
            pltpu.SemaphoreType.DMA((sends,)),
            pltpu.SemaphoreType.DMA((sends,)),
        ],
        compiler_params=pltpu.CompilerParams(
            collective_id=0, has_side_effects=True, vmem_limit_bytes=32 * 1024 * 1024
        ),
        name="gather",
    )(hidden, summary_hidden)
    return near.reshape(NEAR, rows, width), every.reshape(-1, width)


def exchange_kernel(
    near, own, sums, w_in, gain, out_own, out_sum, w_out, out_gain,
    beside, row_sum, z_slot, x_slot, message,
    s_relay, s_direct, s_one, s_slots_x, s_two, s_slots_y,
    w_relay, w_direct, w_one, w_slots_two, w_two, w_slots_three,
    gain_sum, gain_slots, send_sems, recv_sems,
):
    at = places()
    x, y, z = at
    x_hi = lax.axis_index("tx_1")
    greet(at)
    link = Sender(send_sems, recv_sems)

    def halo():
        rows = []
        for j in (0, 2, 1):
            up = link.send(near.at[2, j], beside.at[0, j], row_peer(at, 1))
            down = link.send(near.at[0, j], beside.at[1, j], row_peer(at, -1))
            rows.append((j, up, down))
        yield
        for j, up, down in rows[:2]:
            up.wait_recv()
            down.wait_recv()
            row_sum[j // 2] = added(near.at[1, j], beside.at[0, j], beside.at[1, j]).astype(BF16)
        there = {"tx_0": lax.rem(z + (3 + 2 * x_hi), 4)}
        far = link.send(row_sum.at[x_hi], z_slot, there)
        yield
        _, up, down = rows[2]
        up.wait_recv()
        down.wait_recv()
        out_own[...] = own[...] + added(beside.at[0, 1], beside.at[1, 1])
        far.wait_recv()
        message[...] = added(row_sum.at[1 - x_hi], z_slot).astype(BF16)
        last = link.send(message, x_slot, {"tx_1": 1 - x_hi})
        yield
        yield
        last.wait_recv()
        out_own[...] += x_slot[...].astype(F32)

    def summaries():
        half = sums.shape[0] // 2
        yield from scatter_ring(
            link, 2, at, lambda d, h: sums.at[pl.ds(h * half, half), d], s_relay, s_direct, s_one
        )
        block = out_sum.shape[0]
        yield from scatter_direct(
            link, 0, at,
            lambda d: s_one.at[lax.rem(d, 2), :, pl.ds((d // 2) * block, block)],
            s_slots_x, s_two,
        )
        yield from scatter_direct(link, 1, at, lambda d: s_two.at[d], s_slots_y, out_sum)

    def weights(p):
        a, b, c = p, (p + 1) % 3, (p + 2) % 3
        part = w_in.shape[0] // 3
        size = [part // 4, part // 16, part // 64]
        first = p * part

        def rows_of(ref, start, count):
            return ref.at[pl.ds(pl.multiple_of(start, PACK), count)]

        yield from scatter_ring(
            link, a, at,
            lambda d, h: rows_of(w_in, first + d * size[0] + h * (size[0] // 2), size[0] // 2),
            w_relay.at[p], w_direct.at[p], w_one.at[p],
        )
        yield from scatter_direct(
            link, b, at,
            lambda d: w_one.at[p, d // 2, pl.ds(lax.rem(d, 2) * size[1], size[1])],
            w_slots_two.at[p], w_two.at[p],
        )
        base = first + at[a] * size[0]
        inner = base + at[b] * size[1]
        yield from scatter_direct(
            link, c, at,
            lambda d: rows_of(w_two.at[p], d * size[2], size[2]),
            w_slots_three.at[p],
            rows_of(w_out, inner + at[c] * size[2], size[2]),
        )
        yield from gather_direct(
            link, c, at, lambda d: rows_of(w_out, inner + d * size[2], size[2])
        )
        yield from gather_direct(
            link, b, at, lambda d: rows_of(w_out, base + d * size[1], size[1])
        )
        yield from gather_ring(
            link, a, at,
            lambda d: rows_of(w_out, first + d * size[0], size[0]),
            lambda d, h: rows_of(
                w_out, first + d * size[0] + h * (size[0] // 2), size[0] // 2
            ),
        )

    def gains():
        gain_sum[0] = gain[...]
        for k in range(3):
            yield from scatter_direct(
                link, k, at, lambda d, k=k: gain_sum.at[k], gain_slots.at[k],
                gain_sum.at[k + 1] if k < 2 else out_gain,
            )

    take_turns([halo(), summaries(), weights(0), weights(1), weights(2), gains()])
    link.drain()


def exchange(near_grad, own_grad, sum_grad, w_part, gain_part, block):
    rows, width = own_grad.shape
    vm = pl.BlockSpec(memory_space=pltpu.VMEM)
    total = w_part.shape[0] * width
    part = total // 3
    sends = 6 + 2 + 6 + 3 + 3 + 3 * (6 + 3 + 3 + 3 + 3 + 4) + 9
    sums = sum_grad.reshape(8, 4, 2 * block, width)
    own, sum_own, w_all, gain = pl.pallas_call(
        exchange_kernel,
        out_shape=(
            jax.ShapeDtypeStruct((rows, width), F32),
            jax.ShapeDtypeStruct((block, width), F32),
            jax.ShapeDtypeStruct((total, width), BF16),
            jax.ShapeDtypeStruct((8, width), F32),
        ),
        in_specs=[vm] * 5,
        out_specs=(vm,) * 4,
        scratch_shapes=[
            pltpu.VMEM((2, 3, rows, width), BF16),
            pltpu.VMEM((2, rows, width), BF16),
            pltpu.VMEM((rows, width), BF16),
            pltpu.VMEM((rows, width), BF16),
            pltpu.VMEM((rows, width), BF16),
            pltpu.VMEM((2, 2, 4, 2 * block, width), BF16),
            pltpu.VMEM((2, 2, 4, 2 * block, width), BF16),
            pltpu.VMEM((2, 4, 2 * block, width), BF16),
            pltpu.VMEM((3, 4, block, width), BF16),
            pltpu.VMEM((4, block, width), BF16),
            pltpu.VMEM((3, block, width), BF16),
            pltpu.VMEM((3, 2, 2, part // 8, width), BF16),
            pltpu.VMEM((3, 2, 2, part // 8, width), BF16),
            pltpu.VMEM((3, 2, part // 8, width), BF16),
            pltpu.VMEM((3, 3, part // 16, width), BF16),
            pltpu.VMEM((3, part // 16, width), BF16),
            pltpu.VMEM((3, 3, part // 64, width), BF16),
            pltpu.VMEM((3, 8, width), F32),
            pltpu.VMEM((3, 3, 8, width), F32),
            pltpu.SemaphoreType.DMA((sends,)),
            pltpu.SemaphoreType.DMA((sends,)),
        ],
        compiler_params=pltpu.CompilerParams(
            collective_id=1, has_side_effects=True, vmem_limit_bytes=48 * 1024 * 1024
        ),
        name="exchange",
    )(
        near_grad.reshape(3, 3, rows, width), own_grad, sums, w_part.reshape(total, width), gain_part
    )
    return own, sum_own, w_all.reshape(w_part.shape), jnp.sum(gain, axis=0)


def normalize(rows, gain):
    values = rows.astype(F32)
    scale = lax.rsqrt(jnp.mean(values * values, axis=-1, keepdims=True) + epsilon)
    return ((values * scale * gain).astype(BF16), scale)


def norm_back(rows, scale, gain, grad_norm):
    values = rows.astype(F32)
    scaled = gain * grad_norm
    return scale * scaled - values * scale**3 * jnp.mean(values * scaled, axis=-1, keepdims=True)


def dot(a, b, ca, cb):
    return lax.dot_general(a, b, (((ca,), (cb,)), ((), ())), preferred_element_type=F32)


def layer_kernel(
    meta, near, summ, w, tok, cot,
    updated, near_grad, own_grad, sum_grad, w_part, gain_part,
    xp, kp, vp, dkt, dvt, scores, probs, bias, qs, gs, qst, gst, acc, m_ref, l_ref, d_ref,
    q_all, g_all, o_all, dq_all,
):
    rows = tok.shape[0]
    width = tok.shape[1]
    quads = width // CHUNK
    head_size = width // HEADS
    stack = QUAD * rows
    factor = 1.0 / math.sqrt(head_size)
    n_blocks = summ.shape[0] // SBLK
    yp = kp
    zk = scores.at[:, 0:width]
    zv = scores.at[:, width : 2 * width]

    block_at = []
    total = jnp.int32(0)
    for b in range(n_blocks):
        block_at.append(total)
        flag = meta[NEAR + b]

        @pl.when(flag == 1)
        def _(b=b, total=total):
            xp[pl.ds(pl.multiple_of(total, SBLK), SBLK), :] = summ[b * SBLK : (b + 1) * SBLK, :]

        total = total + SBLK * flag
    summ_end = total
    tile_at = []
    for t in range(NEAR):
        tile_at.append(total)
        n = meta[t]

        @pl.when(n > 0)
        def _(t=t, total=total):
            xp[pl.ds(pl.multiple_of(total, PACK), rows), :] = near[t]

        total = total + ((n + (PACK - 1)) // PACK) * PACK
    xp[pl.ds(pl.multiple_of(total, PACK), CHUNK), :] = jnp.zeros((CHUNK, width), BF16)
    chunks = (total + (CHUNK - 1)) // CHUNK

    place = lax.broadcasted_iota(jnp.int32, bias.shape, 1)
    live = place < summ_end
    for t in range(NEAR):
        live = live | ((place >= tile_at[t]) & (place < tile_at[t] + meta[t]))
    bias[...] = jnp.where(live, 0.0, -1e30)

    own = near[NEAR // 2]
    valid = lax.broadcasted_iota(jnp.int32, (rows, width), 0) < meta[NEAR + n_blocks]
    masked = jnp.where(valid, cot[...].astype(F32), 0.0).astype(BF16)
    q_all[...] = (dot(own, w[0], 1, 0).astype(BF16).astype(F32) * factor).astype(BF16)
    g_all[...] = dot(masked, w[3], 1, 1).astype(BF16)

    def project(c, carry):
        at = pl.ds(pl.multiple_of(c * CHUNK, CHUNK), CHUNK)
        x = xp[at, :]
        kp[at, :] = dot(x, w[1], 1, 0).astype(BF16)
        vp[at, :] = dot(x, w[2], 1, 0).astype(BF16)
        return carry

    lax.fori_loop(0, chunks, project, 0)

    lane_head = lax.broadcasted_iota(jnp.int32, (rows, CHUNK), 1) // head_size
    low, high = slice(0, 128), slice(128, 256)

    for j in range(quads):
        cols = slice(j * CHUNK, (j + 1) * CHUNK)
        q_part = q_all[:, cols].astype(F32)
        g_part = g_all[:, cols].astype(F32)
        for i in range(QUAD):
            here = slice(i * rows, (i + 1) * rows)
            qs[here, :] = jnp.where(lane_head == i, q_part, 0.0).astype(BF16)
            gs[here, :] = jnp.where(lane_head == i, g_part, 0.0).astype(BF16)
        m_ref[...] = jnp.full(m_ref.shape, -3e38, F32)

        def score(c, carry):
            at = pl.ds(pl.multiple_of(c * CHUNK, CHUNK), CHUNK)
            s = dot(qs[...], kp[at, cols], 1, 1) + bias[0:1, at]
            scores[:, at] = s
            m_ref[...] = jnp.maximum(m_ref[...], jnp.maximum(s[:, low], s[:, high]))
            return carry

        lax.fori_loop(0, chunks, score, 0)
        m_ref[...] = jnp.broadcast_to(jnp.max(m_ref[...], axis=1, keepdims=True), m_ref.shape)
        l_ref[...] = jnp.zeros(l_ref.shape, F32)
        acc[...] = jnp.zeros(acc.shape, F32)

        def mix(c, carry):
            at = pl.ds(pl.multiple_of(c * CHUNK, CHUNK), CHUNK)
            s = scores[:, at]
            m = m_ref[...]
            e0 = jnp.exp(s[:, low] - m)
            e1 = jnp.exp(s[:, high] - m)
            l_ref[...] += e0 + e1
            e = jnp.concatenate([e0, e1], axis=1).astype(BF16)
            probs[:, at] = e
            acc[...] += dot(e, vp[at, cols], 1, 0)
            return carry

        lax.fori_loop(0, chunks, mix, 0)
        inv = 1.0 / jnp.sum(l_ref[...], axis=1, keepdims=True)
        out = acc[...] * inv
        d_ref[...] = jnp.broadcast_to(
            jnp.sum(out * gs[...].astype(F32), axis=1, keepdims=True), d_ref.shape
        )
        picked = jnp.zeros((rows, CHUNK), F32)
        for i in range(QUAD):
            here = slice(i * rows, (i + 1) * rows)
            picked = jnp.where(lane_head == i, out[here], picked)
        o_all[:, cols] = picked.astype(BF16)
        qst[...] = (qs[...].astype(F32) * inv).astype(BF16).T
        gst[...] = (gs[...].astype(F32) * inv).astype(BF16).T
        l_ref[...] = jnp.broadcast_to(inv, l_ref.shape)
        acc[...] = jnp.zeros(acc.shape, F32)

        def back(c, carry):
            at = pl.ds(pl.multiple_of(c * CHUNK, CHUNK), CHUNK)
            e = probs[:, at]
            dp = dot(gs[...], vp[at, cols], 1, 1)
            d = d_ref[...]
            delta = jnp.concatenate([dp[:, low] - d, dp[:, high] - d], axis=1)
            ds = (e.astype(F32) * delta).astype(BF16)
            acc[...] += dot(ds, kp[at, cols], 1, 0)
            dkt[cols, at] = dot(qst[...], ds, 1, 0).astype(BF16)
            dvt[cols, at] = dot(gst[...], e, 1, 0).astype(BF16)
            return carry

        lax.fori_loop(0, chunks, back, 0)
        inv2 = l_ref[...] * factor
        dq = acc[...] * jnp.concatenate([inv2, inv2], axis=1)
        picked = jnp.zeros((rows, CHUNK), F32)
        for i in range(QUAD):
            here = slice(i * rows, (i + 1) * rows)
            picked = jnp.where(lane_head == i, dq[here], picked)
        dq_all[:, cols] = picked.astype(BF16)

    zk[...] = jnp.zeros(zk.shape, F32)
    zv[...] = jnp.zeros(zv.shape, F32)
    own_part = dot(dq_all[...], w[0], 1, 1)
    gain_part[...] = jnp.sum(
        (own_part * own.astype(F32)).reshape(rows // 8, 8, width), axis=0
    )

    def finish(c, carry):
        at = pl.ds(pl.multiple_of(c * CHUNK, CHUNK), CHUNK)
        x = xp[at, :]
        dk = dkt[:, at]
        dv = dvt[:, at]
        zk[...] += dot(dk, x, 1, 0)
        zv[...] += dot(dv, x, 1, 0)
        yt = dot(w[1], dk, 1, 0) + dot(w[2], dv, 1, 0)
        y = yt.astype(BF16).T
        yp[at, :] = y
        gain_part[...] += jnp.sum(
            (y.astype(F32) * x.astype(F32)).reshape(CHUNK // 8, 8, width), axis=0
        )
        return carry

    lax.fori_loop(0, chunks, finish, 0)

    w_part[0] = dot(own, dq_all[...], 0, 0).astype(BF16)
    w_part[1] = zk[...].astype(BF16).T
    w_part[2] = zv[...].astype(BF16).T
    w_part[3] = dot(o_all[...], masked, 0, 0).astype(BF16)

    row_at = lax.broadcasted_iota(jnp.int32, (rows, width), 0)
    for t in range(NEAR):
        y = yp[pl.ds(pl.multiple_of(tile_at[t], PACK), rows), :].astype(F32)
        y = jnp.where(row_at < meta[t], y, 0.0)
        if t == NEAR // 2:
            own_grad[...] = y + own_part
            near_grad[t] = jnp.zeros((rows, width), BF16)
        else:
            near_grad[t] = y.astype(BF16)
    for b in range(n_blocks):
        y = yp[pl.ds(pl.multiple_of(block_at[b], SBLK), SBLK), :].astype(F32)
        keep = jnp.zeros((SBLK, width), jnp.int32) + meta[NEAR + b]
        sum_grad[b * SBLK : (b + 1) * SBLK, :] = jnp.where(keep == 1, y, 0.0).astype(BF16)

    mixed = dot(o_all[...], w[3], 1, 0)
    updated[...] = (tok[...].astype(F32) + jnp.where(valid, mixed, 0.0)).astype(BF16)


def layer(meta, near, summ, w, tok, cot):
    rows, width = tok.shape
    most = (NEAR * rows + summ.shape[0] + CHUNK - 1) // CHUNK * CHUNK
    stack = QUAD * rows
    vm = pl.BlockSpec(memory_space=pltpu.VMEM)
    return pl.pallas_call(
        layer_kernel,
        out_shape=(
            jax.ShapeDtypeStruct((rows, width), BF16),
            jax.ShapeDtypeStruct((NEAR, rows, width), BF16),
            jax.ShapeDtypeStruct((rows, width), F32),
            jax.ShapeDtypeStruct(summ.shape, BF16),
            jax.ShapeDtypeStruct((4, width, width), BF16),
            jax.ShapeDtypeStruct((8, width), F32),
        ),
        in_specs=[pl.BlockSpec(memory_space=pltpu.SMEM)] + [vm] * 5,
        out_specs=(vm,) * 6,
        scratch_shapes=[
            pltpu.VMEM((most + CHUNK, width), BF16),
            pltpu.VMEM((most + CHUNK, width), BF16),
            pltpu.VMEM((most, width), BF16),
            pltpu.VMEM((width, most), BF16),
            pltpu.VMEM((width, most), BF16),
            pltpu.VMEM((stack, most), F32),
            pltpu.VMEM((stack, most), BF16),
            pltpu.VMEM((8, most), F32),
            pltpu.VMEM((stack, CHUNK), BF16),
            pltpu.VMEM((stack, CHUNK), BF16),
            pltpu.VMEM((CHUNK, stack), BF16),
            pltpu.VMEM((CHUNK, stack), BF16),
            pltpu.VMEM((stack, CHUNK), F32),
            pltpu.VMEM((stack, 128), F32),
            pltpu.VMEM((stack, 128), F32),
            pltpu.VMEM((stack, 128), F32),
            pltpu.VMEM((rows, width), BF16),
            pltpu.VMEM((rows, width), BF16),
            pltpu.VMEM((rows, width), BF16),
            pltpu.VMEM((rows, width), BF16),
        ],
        compiler_params=pltpu.CompilerParams(vmem_limit_bytes=63 * 1024 * 1024),
        name="layer",
    )(meta, near, summ, w, tok, cot)


def local(
    tokens, summary, counts, tile_pattern, summary_pattern, norm_gain, projections, cotangent
):
    rows, width = tokens.shape[2:]
    zero = jnp.zeros((), jnp.int32)
    grid_row = lax.axis_index(TY)
    grid_col = lax.axis_index(TX)
    token_rows = tokens[0, 0]
    grads_in = cotangent[0, 0]
    hidden, row_scale = normalize(token_rows, norm_gain)
    summary_hidden, summary_scale = normalize(summary, norm_gain)
    near, every = gather(hidden, summary_hidden)
    count_pad = jnp.pad(counts, 1)
    near_counts = lax.dynamic_slice(count_pad, (grid_row, grid_col), (3, 3)).reshape(NEAR)
    flags = lax.dynamic_slice(tile_pattern, (grid_row, grid_col, zero), (1, 1, NEAR)).reshape(NEAR)
    meta = jnp.concatenate(
        [
            jnp.where(flags == 1, near_counts, 0),
            (summary_pattern[0, 0] == 1).astype(jnp.int32),
            near_counts[NEAR // 2 : NEAR // 2 + 1],
        ]
    )
    updated, near_grad, own_grad, sum_grad, w_part, gain_part = layer(
        meta, near, every, projections, token_rows, grads_in
    )
    hidden_grad, summary_hidden_grad, grad_proj, grad_gain = exchange(
        near_grad, own_grad, sum_grad, w_part, gain_part, summary.shape[0]
    )
    grad_proj = grad_proj.astype(F32)
    grad_gain = grad_gain / norm_gain
    grad_tokens = (
        grads_in.astype(F32) + norm_back(token_rows, row_scale, norm_gain, hidden_grad)
    ).astype(BF16)
    grad_summary = norm_back(summary, summary_scale, norm_gain, summary_hidden_grad).astype(BF16)
    return (
        updated.reshape(tokens.shape),
        grad_tokens.reshape(tokens.shape),
        grad_summary,
        grad_proj,
        grad_gain,
    )


def solution(mesh):
    finer = Mesh(
        mesh.devices.reshape(2, 4, 4, 2, mesh.shape["slide"]),
        ("ty_0", "ty_1", "tx_0", "tx_1", "slide"),
    )
    return jax.shard_map(
        local,
        mesh=finer,
        in_specs=(
            P(SLIDE_TY, TX, None, None),
            P(SLIDE_TY_TX, None),
            P("slide", None),
            P("slide", None, None),
            P(SLIDE_TY, TX, None),
            P(),
            P(),
            P(SLIDE_TY, TX, None, None),
        ),
        out_specs=(
            P(SLIDE_TY, TX, None, None),
            P(SLIDE_TY, TX, None, None),
            P(SLIDE_TY_TX, None),
            P("slide", None, None),
            P("slide"),
        ),
        check_vma=False,
    )
```

```python
import math

import jax
import jax.numpy as jnp
from jax import lax
from jax.experimental import pallas as pl
from jax.experimental.pallas import tpu as pltpu
from jax.sharding import Mesh
from jax.sharding import PartitionSpec as P

HEADS = 12
SBLK = 128
QUAD = 4
CHUNK = 256
PACK = 16
NEAR = 9
TX = ("tx_0", "tx_1")
SLIDE_TY = ("slide", "ty_0", "ty_1")
SLIDE_TY_TX = ("slide", "ty_0", "ty_1", "tx_0", "tx_1")
F32 = jnp.float32
BF16 = jnp.bfloat16
MESH = pl.DeviceIdType.MESH

epsilon = 1e-05


def places():
    return (
        2 * lax.axis_index("tx_1") + lax.axis_index("ty_0"),
        lax.axis_index("ty_1"),
        lax.axis_index("tx_0"),
    )


def peer(axis, at, by):
    there = lax.rem(at[axis] + (by + 4), 4)
    if axis == 0:
        return {"tx_1": there // 2, "ty_0": lax.rem(there, 2)}
    return {"ty_1": there} if axis == 1 else {"tx_0": there}


def row_peer(at, by):
    there = lax.rem(lax.axis_index("ty_0") * 4 + at[1] + (by + 8), 8)
    return {"ty_0": there // 4, "ty_1": lax.rem(there, 4)}


def greet(at):
    barrier = pltpu.get_barrier_semaphore()
    others = [peer(axis, at, by) for axis in range(3) for by in (1, 2, 3)]
    others += [row_peer(at, 1), row_peer(at, -1)]
    for other in others:
        pl.semaphore_signal(barrier, inc=1, device_id=other, device_id_type=MESH)
    return lambda: pl.semaphore_wait(barrier, len(others))


class Loader:
    def __init__(self, sems):
        self.sems, self.count = sems, 0

    def copy(self, src, dst):
        copy = pltpu.make_async_copy(src, dst, self.sems.at[self.count])
        self.count += 1
        copy.start()
        return copy


class Sender:
    def __init__(self, send_sems, recv_sems):
        self.send_sems, self.recv_sems = send_sems, recv_sems
        self.copies = []

    def send(self, src, dst, device):
        k = len(self.copies)
        copy = pltpu.make_async_remote_copy(
            src_ref=src,
            dst_ref=dst,
            send_sem=self.send_sems.at[k],
            recv_sem=self.recv_sems.at[k],
            device_id=device,
            device_id_type=MESH,
        )
        copy.start()
        self.copies.append(copy)
        return copy

    def drain(self):
        for copy in self.copies:
            copy.wait_send()


def take_turns(tasks):
    tasks = list(tasks)
    while tasks:
        tasks = [task for task in tasks if next(task, "end") != "end"]


def added(*refs):
    total = refs[0][...].astype(F32)
    for ref in refs[1:]:
        total = total + ref[...].astype(F32)
    return total


def scatter_ring(link, axis, at, piece, held, ready, relay, direct, out):
    c = at[axis]
    right, left, across = [lax.rem(c + k, 4) for k in (1, 3, 2)]
    to_right, to_left = peer(axis, at, 1), peer(axis, at, -1)
    far_a = link.send(piece(across, 0), relay.at[0, 0], to_right)
    far_b = link.send(piece(across, 1), relay.at[0, 1], to_left)
    near_b = link.send(piece(right, 1), direct.at[0, 1], to_right)
    near_a = link.send(piece(left, 0), direct.at[1, 0], to_left)
    yield
    for copy in ready:
        copy.wait()
    far_a.wait_recv()
    relay[1, 0] = added(relay.at[0, 0], held.at[0]).astype(BF16)
    sum_a = link.send(relay.at[1, 0], direct.at[0, 0], to_right)
    far_b.wait_recv()
    relay[1, 1] = added(relay.at[0, 1], held.at[1]).astype(BF16)
    sum_b = link.send(relay.at[1, 1], direct.at[1, 1], to_left)
    yield
    for copy in (near_b, near_a, sum_a, sum_b):
        copy.wait_recv()
    for half in range(2):
        out[half] = added(held.at[2 + half], direct.at[0, half], direct.at[1, half]).astype(BF16)


def scatter_direct(link, axis, at, piece, slots, out):
    copies = [
        link.send(piece(lax.rem(at[axis] + k, 4)), slots.at[k - 1], peer(axis, at, k))
        for k in (1, 3, 2)
    ]
    yield
    for copy in copies:
        copy.wait_recv()
    total = added(piece(at[axis]), slots.at[0], slots.at[1], slots.at[2])
    out[...] = total.astype(out.dtype)


def gather_direct(link, axis, at, place):
    mine = place(at[axis])
    copies = [link.send(mine, mine, peer(axis, at, k)) for k in (1, 3, 2)]
    yield
    for copy in copies:
        copy.wait_recv()


def gather_ring(link, axis, at, place, half_place):
    c = at[axis]
    right, left = lax.rem(c + 1, 4), lax.rem(c + 3, 4)
    to_right, to_left = peer(axis, at, 1), peer(axis, at, -1)
    mine = place(c)
    one = link.send(mine, mine, to_right)
    two = link.send(mine, mine, to_left)
    yield
    one.wait_recv()
    half = half_place(left, 0)
    three = link.send(half, half, to_right)
    two.wait_recv()
    half = half_place(right, 1)
    four = link.send(half, half, to_left)
    yield
    three.wait_recv()
    four.wait_recv()


def gather_kernel(
    tokens, summary, gain, near, every, hidden, summ, local_sems, send_sems, recv_sems
):
    at = places()
    x, y, z = at
    x_hi, x_lo = lax.axis_index("tx_1"), lax.axis_index("ty_0")
    met = greet(at)
    summ[...] = normalize(summary[...], gain[...])[0]
    hidden[...] = normalize(tokens[...], gain[...])[0]
    load = Loader(local_sems)
    own = every.at[x_lo, y, z, x_hi]
    kept = [load.copy(summ, own), load.copy(hidden, near.at[1, 1])]
    met()
    link = Sender(send_sems, recv_sems)
    from_x, from_z = 2 - 2 * x_hi, 2 * x_hi

    def halo():
        beside = link.send(hidden, near.at[1, 2 * x_hi], {"tx_1": 1 - x_hi})
        rows = [
            link.send(hidden, near.at[0, 1], row_peer(at, 1)),
            link.send(hidden, near.at[2, 1], row_peer(at, -1)),
        ]
        yield
        beside.wait_recv()
        there = {"tx_0": lax.rem(z + (5 - 2 * x_hi), 4)}
        beyond = link.send(near.at[1, from_x], near.at[1, from_z], there)
        rows.append(link.send(near.at[1, from_x], near.at[0, from_x], row_peer(at, 1)))
        rows.append(link.send(near.at[1, from_x], near.at[2, from_x], row_peer(at, -1)))
        yield
        beyond.wait_recv()
        rows.append(link.send(near.at[1, from_z], near.at[0, from_z], row_peer(at, 1)))
        rows.append(link.send(near.at[1, from_z], near.at[2, from_z], row_peer(at, -1)))
        yield
        yield
        yield
        for copy in rows:
            copy.wait_recv()

    def summaries():
        copies = [link.send(summ, own, peer(1, at, k)) for k in (1, 3, 2)]
        yield
        kept[0].wait()
        for copy in copies:
            copy.wait_recv()
        yield from gather_direct(
            link, 0, at, lambda d: every.at[lax.rem(d, 2), :, z, d // 2]
        )
        yield from gather_ring(
            link, 2, at, lambda d: every.at[:, :, d], lambda d, half: every.at[half, :, d]
        )

    take_turns([summaries(), halo()])
    kept[1].wait()
    link.drain()


def gather(tokens, summary, gain):
    rows, width = tokens.shape
    block = summary.shape[0]
    vm = pl.BlockSpec(memory_space=pltpu.VMEM)
    sends = 3 + 3 + 4 + 3 + 3 + 2
    near, every = pl.pallas_call(
        gather_kernel,
        out_shape=(
            jax.ShapeDtypeStruct((3, 3, rows, width), BF16),
            jax.ShapeDtypeStruct((2, 4, 4, 2, block, width), BF16),
        ),
        in_specs=[vm] * 3,
        out_specs=(pl.BlockSpec(memory_space=pl.ANY),) * 2,
        scratch_shapes=[
            pltpu.VMEM((rows, width), BF16),
            pltpu.VMEM((block, width), BF16),
            pltpu.SemaphoreType.DMA((2,)),
            pltpu.SemaphoreType.DMA((sends,)),
            pltpu.SemaphoreType.DMA((sends,)),
        ],
        compiler_params=pltpu.CompilerParams(
            collective_id=0, has_side_effects=True, vmem_limit_bytes=60 * 1024 * 1024
        ),
        name="gather",
    )(tokens, summary, gain)
    return near.reshape(NEAR, rows, width), every.reshape(-1, width)


def exchange_kernel(
    near, own, sums, w_in, gain_in, tokens, summary, gain, cot,
    grad_tokens, grad_summary, grad_gain, w_out,
    own_v, mid, tok_v, sum_v, gain_v, cot_v, s_loc, w_loc,
    beside, row_sum, z_slot, x_slot, message,
    s_relay, s_direct, s_one, s_slots_x, s_two, s_slots_y, s_sum,
    w_relay, w_direct, w_one, w_slots_two, w_two, w_slots_three,
    gain_sum, gain_slots, local_sems, send_sems, recv_sems,
):
    at = places()
    x, y, z = at
    x_hi = lax.axis_index("tx_1")
    met = greet(at)
    load = Loader(local_sems)
    width = w_in.shape[1]
    wide = width // 2
    part = w_in.shape[0] // 3
    size = [part // 4, part // 16, part // 64]
    s_half = sums.shape[0] // 2

    def rows_of(ref, start, count, q):
        return ref.at[
            pl.ds(pl.multiple_of(start, PACK), count), q * wide : (q + 1) * wide
        ]

    def s_piece(d, h):
        return sums.at[pl.ds(h * s_half, s_half), d]

    def w_piece(p, q):
        half = size[0] // 2
        return lambda d, h: rows_of(w_in, p * part + d * size[0] + h * half, half, q)

    def own_pieces(piece, axis, slots):
        c = at[axis]
        right, left = lax.rem(c + 1, 4), lax.rem(c + 3, 4)
        wanted = ((right, 0), (left, 1), (c, 0), (c, 1))
        return [load.copy(piece(*wanted[k]), slots.at[k]) for k in range(4)]

    w_ready = {
        (p, q): own_pieces(w_piece(p, q), p, w_loc.at[p, q]) for q in range(2) for p in range(3)
    }
    s_ready = own_pieces(s_piece, 2, s_loc)
    mid_ready = load.copy(near.at[1], mid)
    gain_ready = load.copy(gain_in, gain_sum.at[0])
    rest_ready = [
        load.copy(own, own_v), load.copy(tokens, tok_v), load.copy(summary, sum_v),
        load.copy(gain, gain_v), load.copy(cot, cot_v),
    ]
    met()
    link = Sender(send_sems, recv_sems)

    def halo():
        rows = []
        for j in (0, 2, 1):
            up = link.send(near.at[2, j], beside.at[0, j], row_peer(at, 1))
            down = link.send(near.at[0, j], beside.at[1, j], row_peer(at, -1))
            rows.append((j, up, down))
        yield
        mid_ready.wait()
        for j, up, down in rows[:2]:
            up.wait_recv()
            down.wait_recv()
            row_sum[j // 2] = added(mid.at[j], beside.at[0, j], beside.at[1, j]).astype(BF16)
        there = {"tx_0": lax.rem(z + (3 + 2 * x_hi), 4)}
        far = link.send(row_sum.at[x_hi], z_slot, there)
        yield
        far.wait_recv()
        message[...] = added(row_sum.at[1 - x_hi], z_slot).astype(BF16)
        last = link.send(message, x_slot, {"tx_1": 1 - x_hi})
        yield
        _, up, down = rows[2]
        up.wait_recv()
        down.wait_recv()
        for copy in rest_ready:
            copy.wait()
        own_v[...] += added(beside.at[0, 1], beside.at[1, 1])
        yield
        yield
        last.wait_recv()
        hidden_grad = own_v[...] + x_slot[...].astype(F32)
        scale = row_scale(tok_v[...])
        back = norm_back(tok_v[...], scale, gain_v[...], hidden_grad)
        grad_tokens[...] = (cot_v[...].astype(F32) + back).astype(BF16)

    def summaries():
        yield from scatter_ring(
            link, 2, at, s_piece, s_loc, s_ready, s_relay, s_direct, s_one
        )
        block = summary.shape[0]
        yield from scatter_direct(
            link, 0, at,
            lambda d: s_one.at[lax.rem(d, 2), :, pl.ds((d // 2) * block, block)],
            s_slots_x, s_two,
        )
        yield from scatter_direct(link, 1, at, lambda d: s_two.at[d], s_slots_y, s_sum)
        scale = row_scale(sum_v[...])
        back = norm_back(sum_v[...], scale, gain_v[...], s_sum[...])
        grad_summary[...] = back.astype(BF16)

    def weights(p, q):
        a, b, c = p, (p + 1) % 3, (p + 2) % 3
        first = p * part
        yield from scatter_ring(
            link, a, at, w_piece(p, q), w_loc.at[p, q], w_ready[p, q],
            w_relay.at[p, q], w_direct.at[p, q], w_one.at[p, q],
        )
        yield from scatter_direct(
            link, b, at,
            lambda d: w_one.at[p, q, d // 2, pl.ds(lax.rem(d, 2) * size[1], size[1])],
            w_slots_two.at[p, q], w_two.at[p, q],
        )
        base = first + at[a] * size[0]
        inner = base + at[b] * size[1]
        yield from scatter_direct(
            link, c, at,
            lambda d: w_two.at[p, q, pl.ds(pl.multiple_of(d * size[2], PACK), size[2])],
            w_slots_three.at[p, q],
            rows_of(w_out, inner + at[c] * size[2], size[2], q),
        )
        yield from gather_direct(
            link, c, at, lambda d: rows_of(w_out, inner + d * size[2], size[2], q)
        )
        yield from gather_direct(
            link, b, at, lambda d: rows_of(w_out, base + d * size[1], size[1], q)
        )
        yield from gather_ring(
            link, a, at,
            lambda d: rows_of(w_out, first + d * size[0], size[0], q),
            lambda d, h: rows_of(
                w_out, first + d * size[0] + h * (size[0] // 2), size[0] // 2, q
            ),
        )

    def gains():
        gain_ready.wait()
        for k in range(3):
            yield from scatter_direct(
                link, k, at, lambda d, k=k: gain_sum.at[k], gain_slots.at[k], gain_sum.at[k + 1]
            )
        total = jnp.sum(gain_sum[3], axis=0, keepdims=True)
        grad_gain[...] = total / gain_v[...]

    first_half = [weights(p, 0) for p in range(3)]
    second_half = [weights(p, 1) for p in range(3)]
    take_turns([*first_half, halo(), *second_half, summaries(), gains()])
    link.drain()


def exchange(
    near_grad, own_grad, sum_grad, w_part, gain_part, tokens, summary, norm_gain, cot
):
    rows, width = own_grad.shape
    block = summary.shape[0]
    vm = pl.BlockSpec(memory_space=pltpu.VMEM)
    total = w_part.shape[0] * width
    part = total // 3
    wide = width // 2
    sends = 6 + 2 + 6 + 3 + 3 + 6 * (6 + 3 + 3 + 3 + 3 + 4) + 9
    loads = 24 + 4 + 2 + 5
    sums = sum_grad.reshape(8, 4, 2 * block, width)
    grad_tokens, grad_summary, gain, w_all = pl.pallas_call(
        exchange_kernel,
        out_shape=(
            jax.ShapeDtypeStruct((rows, width), BF16),
            jax.ShapeDtypeStruct((block, width), BF16),
            jax.ShapeDtypeStruct((1, width), F32),
            jax.ShapeDtypeStruct((total, width), BF16),
        ),
        in_specs=[pl.BlockSpec(memory_space=pl.ANY)] * 9,
        out_specs=(vm,) * 4,
        scratch_shapes=[
            pltpu.VMEM((rows, width), F32),
            pltpu.VMEM((3, rows, width), BF16),
            pltpu.VMEM((rows, width), BF16),
            pltpu.VMEM((block, width), BF16),
            pltpu.VMEM((1, width), F32),
            pltpu.VMEM((rows, width), BF16),
            pltpu.VMEM((4, 4, 2 * block, width), BF16),
            pltpu.VMEM((3, 2, 4, part // 8, wide), BF16),
            pltpu.VMEM((2, 3, rows, width), BF16),
            pltpu.VMEM((2, rows, width), BF16),
            pltpu.VMEM((rows, width), BF16),
            pltpu.VMEM((rows, width), BF16),
            pltpu.VMEM((rows, width), BF16),
            pltpu.VMEM((2, 2, 4, 2 * block, width), BF16),
            pltpu.VMEM((2, 2, 4, 2 * block, width), BF16),
            pltpu.VMEM((2, 4, 2 * block, width), BF16),
            pltpu.VMEM((3, 4, block, width), BF16),
            pltpu.VMEM((4, block, width), BF16),
            pltpu.VMEM((3, block, width), BF16),
            pltpu.VMEM((block, width), F32),
            pltpu.VMEM((3, 2, 2, 2, part // 8, wide), BF16),
            pltpu.VMEM((3, 2, 2, 2, part // 8, wide), BF16),
            pltpu.VMEM((3, 2, 2, part // 8, wide), BF16),
            pltpu.VMEM((3, 2, 3, part // 16, wide), BF16),
            pltpu.VMEM((3, 2, part // 16, wide), BF16),
            pltpu.VMEM((3, 2, 3, part // 64, wide), BF16),
            pltpu.VMEM((4, 8, width), F32),
            pltpu.VMEM((3, 3, 8, width), F32),
            pltpu.SemaphoreType.DMA((loads,)),
            pltpu.SemaphoreType.DMA((sends,)),
            pltpu.SemaphoreType.DMA((sends,)),
        ],
        compiler_params=pltpu.CompilerParams(
            collective_id=1, has_side_effects=True, vmem_limit_bytes=60 * 1024 * 1024
        ),
        name="exchange",
    )(
        near_grad.reshape(3, 3, rows, width), own_grad, sums, w_part.reshape(total, width),
        gain_part, tokens, summary, norm_gain, cot,
    )
    return grad_tokens, grad_summary, gain, w_all.reshape(w_part.shape)


def row_scale(rows):
    values = rows.astype(F32)
    return lax.rsqrt(jnp.mean(values * values, axis=-1, keepdims=True) + epsilon)


def normalize(rows, gain):
    scale = row_scale(rows)
    return ((rows.astype(F32) * scale * gain).astype(BF16), scale)


def norm_back(rows, scale, gain, grad_norm):
    values = rows.astype(F32)
    scaled = gain * grad_norm
    return scale * scaled - values * scale**3 * jnp.mean(values * scaled, axis=-1, keepdims=True)


def dot(a, b, ca, cb):
    return lax.dot_general(a, b, (((ca,), (cb,)), ((), ())), preferred_element_type=F32)


def layer_kernel(
    counts, pattern, blocks, near, summ, w_in, tok, cot,
    updated, near_out, own_out, sum_out, w_out, gain_part,
    w, own_v, near_grad, own_grad, sum_grad, w_part, pack_sems, local_sems,
    xp, kp, vp, dkt, dvt, scores, probs, bias, qs, gs, qst, gst, acc, m_ref, l_ref, d_ref,
    q_all, g_all, o_all, dq_all,
):
    rows = tok.shape[0]
    width = tok.shape[1]
    quads = width // CHUNK
    head_size = width // HEADS
    stack = QUAD * rows
    factor = 1.0 / math.sqrt(head_size)
    n_blocks = summ.shape[0] // SBLK
    yp = kp
    zk = scores.at[:, 0:width]
    zv = scores.at[:, width : 2 * width]

    load = Loader(local_sems)
    own_ready = load.copy(near.at[NEAR // 2], own_v)
    w_ready = [load.copy(w_in.at[k], w.at[k]) for k in (0, 3, 1, 2)]

    grid_row = 4 * lax.axis_index("ty_0") + lax.axis_index("ty_1")
    grid_col = 2 * lax.axis_index("tx_0") + lax.axis_index("tx_1")
    meta = []
    for t in range(NEAR):
        r, c = grid_row + (t // 3 - 1), grid_col + (t % 3 - 1)
        inside = (r >= 0) & (r < 8) & (c >= 0) & (c < 8)
        n = counts[jnp.clip(r, 0, 7), jnp.clip(c, 0, 7)]
        meta.append(jnp.where(inside & (pattern[grid_row, grid_col, t] == 1), n, 0))
    for b in range(n_blocks):
        meta.append(jnp.where(blocks[0, 0, b] == 1, 1, 0))
    meta.append(counts[grid_row, grid_col])

    def packed(k, src, at, size):
        return pltpu.make_async_copy(
            src.at[pl.ds(0, size)], xp.at[pl.ds(pl.multiple_of(at, PACK), size)], pack_sems.at[k]
        )

    packs = []
    block_at = []
    total = jnp.int32(0)
    for b in range(n_blocks):
        block_at.append(total)
        flag = meta[NEAR + b]

        src = summ.at[pl.ds(b * SBLK, SBLK)]
        packs.append((flag == 1, packed(NEAR + b, src, total, SBLK)))
        total = total + SBLK * flag
    summ_end = total
    tile_at = []
    for t in range(NEAR):
        tile_at.append(total)
        n = meta[t]

        size = pl.multiple_of(((n + (PACK - 1)) // PACK) * PACK, PACK)
        packs.append((n > 0, packed(t, near.at[t], total, size)))
        total = total + size
    for live, copy in packs:
        pl.when(live)(copy.start)
    xp[pl.ds(pl.multiple_of(total, PACK), CHUNK), :] = jnp.zeros((CHUNK, width), BF16)
    chunks = (total + (CHUNK - 1)) // CHUNK

    place = lax.broadcasted_iota(jnp.int32, bias.shape, 1)
    live = place < summ_end
    for t in range(NEAR):
        live = live | ((place >= tile_at[t]) & (place < tile_at[t] + meta[t]))
    bias[...] = jnp.where(live, 0.0, -1e30)

    own_ready.wait()
    for copy in w_ready[:2]:
        copy.wait()
    own = own_v[...]
    valid = lax.broadcasted_iota(jnp.int32, (rows, width), 0) < meta[NEAR + n_blocks]
    masked = jnp.where(valid, cot[...].astype(F32), 0.0).astype(BF16)
    q_all[...] = (dot(own, w[0], 1, 0).astype(BF16).astype(F32) * factor).astype(BF16)
    g_all[...] = dot(masked, w[3], 1, 1).astype(BF16)

    for copy in w_ready[2:]:
        copy.wait()
    for live, copy in packs:
        pl.when(live)(copy.wait)

    def project(c, carry):
        at = pl.ds(pl.multiple_of(c * CHUNK, CHUNK), CHUNK)
        x = xp[at, :]
        kp[at, :] = dot(x, w[1], 1, 0).astype(BF16)
        vp[at, :] = dot(x, w[2], 1, 0).astype(BF16)
        return carry

    lax.fori_loop(0, chunks, project, 0)

    lane_head = lax.broadcasted_iota(jnp.int32, (rows, CHUNK), 1) // head_size
    low, high = slice(0, 128), slice(128, 256)

    for j in range(quads):
        cols = slice(j * CHUNK, (j + 1) * CHUNK)
        q_part = q_all[:, cols].astype(F32)
        g_part = g_all[:, cols].astype(F32)
        for i in range(QUAD):
            here = slice(i * rows, (i + 1) * rows)
            qs[here, :] = jnp.where(lane_head == i, q_part, 0.0).astype(BF16)
            gs[here, :] = jnp.where(lane_head == i, g_part, 0.0).astype(BF16)
        m_ref[...] = jnp.full(m_ref.shape, -3e38, F32)

        def score(c, carry):
            at = pl.ds(pl.multiple_of(c * CHUNK, CHUNK), CHUNK)
            s = dot(qs[...], kp[at, cols], 1, 1) + bias[0:1, at]
            scores[:, at] = s
            m_ref[...] = jnp.maximum(m_ref[...], jnp.maximum(s[:, low], s[:, high]))
            return carry

        lax.fori_loop(0, chunks, score, 0)
        m_ref[...] = jnp.broadcast_to(jnp.max(m_ref[...], axis=1, keepdims=True), m_ref.shape)
        l_ref[...] = jnp.zeros(l_ref.shape, F32)
        acc[...] = jnp.zeros(acc.shape, F32)

        def mix(c, carry):
            at = pl.ds(pl.multiple_of(c * CHUNK, CHUNK), CHUNK)
            s = scores[:, at]
            m = m_ref[...]
            e0 = jnp.exp(s[:, low] - m)
            e1 = jnp.exp(s[:, high] - m)
            l_ref[...] += e0 + e1
            e = jnp.concatenate([e0, e1], axis=1).astype(BF16)
            probs[:, at] = e
            acc[...] += dot(e, vp[at, cols], 1, 0)
            return carry

        lax.fori_loop(0, chunks, mix, 0)
        inv = 1.0 / jnp.sum(l_ref[...], axis=1, keepdims=True)
        out = acc[...] * inv
        d_ref[...] = jnp.broadcast_to(
            jnp.sum(out * gs[...].astype(F32), axis=1, keepdims=True), d_ref.shape
        )
        picked = jnp.zeros((rows, CHUNK), F32)
        for i in range(QUAD):
            here = slice(i * rows, (i + 1) * rows)
            picked = jnp.where(lane_head == i, out[here], picked)
        o_all[:, cols] = picked.astype(BF16)
        qst[...] = (qs[...].astype(F32) * inv).astype(BF16).T
        gst[...] = (gs[...].astype(F32) * inv).astype(BF16).T
        l_ref[...] = jnp.broadcast_to(inv, l_ref.shape)
        acc[...] = jnp.zeros(acc.shape, F32)

        def back(c, carry):
            at = pl.ds(pl.multiple_of(c * CHUNK, CHUNK), CHUNK)
            e = probs[:, at]
            dp = dot(gs[...], vp[at, cols], 1, 1)
            d = d_ref[...]
            delta = jnp.concatenate([dp[:, low] - d, dp[:, high] - d], axis=1)
            ds = (e.astype(F32) * delta).astype(BF16)
            acc[...] += dot(ds, kp[at, cols], 1, 0)
            dkt[cols, at] = dot(qst[...], ds, 1, 0).astype(BF16)
            dvt[cols, at] = dot(gst[...], e, 1, 0).astype(BF16)
            return carry

        lax.fori_loop(0, chunks, back, 0)
        inv2 = l_ref[...] * factor
        dq = acc[...] * jnp.concatenate([inv2, inv2], axis=1)
        picked = jnp.zeros((rows, CHUNK), F32)
        for i in range(QUAD):
            here = slice(i * rows, (i + 1) * rows)
            picked = jnp.where(lane_head == i, dq[here], picked)
        dq_all[:, cols] = picked.astype(BF16)

    w_part[0] = dot(own, dq_all[...], 0, 0).astype(BF16)
    w_part[3] = dot(o_all[...], masked, 0, 0).astype(BF16)
    sent = [load.copy(w_part.at[k], w_out.at[k]) for k in (0, 3)]
    mixed = dot(o_all[...], w[3], 1, 0)
    updated[...] = (tok[...].astype(F32) + jnp.where(valid, mixed, 0.0)).astype(BF16)

    zk[...] = jnp.zeros(zk.shape, F32)
    zv[...] = jnp.zeros(zv.shape, F32)
    own_part = dot(dq_all[...], w[0], 1, 1)
    gain_part[...] = jnp.sum(
        (own_part * own.astype(F32)).reshape(rows // 8, 8, width), axis=0
    )

    def finish(c, carry):
        at = pl.ds(pl.multiple_of(c * CHUNK, CHUNK), CHUNK)
        x = xp[at, :]
        dk = dkt[:, at]
        dv = dvt[:, at]
        zk[...] += dot(dk, x, 1, 0)
        zv[...] += dot(dv, x, 1, 0)
        yt = dot(w[1], dk, 1, 0) + dot(w[2], dv, 1, 0)
        y = yt.astype(BF16).T
        yp[at, :] = y
        gain_part[...] += jnp.sum(
            (y.astype(F32) * x.astype(F32)).reshape(CHUNK // 8, 8, width), axis=0
        )
        return carry

    lax.fori_loop(0, chunks, finish, 0)

    w_part[1] = zk[...].astype(BF16).T
    sent.append(load.copy(w_part.at[1], w_out.at[1]))
    w_part[2] = zv[...].astype(BF16).T
    sent.append(load.copy(w_part.at[2], w_out.at[2]))

    row_at = lax.broadcasted_iota(jnp.int32, (rows, width), 0)
    for t in range(NEAR):
        y = yp[pl.ds(pl.multiple_of(tile_at[t], PACK), rows), :].astype(F32)
        y = jnp.where(row_at < meta[t], y, 0.0)
        if t == NEAR // 2:
            own_grad[...] = y + own_part
            sent.append(load.copy(own_grad, own_out))
        else:
            near_grad[t] = y.astype(BF16)
            sent.append(load.copy(near_grad.at[t], near_out.at[t]))
    for b in range(n_blocks):
        y = yp[pl.ds(pl.multiple_of(block_at[b], SBLK), SBLK), :].astype(F32)
        keep = jnp.zeros((SBLK, width), jnp.int32) + meta[NEAR + b]
        sum_grad[b * SBLK : (b + 1) * SBLK, :] = jnp.where(keep == 1, y, 0.0).astype(BF16)
    sent.append(load.copy(sum_grad, sum_out))
    for copy in sent:
        copy.wait()


def layer(counts, pattern, blocks, near, summ, w, tok, cot):
    rows, width = tok.shape
    most = (NEAR * rows + summ.shape[0] + CHUNK - 1) // CHUNK * CHUNK
    stack = QUAD * rows
    vm = pl.BlockSpec(memory_space=pltpu.VMEM)
    sm = pl.BlockSpec(memory_space=pltpu.SMEM)
    far = pl.BlockSpec(memory_space=pl.ANY)
    n_blocks = summ.shape[0] // SBLK
    return pl.pallas_call(
        layer_kernel,
        out_shape=(
            jax.ShapeDtypeStruct((rows, width), BF16),
            jax.ShapeDtypeStruct((NEAR, rows, width), BF16),
            jax.ShapeDtypeStruct((rows, width), F32),
            jax.ShapeDtypeStruct(summ.shape, BF16),
            jax.ShapeDtypeStruct((4, width, width), BF16),
            jax.ShapeDtypeStruct((8, width), F32),
        ),
        in_specs=[sm] * 3 + [far] * 3 + [vm] * 2,
        out_specs=(vm, far, far, far, far, vm),
        scratch_shapes=[
            pltpu.VMEM((4, width, width), BF16),
            pltpu.VMEM((rows, width), BF16),
            pltpu.VMEM((NEAR, rows, width), BF16),
            pltpu.VMEM((rows, width), F32),
            pltpu.VMEM(summ.shape, BF16),
            pltpu.VMEM((4, width, width), BF16),
            pltpu.SemaphoreType.DMA((NEAR + n_blocks,)),
            pltpu.SemaphoreType.DMA((5 + 4 + NEAR + 2,)),
            pltpu.VMEM((most + CHUNK, width), BF16),
            pltpu.VMEM((most + CHUNK, width), BF16),
            pltpu.VMEM((most, width), BF16),
            pltpu.VMEM((width, most), BF16),
            pltpu.VMEM((width, most), BF16),
            pltpu.VMEM((stack, most), F32),
            pltpu.VMEM((stack, most), BF16),
            pltpu.VMEM((8, most), F32),
            pltpu.VMEM((stack, CHUNK), BF16),
            pltpu.VMEM((stack, CHUNK), BF16),
            pltpu.VMEM((CHUNK, stack), BF16),
            pltpu.VMEM((CHUNK, stack), BF16),
            pltpu.VMEM((stack, CHUNK), F32),
            pltpu.VMEM((stack, 128), F32),
            pltpu.VMEM((stack, 128), F32),
            pltpu.VMEM((stack, 128), F32),
            pltpu.VMEM((rows, width), BF16),
            pltpu.VMEM((rows, width), BF16),
            pltpu.VMEM((rows, width), BF16),
            pltpu.VMEM((rows, width), BF16),
        ],
        compiler_params=pltpu.CompilerParams(vmem_limit_bytes=63 * 1024 * 1024),
        name="layer",
    )(counts, pattern, blocks, near, summ, w, tok, cot)


def local(
    tokens, summary, counts, tile_pattern, summary_pattern, norm_gain, projections, cotangent
):
    rows, width = tokens.shape[2:]
    token_rows = tokens[0, 0]
    grads_in = cotangent[0, 0]
    gain = norm_gain.reshape(1, width)
    near, every = gather(token_rows, summary, gain)
    updated, near_grad, own_grad, sum_grad, w_part, gain_part = layer(
        counts, tile_pattern, summary_pattern, near, every, projections, token_rows, grads_in
    )
    grad_tokens, grad_summary, grad_gain, grad_proj = exchange(
        near_grad, own_grad, sum_grad, w_part, gain_part, token_rows, summary, gain, grads_in
    )
    return (
        updated.reshape(tokens.shape),
        grad_tokens.reshape(tokens.shape),
        grad_summary,
        grad_proj.astype(F32),
        grad_gain.reshape(width),
    )


def solution(mesh):
    finer = Mesh(
        mesh.devices.reshape(2, 4, 4, 2, mesh.shape["slide"]),
        ("ty_0", "ty_1", "tx_0", "tx_1", "slide"),
    )
    return jax.shard_map(
        local,
        mesh=finer,
        in_specs=(
            P(SLIDE_TY, TX, None, None),
            P(SLIDE_TY_TX, None),
            P("slide", None),
            P("slide", None, None),
            P(SLIDE_TY, TX, None),
            P(),
            P(),
            P(SLIDE_TY, TX, None, None),
        ),
        out_specs=(
            P(SLIDE_TY, TX, None, None),
            P(SLIDE_TY, TX, None, None),
            P(SLIDE_TY_TX, None),
            P("slide", None, None),
            P("slide"),
        ),
        check_vma=False,
    )
```

```python
import functools
import math

import jax
import jax.numpy as jnp
from jax import lax
from jax.experimental import pallas as pl
from jax.experimental.pallas import tpu as pltpu
from jax.sharding import Mesh
from jax.sharding import PartitionSpec as P

HEADS = 12
SBLK = 128
QUAD = 4
CHUNK = 256
PACK = 16
NEAR = 9
TX = ("tx_0", "tx_1")
SLIDE_TY = ("slide", "ty_0", "ty_1")
SLIDE_TY_TX = ("slide", "ty_0", "ty_1", "tx_0", "tx_1")
F32 = jnp.float32
BF16 = jnp.bfloat16
MESH = pl.DeviceIdType.MESH

epsilon = 1e-05


def places():
    return (
        2 * lax.axis_index("tx_1") + lax.axis_index("ty_0"),
        lax.axis_index("ty_1"),
        lax.axis_index("tx_0"),
    )


def peer(axis, at, by):
    there = lax.rem(at[axis] + (by + 4), 4)
    if axis == 0:
        return {"tx_1": there // 2, "ty_0": lax.rem(there, 2)}
    return {"ty_1": there} if axis == 1 else {"tx_0": there}


def row_peer(at, by):
    there = lax.rem(lax.axis_index("ty_0") * 4 + at[1] + (by + 8), 8)
    return {"ty_0": there // 4, "ty_1": lax.rem(there, 4)}


def greet(at):
    barrier = pltpu.get_barrier_semaphore()
    others = [peer(axis, at, by) for axis in range(3) for by in (1, 2, 3)]
    others += [row_peer(at, 1), row_peer(at, -1)]
    for other in others:
        pl.semaphore_signal(barrier, inc=1, device_id=other, device_id_type=MESH)
    return lambda: pl.semaphore_wait(barrier, len(others))


class Loader:
    def __init__(self, sems):
        self.sems, self.count = sems, 0

    def copy(self, src, dst):
        copy = pltpu.make_async_copy(src, dst, self.sems.at[self.count])
        self.count += 1
        copy.start()
        return copy


class Sender:
    def __init__(self, send_sems, recv_sems):
        self.send_sems, self.recv_sems = send_sems, recv_sems
        self.copies = []

    def send(self, src, dst, device):
        k = len(self.copies)
        copy = pltpu.make_async_remote_copy(
            src_ref=src,
            dst_ref=dst,
            send_sem=self.send_sems.at[k],
            recv_sem=self.recv_sems.at[k],
            device_id=device,
            device_id_type=MESH,
        )
        copy.start()
        self.copies.append(copy)
        return copy

    def drain(self):
        for copy in self.copies:
            copy.wait_send()


def take_turns(tasks):
    tasks = list(tasks)
    while tasks:
        tasks = [task for task in tasks if next(task, "end") != "end"]


def later(turns, task):
    for _ in range(turns):
        yield
    yield from task


def send_across(link, at, src, relay, slots):
    wide = src.shape[1] // 2
    halves = [slice(0, wide), slice(wide, 2 * wide)]
    ways = [peer(0, at, 1), peer(0, at, -1)]
    first = [link.send(src.at[:, halves[k]], relay.at[k], ways[k]) for k in range(2)]
    yield
    second = []
    for k in range(2):
        first[k].wait_recv()
        second.append(link.send(relay.at[k], slots[k].at[:, halves[k]], ways[k]))
    yield
    for copy in second:
        copy.wait_recv()


def added(*refs):
    total = refs[0][...].astype(F32)
    for ref in refs[1:]:
        total = total + ref[...].astype(F32)
    return total


def scatter_ring(link, axis, at, piece, held, ready, relay, direct, out):
    c = at[axis]
    right, left, across = [lax.rem(c + k, 4) for k in (1, 3, 2)]
    to_right, to_left = peer(axis, at, 1), peer(axis, at, -1)
    far_a = link.send(piece(across, 0), relay.at[0, 0], to_right)
    far_b = link.send(piece(across, 1), relay.at[0, 1], to_left)
    near_b = link.send(piece(right, 1), direct.at[0, 1], to_right)
    near_a = link.send(piece(left, 0), direct.at[1, 0], to_left)
    yield
    for copy in ready:
        copy.wait()
    far_a.wait_recv()
    relay[1, 0] = added(relay.at[0, 0], held.at[0]).astype(BF16)
    sum_a = link.send(relay.at[1, 0], direct.at[0, 0], to_right)
    far_b.wait_recv()
    relay[1, 1] = added(relay.at[0, 1], held.at[1]).astype(BF16)
    sum_b = link.send(relay.at[1, 1], direct.at[1, 1], to_left)
    yield
    for copy in (near_b, near_a, sum_a, sum_b):
        copy.wait_recv()
    for half in range(2):
        out[half] = added(held.at[2 + half], direct.at[0, half], direct.at[1, half]).astype(BF16)


def scatter_direct(link, axis, at, piece, slots, out):
    copies = [
        link.send(piece(lax.rem(at[axis] + k, 4)), slots.at[k - 1], peer(axis, at, k))
        for k in (1, 3, 2)
    ]
    yield
    for copy in copies:
        copy.wait_recv()
    total = added(piece(at[axis]), slots.at[0], slots.at[1], slots.at[2])
    out[...] = total.astype(out.dtype)


def gather_direct(link, axis, at, place):
    mine = place(at[axis])
    copies = [link.send(mine, mine, peer(axis, at, k)) for k in (1, 3, 2)]
    yield
    for copy in copies:
        copy.wait_recv()


def gather_ring(link, axis, at, place, half_place):
    c = at[axis]
    right, left = lax.rem(c + 1, 4), lax.rem(c + 3, 4)
    to_right, to_left = peer(axis, at, 1), peer(axis, at, -1)
    mine = place(c)
    one = link.send(mine, mine, to_right)
    two = link.send(mine, mine, to_left)
    yield
    one.wait_recv()
    half = half_place(left, 0)
    three = link.send(half, half, to_right)
    two.wait_recv()
    half = half_place(right, 1)
    four = link.send(half, half, to_left)
    yield
    three.wait_recv()
    four.wait_recv()


def gather_kernel(
    tokens, summary, gain, near, every, hidden, summ, relay, local_sems, send_sems, recv_sems
):
    at = places()
    x, y, z = at
    x_hi, x_lo = lax.axis_index("tx_1"), lax.axis_index("ty_0")
    met = greet(at)
    summ[...] = normalize(summary[...], gain[...])[0]
    hidden[...] = normalize(tokens[...], gain[...])[0]
    load = Loader(local_sems)
    own = every.at[x_lo, y, z, x_hi]
    kept = [load.copy(summ, own), load.copy(hidden, near.at[1, 1])]
    met()
    link = Sender(send_sems, recv_sems)
    from_x, from_z = 2 - 2 * x_hi, 2 * x_hi

    def halo():
        slots = [near.at[1, 2 - 2 * (lax.rem(x + by, 4) // 2)] for by in (1, 3)]
        beside = send_across(link, at, hidden, relay, slots)
        next(beside)
        rows = [
            link.send(hidden, near.at[0, 1], row_peer(at, 1)),
            link.send(hidden, near.at[2, 1], row_peer(at, -1)),
        ]
        yield
        next(beside)
        yield
        for _ in beside:
            pass
        there = {"tx_0": lax.rem(z + (5 - 2 * x_hi), 4)}
        beyond = link.send(near.at[1, from_x], near.at[1, from_z], there)
        rows.append(link.send(near.at[1, from_x], near.at[0, from_x], row_peer(at, 1)))
        rows.append(link.send(near.at[1, from_x], near.at[2, from_x], row_peer(at, -1)))
        yield
        beyond.wait_recv()
        rows.append(link.send(near.at[1, from_z], near.at[0, from_z], row_peer(at, 1)))
        rows.append(link.send(near.at[1, from_z], near.at[2, from_z], row_peer(at, -1)))
        yield
        yield
        yield
        for copy in rows:
            copy.wait_recv()

    def summaries():
        copies = [link.send(summ, own, peer(1, at, k)) for k in (1, 3, 2)]
        yield
        kept[0].wait()
        for copy in copies:
            copy.wait_recv()
        yield from gather_direct(
            link, 0, at, lambda d: every.at[lax.rem(d, 2), :, z, d // 2]
        )
        yield from gather_ring(
            link, 2, at, lambda d: every.at[:, :, d], lambda d, half: every.at[half, :, d]
        )

    take_turns([halo(), summaries()])
    kept[1].wait()
    link.drain()


def gather(tokens, summary, gain):
    rows, width = tokens.shape
    block = summary.shape[0]
    vm = pl.BlockSpec(memory_space=pltpu.VMEM)
    sends = 4 + 6 + 1 + 3 + 3 + 4
    near, every = pl.pallas_call(
        gather_kernel,
        out_shape=(
            jax.ShapeDtypeStruct((3, 3, rows, width), BF16),
            jax.ShapeDtypeStruct((2, 4, 4, 2, block, width), BF16),
        ),
        in_specs=[vm] * 3,
        out_specs=(pl.BlockSpec(memory_space=pltpu.HBM),) * 2,
        scratch_shapes=[
            pltpu.VMEM((rows, width), BF16),
            pltpu.VMEM((block, width), BF16),
            pltpu.VMEM((2, rows, width // 2), BF16),
            pltpu.SemaphoreType.DMA((2,)),
            pltpu.SemaphoreType.DMA((sends,)),
            pltpu.SemaphoreType.DMA((sends,)),
        ],
        compiler_params=pltpu.CompilerParams(
            collective_id=0, has_side_effects=True, vmem_limit_bytes=60 * 1024 * 1024
        ),
        name="gather",
    )(tokens, summary, gain)
    return near.reshape(NEAR, rows, width), every.reshape(-1, width)


def exchange_kernel(
    near, own, sums, w_in, gain_in, tokens, summary, gain, cot,
    grad_tokens, grad_summary, grad_gain, w_out,
    own_v, mid, tok_v, sum_v, gain_v, cot_v, s_loc, w_loc,
    beside, row_sum, z_slot, x_slot, x_relay, message,
    s_relay, s_direct, s_one, s_slots_x, s_two, s_slots_y, s_sum,
    w_relay, w_direct, w_one, w_slots_two, w_two, w_slots_three, w_three,
    gain_sum, gain_slots, local_sems, send_sems, recv_sems,
):
    at = places()
    x, y, z = at
    x_hi = lax.axis_index("tx_1")
    met = greet(at)
    load = Loader(local_sems)
    width = w_in.shape[1]
    wide = width // 2
    part = w_in.shape[0] // 3
    size = [part // 4, part // 16, part // 64]
    s_half = sums.shape[0] // 2

    def rows_of(ref, start, count, q):
        return ref.at[
            pl.ds(pl.multiple_of(start, PACK), count), q * wide : (q + 1) * wide
        ]

    def s_piece(d, h):
        return sums.at[pl.ds(h * s_half, s_half), d]

    def w_piece(p, q):
        half = size[0] // 2
        return lambda d, h: rows_of(w_in, p * part + d * size[0] + h * half, half, q)

    def own_pieces(piece, axis, slots):
        c = at[axis]
        right, left = lax.rem(c + 1, 4), lax.rem(c + 3, 4)
        wanted = ((right, 0), (left, 1), (c, 0), (c, 1))
        return [load.copy(piece(*wanted[k]), slots.at[k]) for k in range(4)]

    w_ready = {
        (p, q): own_pieces(w_piece(p, q), p, w_loc.at[p, q]) for q in range(2) for p in range(3)
    }
    s_ready = own_pieces(s_piece, 2, s_loc)
    mid_ready = load.copy(near.at[1], mid)
    gain_ready = load.copy(gain_in, gain_sum.at[0])
    rest_ready = [
        load.copy(own, own_v), load.copy(tokens, tok_v), load.copy(summary, sum_v),
        load.copy(gain, gain_v), load.copy(cot, cot_v),
    ]
    met()
    link = Sender(send_sems, recv_sems)

    def halo():
        rows = []
        for j in (0, 2, 1):
            up = link.send(near.at[2, j], beside.at[0, j], row_peer(at, 1))
            down = link.send(near.at[0, j], beside.at[1, j], row_peer(at, -1))
            rows.append((j, up, down))
        yield
        mid_ready.wait()
        for j, up, down in rows[:2]:
            up.wait_recv()
            down.wait_recv()
            row_sum[j // 2] = added(mid.at[j], beside.at[0, j], beside.at[1, j]).astype(BF16)
        there = {"tx_0": lax.rem(z + (3 + 2 * x_hi), 4)}
        far = link.send(row_sum.at[x_hi], z_slot, there)
        yield
        far.wait_recv()
        message[...] = added(row_sum.at[1 - x_hi], z_slot).astype(BF16)
        last = send_across(link, at, message, x_relay, (x_slot, x_slot))
        next(last)
        yield
        next(last)
        _, up, down = rows[2]
        up.wait_recv()
        down.wait_recv()
        for copy in rest_ready:
            copy.wait()
        own_v[...] += added(beside.at[0, 1], beside.at[1, 1])
        yield
        for _ in last:
            pass
        hidden_grad = own_v[...] + x_slot[...].astype(F32)
        scale = row_scale(tok_v[...])
        back = norm_back(tok_v[...], scale, gain_v[...], hidden_grad)
        grad_tokens[...] = (cot_v[...].astype(F32) + back).astype(BF16)

    def summaries():
        yield from scatter_ring(
            link, 2, at, s_piece, s_loc, s_ready, s_relay, s_direct, s_one
        )
        block = summary.shape[0]
        yield from scatter_direct(
            link, 0, at,
            lambda d: s_one.at[lax.rem(d, 2), :, pl.ds((d // 2) * block, block)],
            s_slots_x, s_two,
        )
        yield from scatter_direct(link, 1, at, lambda d: s_two.at[d], s_slots_y, s_sum)
        scale = row_scale(sum_v[...])
        back = norm_back(sum_v[...], scale, gain_v[...], s_sum[...])
        grad_summary[...] = back.astype(BF16)

    def weights(p, q):
        a, b, c = p, (p + 1) % 3, (p + 2) % 3
        first = p * part
        yield from scatter_ring(
            link, a, at, w_piece(p, q), w_loc.at[p, q], w_ready[p, q],
            w_relay.at[p, q], w_direct.at[p, q], w_one.at[p, q],
        )
        yield from scatter_direct(
            link, b, at,
            lambda d: w_one.at[p, q, d // 2, pl.ds(lax.rem(d, 2) * size[1], size[1])],
            w_slots_two.at[p, q], w_two.at[p, q],
        )
        base = first + at[a] * size[0]
        inner = base + at[b] * size[1]
        yield from scatter_direct(
            link, c, at,
            lambda d: w_two.at[p, q, pl.ds(pl.multiple_of(d * size[2], PACK), size[2])],
            w_slots_three.at[p, q],
            w_three.at[p, q],
        )
        mine = rows_of(w_out, inner + at[c] * size[2], size[2], q)
        copies = [link.send(w_three.at[p, q], mine, peer(c, at, k)) for k in (1, 3, 2)]
        kept = load.copy(w_three.at[p, q], mine)
        yield
        kept.wait()
        for copy in copies:
            copy.wait_recv()
        yield from gather_direct(
            link, b, at, lambda d: rows_of(w_out, base + d * size[1], size[1], q)
        )
        yield from gather_ring(
            link, a, at,
            lambda d: rows_of(w_out, first + d * size[0], size[0], q),
            lambda d, h: rows_of(
                w_out, first + d * size[0] + h * (size[0] // 2), size[0] // 2, q
            ),
        )

    def gains():
        gain_ready.wait()
        for k in range(3):
            yield from scatter_direct(
                link, k, at, lambda d, k=k: gain_sum.at[k], gain_slots.at[k], gain_sum.at[k + 1]
            )
        total = jnp.sum(gain_sum[3], axis=0, keepdims=True)
        grad_gain[...] = total / gain_v[...]

    first_half = [weights(p, 0) for p in range(3)]
    second_half = [weights(p, 1) for p in range(3)]
    take_turns(
        [*first_half, *second_half, later(1, halo()), later(1, summaries()), later(2, gains())]
    )
    link.drain()


def exchange(
    near_grad, own_grad, sum_grad, w_part, gain_part, tokens, summary, norm_gain, cot
):
    rows, width = own_grad.shape
    block = summary.shape[0]
    vm = pl.BlockSpec(memory_space=pltpu.VMEM)
    total = w_part.shape[0] * width
    part = total // 3
    wide = width // 2
    sends = 6 + 5 + 6 + 3 + 3 + 6 * (6 + 3 + 3 + 3 + 3 + 4) + 9
    loads = 24 + 4 + 2 + 5 + 6
    sums = sum_grad.reshape(8, 4, 2 * block, width)
    grad_tokens, grad_summary, gain, w_all = pl.pallas_call(
        exchange_kernel,
        out_shape=(
            jax.ShapeDtypeStruct((rows, width), BF16),
            jax.ShapeDtypeStruct((block, width), BF16),
            jax.ShapeDtypeStruct((1, width), F32),
            jax.ShapeDtypeStruct((total, width), BF16),
        ),
        in_specs=[pl.BlockSpec(memory_space=pltpu.HBM)] * 9,
        out_specs=(vm, vm, vm, pl.BlockSpec(memory_space=pltpu.HBM)),
        scratch_shapes=[
            pltpu.VMEM((rows, width), F32),
            pltpu.VMEM((3, rows, width), BF16),
            pltpu.VMEM((rows, width), BF16),
            pltpu.VMEM((block, width), BF16),
            pltpu.VMEM((1, width), F32),
            pltpu.VMEM((rows, width), BF16),
            pltpu.VMEM((4, 4, 2 * block, width), BF16),
            pltpu.VMEM((3, 2, 4, part // 8, wide), BF16),
            pltpu.VMEM((2, 3, rows, width), BF16),
            pltpu.VMEM((2, rows, width), BF16),
            pltpu.VMEM((rows, width), BF16),
            pltpu.VMEM((rows, width), BF16),
            pltpu.VMEM((2, rows, wide), BF16),
            pltpu.VMEM((rows, width), BF16),
            pltpu.VMEM((2, 2, 4, 2 * block, width), BF16),
            pltpu.VMEM((2, 2, 4, 2 * block, width), BF16),
            pltpu.VMEM((2, 4, 2 * block, width), BF16),
            pltpu.VMEM((3, 4, block, width), BF16),
            pltpu.VMEM((4, block, width), BF16),
            pltpu.VMEM((3, block, width), BF16),
            pltpu.VMEM((block, width), F32),
            pltpu.VMEM((3, 2, 2, 2, part // 8, wide), BF16),
            pltpu.VMEM((3, 2, 2, 2, part // 8, wide), BF16),
            pltpu.VMEM((3, 2, 2, part // 8, wide), BF16),
            pltpu.VMEM((3, 2, 3, part // 16, wide), BF16),
            pltpu.VMEM((3, 2, part // 16, wide), BF16),
            pltpu.VMEM((3, 2, 3, part // 64, wide), BF16),
            pltpu.VMEM((3, 2, part // 64, wide), BF16),
            pltpu.VMEM((4, 8, width), F32),
            pltpu.VMEM((3, 3, 8, width), F32),
            pltpu.SemaphoreType.DMA((loads,)),
            pltpu.SemaphoreType.DMA((sends,)),
            pltpu.SemaphoreType.DMA((sends,)),
        ],
        compiler_params=pltpu.CompilerParams(
            collective_id=1, has_side_effects=True, vmem_limit_bytes=60 * 1024 * 1024
        ),
        name="exchange",
    )(
        near_grad.reshape(3, 3, rows, width), own_grad, sums, w_part.reshape(total, width),
        gain_part, tokens, summary, norm_gain, cot,
    )
    return grad_tokens, grad_summary, gain, widen(w_all).reshape(w_part.shape)


def widen_kernel(narrow, wide, held, stage, in_sems, out_sems):
    rows = stage.shape[1]
    count = narrow.shape[0] // rows
    reads, writes = [], []
    for k in range(count):
        here = pl.ds(k * rows, rows)
        reads.append(pltpu.make_async_copy(narrow.at[here], held.at[k], in_sems.at[k]))
        reads[k].start()
    for k in range(count):
        if k >= 3:
            writes[k - 3].wait()
        reads[k].wait()
        stage[k % 3] = held[k].astype(F32)
        here = pl.ds(k * rows, rows)
        writes.append(pltpu.make_async_copy(stage.at[k % 3], wide.at[here], out_sems.at[k % 3]))
        writes[k].start()
    for copy in writes[-3:]:
        copy.wait()


def widen(narrow):
    total, width = narrow.shape
    count = 12
    far = pl.BlockSpec(memory_space=pltpu.HBM)
    return pl.pallas_call(
        widen_kernel,
        out_shape=jax.ShapeDtypeStruct((total, width), F32),
        in_specs=[far],
        out_specs=far,
        scratch_shapes=[
            pltpu.VMEM((count, total // count, width), BF16),
            pltpu.VMEM((3, total // count, width), F32),
            pltpu.SemaphoreType.DMA((count,)),
            pltpu.SemaphoreType.DMA((3,)),
        ],
        compiler_params=pltpu.CompilerParams(vmem_limit_bytes=60 * 1024 * 1024),
        name="widen",
    )(narrow)


def row_scale(rows):
    values = rows.astype(F32)
    return lax.rsqrt(jnp.mean(values * values, axis=-1, keepdims=True) + epsilon)


def normalize(rows, gain):
    scale = row_scale(rows)
    return ((rows.astype(F32) * scale * gain).astype(BF16), scale)


def norm_back(rows, scale, gain, grad_norm):
    values = rows.astype(F32)
    scaled = gain * grad_norm
    return scale * scaled - values * scale**3 * jnp.mean(values * scaled, axis=-1, keepdims=True)


def dot(a, b, ca, cb):
    return lax.dot_general(a, b, (((ca,), (cb,)), ((), ())), preferred_element_type=F32)


def layer_kernel(
    counts, pattern, blocks, near, summ, w_in, tok, cot,
    updated, near_out, own_out, sum_out, w_out, gain_part,
    w, own_v, near_grad, own_grad, sum_grad, w_part, pack_sems, local_sems,
    xp, kp, vp, dkt, dvt, scores, probs, bias, qs, gs, qst, gst, acc, m_ref, l_ref, d_ref,
    q_all, g_all, o_all, dq_all,
):
    rows = tok.shape[0]
    width = tok.shape[1]
    quads = width // CHUNK
    head_size = width // HEADS
    stack = QUAD * rows
    factor = 1.0 / math.sqrt(head_size)
    n_blocks = summ.shape[0] // SBLK
    yp = kp
    zk = scores.at[:, 0:width]
    zv = scores.at[:, width : 2 * width]

    load = Loader(local_sems)
    own_ready = load.copy(near.at[NEAR // 2], own_v)
    w_ready = [load.copy(w_in.at[k], w.at[k]) for k in (0, 3, 1, 2)]

    grid_row = 4 * lax.axis_index("ty_0") + lax.axis_index("ty_1")
    grid_col = 2 * lax.axis_index("tx_0") + lax.axis_index("tx_1")
    meta = []
    for t in range(NEAR):
        r, c = grid_row + (t // 3 - 1), grid_col + (t % 3 - 1)
        inside = (r >= 0) & (r < 8) & (c >= 0) & (c < 8)
        n = counts[jnp.clip(r, 0, 7), jnp.clip(c, 0, 7)]
        meta.append(jnp.where(inside & (pattern[grid_row, grid_col, t] == 1), n, 0))
    for b in range(n_blocks):
        meta.append(jnp.where(blocks[0, 0, b] == 1, 1, 0))
    meta.append(counts[grid_row, grid_col])

    def packed(k, src, at, size):
        return pltpu.make_async_copy(
            src.at[pl.ds(0, size)], xp.at[pl.ds(pl.multiple_of(at, PACK), size)], pack_sems.at[k]
        )

    packs = []
    block_at = []
    total = jnp.int32(0)
    for b in range(n_blocks):
        block_at.append(total)
        flag = meta[NEAR + b]

        src = summ.at[pl.ds(b * SBLK, SBLK)]
        packs.append((flag == 1, packed(NEAR + b, src, total, SBLK)))
        total = total + SBLK * flag
    summ_end = total
    tile_at = []
    for t in range(NEAR):
        tile_at.append(total)
        n = meta[t]

        size = pl.multiple_of(((n + (PACK - 1)) // PACK) * PACK, PACK)
        packs.append((n > 0, packed(t, near.at[t], total, size)))
        total = total + size
    for live, copy in packs:
        pl.when(live)(copy.start)
    xp[pl.ds(pl.multiple_of(total, PACK), CHUNK), :] = jnp.zeros((CHUNK, width), BF16)
    chunks = (total + (CHUNK - 1)) // CHUNK

    place = lax.broadcasted_iota(jnp.int32, bias.shape, 1)
    live = place < summ_end
    for t in range(NEAR):
        live = live | ((place >= tile_at[t]) & (place < tile_at[t] + meta[t]))
    bias[...] = jnp.where(live, 0.0, -1e30)

    own_ready.wait()
    for copy in w_ready[:2]:
        copy.wait()
    own = own_v[...]
    valid = lax.broadcasted_iota(jnp.int32, (rows, width), 0) < meta[NEAR + n_blocks]
    masked = jnp.where(valid, cot[...].astype(F32), 0.0).astype(BF16)
    q_all[...] = (dot(own, w[0], 1, 0).astype(BF16).astype(F32) * factor).astype(BF16)
    g_all[...] = dot(masked, w[3], 1, 1).astype(BF16)

    for copy in w_ready[2:]:
        copy.wait()
    for live, copy in packs:
        pl.when(live)(copy.wait)

    def sweep(body):
        def pair(c, carry):
            body(pl.multiple_of(c * (2 * CHUNK), 2 * CHUNK), 2 * CHUNK)
            return carry

        def four(c, carry):
            body(pl.multiple_of(c * (4 * CHUNK), 4 * CHUNK), 4 * CHUNK)
            return carry

        lax.fori_loop(0, chunks // 4, four, 0)
        lax.fori_loop(chunks // 4 * 2, chunks // 2, pair, 0)

        @pl.when(lax.rem(chunks, 2) == 1)
        def _():
            body(pl.multiple_of((chunks - 1) * CHUNK, CHUNK), CHUNK)

    def project(start, size):
        at = pl.ds(start, size)
        x = xp[at, :]
        kp[at, :] = dot(x, w[1], 1, 0).astype(BF16)
        vp[at, :] = dot(x, w[2], 1, 0).astype(BF16)

    sweep(project)

    lane_head = lax.broadcasted_iota(jnp.int32, (rows, CHUNK), 1) // head_size

    def lanes(values):
        return [values[:, k : k + 128] for k in range(0, values.shape[1], 128)]


    def stack_up(j):
        q_part = q_all[:, j * CHUNK : (j + 1) * CHUNK].astype(F32)
        g_part = g_all[:, j * CHUNK : (j + 1) * CHUNK].astype(F32)
        for i in range(QUAD):
            here = slice(i * rows, (i + 1) * rows)
            qs[j % 2, here, :] = jnp.where(lane_head == i, q_part, 0.0).astype(BF16)
            gs[j % 2, here, :] = jnp.where(lane_head == i, g_part, 0.0).astype(BF16)
        m_ref[...] = jnp.full(m_ref.shape, -3e38, F32)

    def score(j, start, size):
        at = pl.ds(start, size)
        s = dot(qs[j % 2], kp[at, j * CHUNK : (j + 1) * CHUNK], 1, 1) + bias[0:1, at]
        scores[:, at] = s
        most = m_ref[...]
        for part in lanes(s):
            most = jnp.maximum(most, part)
        m_ref[...] = most

    stack_up(0)
    sweep(functools.partial(score, 0))
    for j in range(quads):
        cols = slice(j * CHUNK, (j + 1) * CHUNK)
        q_now, g_now = qs.at[j % 2], gs.at[j % 2]
        m_ref[...] = jnp.broadcast_to(jnp.max(m_ref[...], axis=1, keepdims=True), m_ref.shape)
        l_ref[...] = jnp.zeros(l_ref.shape, F32)
        acc[...] = jnp.zeros(acc.shape, F32)

        def mix(start, size):
            at = pl.ds(start, size)
            m = m_ref[...]
            e = [jnp.exp(part - m) for part in lanes(scores[:, at])]
            total = l_ref[...]
            for part in e:
                total = total + part
            l_ref[...] = total
            e = jnp.concatenate(e, axis=1).astype(BF16)
            probs[:, at] = e
            acc[...] += dot(e, vp[at, cols], 1, 0)

        sweep(mix)
        inv = 1.0 / jnp.sum(l_ref[...], axis=1, keepdims=True)
        out = acc[...] * inv
        d_ref[...] = jnp.broadcast_to(
            jnp.sum(out * g_now[...].astype(F32), axis=1, keepdims=True), d_ref.shape
        )
        picked = jnp.zeros((rows, CHUNK), F32)
        for i in range(QUAD):
            here = slice(i * rows, (i + 1) * rows)
            picked = jnp.where(lane_head == i, out[here], picked)
        o_all[:, cols] = picked.astype(BF16)
        qst[...] = (q_now[...].astype(F32) * inv).astype(BF16).T
        gst[...] = (g_now[...].astype(F32) * inv).astype(BF16).T
        l_ref[...] = jnp.broadcast_to(inv, l_ref.shape)
        acc[...] = jnp.zeros(acc.shape, F32)
        if j + 1 < quads:
            stack_up(j + 1)

        def back(start, size):
            at = pl.ds(start, size)
            e = probs[:, at]
            d = d_ref[...]
            dp = dot(g_now[...], vp[at, cols], 1, 1)
            delta = jnp.concatenate([part - d for part in lanes(dp)], axis=1)
            ds = (e.astype(F32) * delta).astype(BF16)
            acc[...] += dot(ds, kp[at, cols], 1, 0)
            dkt[cols, at] = dot(qst[...], ds, 1, 0).astype(BF16)
            dvt[cols, at] = dot(gst[...], e, 1, 0).astype(BF16)
            if j + 1 < quads:
                score(j + 1, start, size)

        sweep(back)
        inv2 = l_ref[...] * factor
        dq = acc[...] * jnp.concatenate([inv2, inv2], axis=1)
        picked = jnp.zeros((rows, CHUNK), F32)
        for i in range(QUAD):
            here = slice(i * rows, (i + 1) * rows)
            picked = jnp.where(lane_head == i, dq[here], picked)
        dq_all[:, cols] = picked.astype(BF16)

    w_part[0] = dot(own, dq_all[...], 0, 0).astype(BF16)
    w_part[3] = dot(o_all[...], masked, 0, 0).astype(BF16)
    sent = [load.copy(w_part.at[k], w_out.at[k]) for k in (0, 3)]
    mixed = dot(o_all[...], w[3], 1, 0)
    updated[...] = (tok[...].astype(F32) + jnp.where(valid, mixed, 0.0)).astype(BF16)

    zk[...] = jnp.zeros(zk.shape, F32)
    zv[...] = jnp.zeros(zv.shape, F32)
    own_part = dot(dq_all[...], w[0], 1, 1)
    gain_part[...] = jnp.sum(
        (own_part * own.astype(F32)).reshape(rows // 8, 8, width), axis=0
    )

    def finish(start, size):
        at = pl.ds(start, size)
        x = xp[at, :]
        dk = dkt[:, at]
        dv = dvt[:, at]
        zk[...] += dot(dk, x, 1, 0)
        zv[...] += dot(dv, x, 1, 0)
        yt = dot(w[1], dk, 1, 0) + dot(w[2], dv, 1, 0)
        y = yt.astype(BF16).T
        yp[at, :] = y
        gain_part[...] += jnp.sum(
            (y.astype(F32) * x.astype(F32)).reshape(size // 8, 8, width), axis=0
        )

    sweep(finish)

    w_part[1] = zk[...].astype(BF16).T
    sent.append(load.copy(w_part.at[1], w_out.at[1]))
    w_part[2] = zv[...].astype(BF16).T
    sent.append(load.copy(w_part.at[2], w_out.at[2]))

    row_at = lax.broadcasted_iota(jnp.int32, (rows, width), 0)
    for t in range(NEAR):
        y = yp[pl.ds(pl.multiple_of(tile_at[t], PACK), rows), :].astype(F32)
        y = jnp.where(row_at < meta[t], y, 0.0)
        if t == NEAR // 2:
            own_grad[...] = y + own_part
            sent.append(load.copy(own_grad, own_out))
        else:
            near_grad[t] = y.astype(BF16)
            sent.append(load.copy(near_grad.at[t], near_out.at[t]))
    for b in range(n_blocks):
        y = yp[pl.ds(pl.multiple_of(block_at[b], SBLK), SBLK), :].astype(F32)
        keep = jnp.zeros((SBLK, width), jnp.int32) + meta[NEAR + b]
        sum_grad[b * SBLK : (b + 1) * SBLK, :] = jnp.where(keep == 1, y, 0.0).astype(BF16)
    sent.append(load.copy(sum_grad, sum_out))
    for copy in sent:
        copy.wait()


def layer(counts, pattern, blocks, near, summ, w, tok, cot):
    rows, width = tok.shape
    most = (NEAR * rows + summ.shape[0] + CHUNK - 1) // CHUNK * CHUNK
    stack = QUAD * rows
    vm = pl.BlockSpec(memory_space=pltpu.VMEM)
    sm = pl.BlockSpec(memory_space=pltpu.SMEM)
    far = pl.BlockSpec(memory_space=pl.ANY)
    n_blocks = summ.shape[0] // SBLK
    return pl.pallas_call(
        layer_kernel,
        out_shape=(
            jax.ShapeDtypeStruct((rows, width), BF16),
            jax.ShapeDtypeStruct((NEAR, rows, width), BF16),
            jax.ShapeDtypeStruct((rows, width), F32),
            jax.ShapeDtypeStruct(summ.shape, BF16),
            jax.ShapeDtypeStruct((4, width, width), BF16),
            jax.ShapeDtypeStruct((8, width), F32),
        ),
        in_specs=[sm] * 3 + [far] * 3 + [vm] * 2,
        out_specs=(vm, far, far, far, far, vm),
        scratch_shapes=[
            pltpu.VMEM((4, width, width), BF16),
            pltpu.VMEM((rows, width), BF16),
            pltpu.VMEM((NEAR, rows, width), BF16),
            pltpu.VMEM((rows, width), F32),
            pltpu.VMEM(summ.shape, BF16),
            pltpu.VMEM((4, width, width), BF16),
            pltpu.SemaphoreType.DMA((NEAR + n_blocks,)),
            pltpu.SemaphoreType.DMA((5 + 4 + NEAR + 2,)),
            pltpu.VMEM((most + CHUNK, width), BF16),
            pltpu.VMEM((most + CHUNK, width), BF16),
            pltpu.VMEM((most, width), BF16),
            pltpu.VMEM((width, most), BF16),
            pltpu.VMEM((width, most), BF16),
            pltpu.VMEM((stack, most), F32),
            pltpu.VMEM((stack, most), BF16),
            pltpu.VMEM((8, most), F32),
            pltpu.VMEM((2, stack, CHUNK), BF16),
            pltpu.VMEM((2, stack, CHUNK), BF16),
            pltpu.VMEM((CHUNK, stack), BF16),
            pltpu.VMEM((CHUNK, stack), BF16),
            pltpu.VMEM((stack, CHUNK), F32),
            pltpu.VMEM((stack, 128), F32),
            pltpu.VMEM((stack, 128), F32),
            pltpu.VMEM((stack, 128), F32),
            pltpu.VMEM((rows, width), BF16),
            pltpu.VMEM((rows, width), BF16),
            pltpu.VMEM((rows, width), BF16),
            pltpu.VMEM((rows, width), BF16),
        ],
        compiler_params=pltpu.CompilerParams(vmem_limit_bytes=63 * 1024 * 1024),
        name="layer",
    )(counts, pattern, blocks, near, summ, w, tok, cot)


def local(
    tokens, summary, counts, tile_pattern, summary_pattern, norm_gain, projections, cotangent
):
    rows, width = tokens.shape[2:]
    token_rows = tokens[0, 0]
    grads_in = cotangent[0, 0]
    gain = norm_gain.reshape(1, width)
    near, every = gather(token_rows, summary, gain)
    updated, near_grad, own_grad, sum_grad, w_part, gain_part = layer(
        counts, tile_pattern, summary_pattern, near, every, projections, token_rows, grads_in
    )
    grad_tokens, grad_summary, grad_gain, grad_proj = exchange(
        near_grad, own_grad, sum_grad, w_part, gain_part, token_rows, summary, gain, grads_in
    )
    return (
        updated.reshape(tokens.shape),
        grad_tokens.reshape(tokens.shape),
        grad_summary,
        grad_proj,
        grad_gain.reshape(width),
    )


def solution(mesh):
    finer = Mesh(
        mesh.devices.reshape(2, 4, 4, 2, mesh.shape["slide"]),
        ("ty_0", "ty_1", "tx_0", "tx_1", "slide"),
    )
    return jax.shard_map(
        local,
        mesh=finer,
        in_specs=(
            P(SLIDE_TY, TX, None, None),
            P(SLIDE_TY_TX, None),
            P("slide", None),
            P("slide", None, None),
            P(SLIDE_TY, TX, None),
            P(),
            P(),
            P(SLIDE_TY, TX, None, None),
        ),
        out_specs=(
            P(SLIDE_TY, TX, None, None),
            P(SLIDE_TY, TX, None, None),
            P(SLIDE_TY_TX, None),
            P("slide", None, None),
            P("slide"),
        ),
        check_vma=False,
    )
```

```python
import functools
import math

import jax
import jax.numpy as jnp
from jax import lax
from jax.experimental import pallas as pl
from jax.experimental.pallas import tpu as pltpu
from jax.sharding import Mesh
from jax.sharding import PartitionSpec as P

HEADS = 12
SBLK = 128
QUAD = 4
CHUNK = 256
PACK = 16
NEAR = 9
TX = ("tx_0", "tx_1")
SLIDE_TY = ("slide", "ty_0", "ty_1")
SLIDE_TY_TX = ("slide", "ty_0", "ty_1", "tx_0", "tx_1")
F32 = jnp.float32
BF16 = jnp.bfloat16
MESH = pl.DeviceIdType.MESH

epsilon = 1e-05


def places():
    return (
        2 * lax.axis_index("tx_1") + lax.axis_index("ty_0"),
        lax.axis_index("ty_1"),
        lax.axis_index("tx_0"),
    )


def peer(axis, at, by):
    there = lax.rem(at[axis] + (by + 4), 4)
    if axis == 0:
        return {"tx_1": there // 2, "ty_0": lax.rem(there, 2)}
    return {"ty_1": there} if axis == 1 else {"tx_0": there}


def row_peer(at, by):
    there = lax.rem(lax.axis_index("ty_0") * 4 + at[1] + (by + 8), 8)
    return {"ty_0": there // 4, "ty_1": lax.rem(there, 4)}


def greet(at):
    barrier = pltpu.get_barrier_semaphore()
    others = [peer(axis, at, by) for axis in range(3) for by in (1, 2, 3)]
    others += [row_peer(at, 1), row_peer(at, -1)]
    for other in others:
        pl.semaphore_signal(barrier, inc=1, device_id=other, device_id_type=MESH)
    return lambda: pl.semaphore_wait(barrier, len(others))


class Loader:
    def __init__(self, sems):
        self.sems, self.count = sems, 0

    def copy(self, src, dst):
        copy = pltpu.make_async_copy(src, dst, self.sems.at[self.count])
        self.count += 1
        copy.start()
        return copy


class Sender:
    def __init__(self, send_sems, recv_sems):
        self.send_sems, self.recv_sems = send_sems, recv_sems
        self.copies = []

    def send(self, src, dst, device):
        k = len(self.copies)
        copy = pltpu.make_async_remote_copy(
            src_ref=src,
            dst_ref=dst,
            send_sem=self.send_sems.at[k],
            recv_sem=self.recv_sems.at[k],
            device_id=device,
            device_id_type=MESH,
        )
        copy.start()
        self.copies.append(copy)
        return copy

    def drain(self):
        for copy in self.copies:
            copy.wait_send()


def take_turns(tasks):
    tasks = list(tasks)
    while tasks:
        tasks = [task for task in tasks if next(task, "end") != "end"]


def later(turns, task):
    for _ in range(turns):
        yield
    yield from task


def send_across(link, at, src, relay, slots):
    wide = src.shape[1] // 2
    halves = [slice(0, wide), slice(wide, 2 * wide)]
    ways = [peer(0, at, 1), peer(0, at, -1)]
    first = [link.send(src.at[:, halves[k]], relay.at[k], ways[k]) for k in range(2)]
    yield
    second = []
    for k in range(2):
        first[k].wait_recv()
        second.append(link.send(relay.at[k], slots[k].at[:, halves[k]], ways[k]))
    yield
    for copy in second:
        copy.wait_recv()


def added(*refs):
    total = refs[0][...].astype(F32)
    for ref in refs[1:]:
        total = total + ref[...].astype(F32)
    return total


def scatter_ring(link, axis, at, piece, held, ready, relay, direct, out):
    c = at[axis]
    right, left, across = [lax.rem(c + k, 4) for k in (1, 3, 2)]
    to_right, to_left = peer(axis, at, 1), peer(axis, at, -1)
    far_a = link.send(piece(across, 0), relay.at[0, 0], to_right)
    far_b = link.send(piece(across, 1), relay.at[0, 1], to_left)
    near_b = link.send(piece(right, 1), direct.at[0, 1], to_right)
    near_a = link.send(piece(left, 0), direct.at[1, 0], to_left)
    yield
    for copy in ready:
        copy.wait()
    far_a.wait_recv()
    relay[1, 0] = added(relay.at[0, 0], held.at[0]).astype(BF16)
    sum_a = link.send(relay.at[1, 0], direct.at[0, 0], to_right)
    far_b.wait_recv()
    relay[1, 1] = added(relay.at[0, 1], held.at[1]).astype(BF16)
    sum_b = link.send(relay.at[1, 1], direct.at[1, 1], to_left)
    yield
    for copy in (near_b, near_a, sum_a, sum_b):
        copy.wait_recv()
    for half in range(2):
        out[half] = added(held.at[2 + half], direct.at[0, half], direct.at[1, half]).astype(BF16)


def scatter_direct(link, axis, at, piece, slots, out):
    copies = [
        link.send(piece(lax.rem(at[axis] + k, 4)), slots.at[k - 1], peer(axis, at, k))
        for k in (1, 3, 2)
    ]
    yield
    for copy in copies:
        copy.wait_recv()
    total = added(piece(at[axis]), slots.at[0], slots.at[1], slots.at[2])
    out[...] = total.astype(out.dtype)


def gather_direct(link, axis, at, place):
    mine = place(at[axis])
    copies = [link.send(mine, mine, peer(axis, at, k)) for k in (1, 3, 2)]
    yield
    for copy in copies:
        copy.wait_recv()


def gather_ring(link, axis, at, place, half_place):
    c = at[axis]
    right, left = lax.rem(c + 1, 4), lax.rem(c + 3, 4)
    to_right, to_left = peer(axis, at, 1), peer(axis, at, -1)
    mine = place(c)
    one = link.send(mine, mine, to_right)
    two = link.send(mine, mine, to_left)
    yield
    one.wait_recv()
    half = half_place(left, 0)
    three = link.send(half, half, to_right)
    two.wait_recv()
    half = half_place(right, 1)
    four = link.send(half, half, to_left)
    yield
    three.wait_recv()
    four.wait_recv()


def gather_kernel(
    tokens, summary, gain, near, every, hidden, summ, relay, local_sems, send_sems, recv_sems
):
    at = places()
    x, y, z = at
    x_hi, x_lo = lax.axis_index("tx_1"), lax.axis_index("ty_0")
    met = greet(at)
    summ[...] = normalize(summary[...], gain[...].reshape(1, -1))[0]
    hidden[...] = normalize(tokens[...], gain[...].reshape(1, -1))[0]
    load = Loader(local_sems)
    own = every.at[x_lo, y, z, x_hi]
    kept = [load.copy(summ, own), load.copy(hidden, near.at[1, 1])]
    met()
    link = Sender(send_sems, recv_sems)
    from_x, from_z = 2 - 2 * x_hi, 2 * x_hi

    def halo():
        slots = [near.at[1, 2 - 2 * (lax.rem(x + by, 4) // 2)] for by in (1, 3)]
        beside = send_across(link, at, hidden, relay, slots)
        next(beside)
        rows = [
            link.send(hidden, near.at[0, 1], row_peer(at, 1)),
            link.send(hidden, near.at[2, 1], row_peer(at, -1)),
        ]
        yield
        next(beside)
        yield
        for _ in beside:
            pass
        there = {"tx_0": lax.rem(z + (5 - 2 * x_hi), 4)}
        beyond = link.send(near.at[1, from_x], near.at[1, from_z], there)
        rows.append(link.send(near.at[1, from_x], near.at[0, from_x], row_peer(at, 1)))
        rows.append(link.send(near.at[1, from_x], near.at[2, from_x], row_peer(at, -1)))
        yield
        beyond.wait_recv()
        rows.append(link.send(near.at[1, from_z], near.at[0, from_z], row_peer(at, 1)))
        rows.append(link.send(near.at[1, from_z], near.at[2, from_z], row_peer(at, -1)))
        yield
        yield
        yield
        for copy in rows:
            copy.wait_recv()

    def summaries():
        copies = [link.send(summ, own, peer(1, at, k)) for k in (1, 3, 2)]
        yield
        kept[0].wait()
        for copy in copies:
            copy.wait_recv()
        yield from gather_direct(
            link, 0, at, lambda d: every.at[lax.rem(d, 2), :, z, d // 2]
        )
        yield from gather_ring(
            link, 2, at, lambda d: every.at[:, :, d], lambda d, half: every.at[half, :, d]
        )

    take_turns([halo(), summaries()])
    kept[1].wait()
    link.drain()


def gather(tokens, summary, gain):
    rows, width = tokens.shape
    block = summary.shape[0]
    vm = pl.BlockSpec(memory_space=pltpu.VMEM)
    sends = 4 + 6 + 1 + 3 + 3 + 4
    near, every = pl.pallas_call(
        gather_kernel,
        out_shape=(
            jax.ShapeDtypeStruct((3, 3, rows, width), BF16),
            jax.ShapeDtypeStruct((2, 4, 4, 2, block, width), BF16),
        ),
        in_specs=[vm] * 3,
        out_specs=(pl.BlockSpec(memory_space=pltpu.HBM),) * 2,
        scratch_shapes=[
            pltpu.VMEM((rows, width), BF16),
            pltpu.VMEM((block, width), BF16),
            pltpu.VMEM((2, rows, width // 2), BF16),
            pltpu.SemaphoreType.DMA((2,)),
            pltpu.SemaphoreType.DMA((sends,)),
            pltpu.SemaphoreType.DMA((sends,)),
        ],
        compiler_params=pltpu.CompilerParams(
            collective_id=0, has_side_effects=True, vmem_limit_bytes=60 * 1024 * 1024
        ),
        name="gather",
    )(tokens, summary, gain)
    return near.reshape(NEAR, rows, width), every.reshape(-1, width)


def exchange_kernel(
    near, own, sums, w_in, gain_in, tokens, summary, gain, cot,
    grad_tokens, grad_summary, grad_gain, w_out,
    own_v, mid, tok_v, sum_v, cot_v, s_loc, w_loc,
    beside, row_sum, z_slot, x_slot, x_relay, message,
    s_relay, s_direct, s_one, s_slots_x, s_two, s_slots_y, s_sum,
    w_relay, w_direct, w_one, w_slots_two, w_two, w_slots_three, w_three,
    gain_sum, gain_slots, local_sems, send_sems, recv_sems,
):
    at = places()
    x, y, z = at
    x_hi = lax.axis_index("tx_1")
    met = greet(at)
    load = Loader(local_sems)
    part = w_in.shape[1] // 3
    size = [part // 4, part // 16, part // 64]
    s_half = sums.shape[0] // 2

    def rows_of(ref, start, count, q):
        return ref.at[q, pl.ds(pl.multiple_of(start, PACK), count)]

    def s_piece(d, h):
        return sums.at[pl.ds(h * s_half, s_half), d]

    def w_piece(p, q):
        half = size[0] // 2
        return lambda d, h: rows_of(w_in, p * part + d * size[0] + h * half, half, q)

    def own_pieces(piece, axis, slots):
        c = at[axis]
        right, left = lax.rem(c + 1, 4), lax.rem(c + 3, 4)
        wanted = ((right, 0), (left, 1), (c, 0), (c, 1))
        return [load.copy(piece(*wanted[k]), slots.at[k]) for k in range(4)]

    w_ready = {
        (p, q): own_pieces(w_piece(p, q), p, w_loc.at[p, q]) for q in range(2) for p in range(3)
    }
    s_ready = own_pieces(s_piece, 2, s_loc)
    mid_ready = load.copy(near.at[1], mid)
    gain_ready = load.copy(gain_in, gain_sum.at[0])
    rest_ready = [
        load.copy(own, own_v), load.copy(tokens, tok_v), load.copy(summary, sum_v),
        load.copy(cot, cot_v),
    ]
    met()
    link = Sender(send_sems, recv_sems)

    def halo():
        rows = []
        for j in (0, 2, 1):
            up = link.send(near.at[2, j], beside.at[0, j], row_peer(at, 1))
            down = link.send(near.at[0, j], beside.at[1, j], row_peer(at, -1))
            rows.append((j, up, down))
        yield
        mid_ready.wait()
        for j, up, down in rows[:2]:
            up.wait_recv()
            down.wait_recv()
            row_sum[j // 2] = added(mid.at[j], beside.at[0, j], beside.at[1, j]).astype(BF16)
        there = {"tx_0": lax.rem(z + (3 + 2 * x_hi), 4)}
        far = link.send(row_sum.at[x_hi], z_slot, there)
        yield
        far.wait_recv()
        message[...] = added(row_sum.at[1 - x_hi], z_slot).astype(BF16)
        last = send_across(link, at, message, x_relay, (x_slot, x_slot))
        next(last)
        yield
        next(last)
        _, up, down = rows[2]
        up.wait_recv()
        down.wait_recv()
        for copy in rest_ready:
            copy.wait()
        own_v[...] += added(beside.at[0, 1], beside.at[1, 1])
        yield
        for _ in last:
            pass
        hidden_grad = own_v[...] + x_slot[...].astype(F32)
        scale = row_scale(tok_v[...])
        back = norm_back(tok_v[...], scale, gain[...].reshape(1, -1), hidden_grad)
        grad_tokens[...] = (cot_v[...].astype(F32) + back).astype(BF16)

    def summaries():
        yield from scatter_ring(
            link, 2, at, s_piece, s_loc, s_ready, s_relay, s_direct, s_one
        )
        block = summary.shape[0]
        yield from scatter_direct(
            link, 0, at,
            lambda d: s_one.at[lax.rem(d, 2), :, pl.ds((d // 2) * block, block)],
            s_slots_x, s_two,
        )
        yield from scatter_direct(link, 1, at, lambda d: s_two.at[d], s_slots_y, s_sum)
        scale = row_scale(sum_v[...])
        back = norm_back(sum_v[...], scale, gain[...].reshape(1, -1), s_sum[...])
        grad_summary[...] = back.astype(BF16)

    def weights(p, q):
        a, b, c = p, (p + 1) % 3, (p + 2) % 3
        first = p * part
        yield from scatter_ring(
            link, a, at, w_piece(p, q), w_loc.at[p, q], w_ready[p, q],
            w_relay.at[p, q], w_direct.at[p, q], w_one.at[p, q],
        )
        yield from scatter_direct(
            link, b, at,
            lambda d: w_one.at[p, q, d // 2, pl.ds(lax.rem(d, 2) * size[1], size[1])],
            w_slots_two.at[p, q], w_two.at[p, q],
        )
        base = first + at[a] * size[0]
        inner = base + at[b] * size[1]
        yield from scatter_direct(
            link, c, at,
            lambda d: w_two.at[p, q, pl.ds(pl.multiple_of(d * size[2], PACK), size[2])],
            w_slots_three.at[p, q],
            w_three.at[p, q],
        )
        mine = rows_of(w_out, inner + at[c] * size[2], size[2], q)
        copies = [link.send(w_three.at[p, q], mine, peer(c, at, k)) for k in (1, 3, 2)]
        kept = load.copy(w_three.at[p, q], mine)
        yield
        kept.wait()
        for copy in copies:
            copy.wait_recv()
        yield from gather_direct(
            link, b, at, lambda d: rows_of(w_out, base + d * size[1], size[1], q)
        )
        yield from gather_ring(
            link, a, at,
            lambda d: rows_of(w_out, first + d * size[0], size[0], q),
            lambda d, h: rows_of(
                w_out, first + d * size[0] + h * (size[0] // 2), size[0] // 2, q
            ),
        )

    def gains():
        gain_ready.wait()
        for k in range(3):
            yield from scatter_direct(
                link, k, at, lambda d, k=k: gain_sum.at[k], gain_slots.at[k], gain_sum.at[k + 1]
            )
        total = jnp.sum(gain_sum[3], axis=0, keepdims=True)
        grad_gain[...] = total / gain[...].reshape(1, -1)

    first_half = [weights(p, 0) for p in range(3)]
    second_half = [weights(p, 1) for p in range(3)]
    take_turns(
        [*first_half, *second_half, later(2, halo()), later(2, summaries()), later(3, gains())]
    )
    link.drain()


def exchange(
    near_grad, own_grad, sum_grad, w_part, gain_part, tokens, summary, norm_gain, cot
):
    rows, width = own_grad.shape
    block = summary.shape[0]
    vm = pl.BlockSpec(memory_space=pltpu.VMEM)
    far = pl.BlockSpec(memory_space=pltpu.HBM)
    total = w_part.shape[1]
    part = total // 3
    wide = width // 2
    sends = 6 + 5 + 6 + 3 + 3 + 6 * (6 + 3 + 3 + 3 + 3 + 4) + 9
    loads = 24 + 4 + 2 + 4 + 6
    sums = sum_grad.reshape(8, 4, 2 * block, width)
    grad_tokens, grad_summary, gain, w_all = pl.pallas_call(
        exchange_kernel,
        out_shape=(
            jax.ShapeDtypeStruct((rows, width), BF16),
            jax.ShapeDtypeStruct((block, width), BF16),
            jax.ShapeDtypeStruct((1, width), F32),
            jax.ShapeDtypeStruct((2, total, wide), BF16),
        ),
        in_specs=[far] * 7 + [vm, far],
        out_specs=(vm, vm, vm, far),
        scratch_shapes=[
            pltpu.VMEM((rows, width), F32),
            pltpu.VMEM((3, rows, width), BF16),
            pltpu.VMEM((rows, width), BF16),
            pltpu.VMEM((block, width), BF16),
            pltpu.VMEM((rows, width), BF16),
            pltpu.VMEM((4, 4, 2 * block, width), BF16),
            pltpu.VMEM((3, 2, 4, part // 8, wide), BF16),
            pltpu.VMEM((2, 3, rows, width), BF16),
            pltpu.VMEM((2, rows, width), BF16),
            pltpu.VMEM((rows, width), BF16),
            pltpu.VMEM((rows, width), BF16),
            pltpu.VMEM((2, rows, wide), BF16),
            pltpu.VMEM((rows, width), BF16),
            pltpu.VMEM((2, 2, 4, 2 * block, width), BF16),
            pltpu.VMEM((2, 2, 4, 2 * block, width), BF16),
            pltpu.VMEM((2, 4, 2 * block, width), BF16),
            pltpu.VMEM((3, 4, block, width), BF16),
            pltpu.VMEM((4, block, width), BF16),
            pltpu.VMEM((3, block, width), BF16),
            pltpu.VMEM((block, width), F32),
            pltpu.VMEM((3, 2, 2, 2, part // 8, wide), BF16),
            pltpu.VMEM((3, 2, 2, 2, part // 8, wide), BF16),
            pltpu.VMEM((3, 2, 2, part // 8, wide), BF16),
            pltpu.VMEM((3, 2, 3, part // 16, wide), BF16),
            pltpu.VMEM((3, 2, part // 16, wide), BF16),
            pltpu.VMEM((3, 2, 3, part // 64, wide), BF16),
            pltpu.VMEM((3, 2, part // 64, wide), BF16),
            pltpu.VMEM((4, 8, width), F32),
            pltpu.VMEM((3, 3, 8, width), F32),
            pltpu.SemaphoreType.DMA((loads,)),
            pltpu.SemaphoreType.DMA((sends,)),
            pltpu.SemaphoreType.DMA((sends,)),
        ],
        compiler_params=pltpu.CompilerParams(
            collective_id=1, has_side_effects=True, vmem_limit_bytes=60 * 1024 * 1024
        ),
        name="exchange",
    )(
        near_grad.reshape(3, 3, rows, width), own_grad, sums, w_part,
        gain_part, tokens, summary, norm_gain, cot,
    )
    return widen(w_all, grad_tokens, grad_summary, gain)


def widen_kernel(
    narrow, tok_in, sum_in, gain_in, wide, tok_out, sum_out, gain_out,
    held, stage, in_sems, out_sems, pass_sems,
):
    passed = [
        pltpu.make_async_copy(tok_in, tok_out, pass_sems.at[0]),
        pltpu.make_async_copy(sum_in, sum_out, pass_sems.at[1]),
    ]
    rows = stage.shape[1]
    count = narrow.shape[1] // rows
    reads, writes = [], []
    for k in range(count):
        here = pl.ds(k * rows, rows)
        reads.append(pltpu.make_async_copy(narrow.at[:, here], held.at[k], in_sems.at[k]))
        reads[k].start()
    for copy in passed:
        copy.start()
    gain_out[...] = gain_in[...].reshape(gain_out.shape)
    for k in range(count):
        if k >= 3:
            writes[k - 3].wait()
        reads[k].wait()
        stage[k % 3] = jnp.concatenate([held[k, 0], held[k, 1]], axis=1).astype(F32)
        here = pl.ds(k * rows, rows)
        writes.append(pltpu.make_async_copy(stage.at[k % 3], wide.at[here], out_sems.at[k % 3]))
        writes[k].start()
    for copy in writes[-3:] + passed:
        copy.wait()


def widen(narrow, grad_tokens, grad_summary, gain):
    total, width = narrow.shape[1], 2 * narrow.shape[2]
    count = 12
    vm = pl.BlockSpec(memory_space=pltpu.VMEM)
    far = pl.BlockSpec(memory_space=pltpu.HBM)
    return pl.pallas_call(
        widen_kernel,
        out_shape=(
            jax.ShapeDtypeStruct((total, width), F32),
            jax.ShapeDtypeStruct(grad_tokens.shape, BF16),
            jax.ShapeDtypeStruct(grad_summary.shape, BF16),
            jax.ShapeDtypeStruct((width,), F32),
        ),
        in_specs=[far, far, far, vm],
        out_specs=(far, far, far, vm),
        scratch_shapes=[
            pltpu.VMEM((count, 2, total // count, width // 2), BF16),
            pltpu.VMEM((3, total // count, width), F32),
            pltpu.SemaphoreType.DMA((count,)),
            pltpu.SemaphoreType.DMA((3,)),
            pltpu.SemaphoreType.DMA((2,)),
        ],
        compiler_params=pltpu.CompilerParams(vmem_limit_bytes=60 * 1024 * 1024),
        name="widen",
    )(narrow, grad_tokens, grad_summary, gain)


def row_scale(rows):
    values = rows.astype(F32)
    return lax.rsqrt(jnp.mean(values * values, axis=-1, keepdims=True) + epsilon)


def normalize(rows, gain):
    scale = row_scale(rows)
    return ((rows.astype(F32) * scale * gain).astype(BF16), scale)


def norm_back(rows, scale, gain, grad_norm):
    values = rows.astype(F32)
    scaled = gain * grad_norm
    return scale * scaled - values * scale**3 * jnp.mean(values * scaled, axis=-1, keepdims=True)


def dot(a, b, ca, cb):
    return lax.dot_general(a, b, (((ca,), (cb,)), ((), ())), preferred_element_type=F32)


def layer_kernel(
    counts, pattern, blocks, near, summ, w_in, tok, cot,
    updated, near_out, own_out, sum_out, w_out, gain_part,
    w, own_v, near_grad, own_grad, sum_grad, w_part, pack_sems, local_sems,
    xp, kp, vp, dkt, dvt, scores, probs, bias, qs, gs, qst, gst, acc, m_ref, l_ref, d_ref,
    q_all, g_all, o_all, dq_all,
):
    rows = tok.shape[0]
    width = tok.shape[1]
    quads = width // CHUNK
    head_size = width // HEADS
    stack = QUAD * rows
    factor = 1.0 / math.sqrt(head_size)
    n_blocks = summ.shape[0] // SBLK
    yp = kp
    zk = scores.at[:, 0:width]
    zv = scores.at[:, width : 2 * width]

    load = Loader(local_sems)
    own_ready = load.copy(near.at[NEAR // 2], own_v)
    w_ready = [load.copy(w_in.at[k], w.at[k]) for k in (0, 3, 1, 2)]

    grid_row = 4 * lax.axis_index("ty_0") + lax.axis_index("ty_1")
    grid_col = 2 * lax.axis_index("tx_0") + lax.axis_index("tx_1")
    meta = []
    for t in range(NEAR):
        r, c = grid_row + (t // 3 - 1), grid_col + (t % 3 - 1)
        inside = (r >= 0) & (r < 8) & (c >= 0) & (c < 8)
        n = counts[jnp.clip(r, 0, 7), jnp.clip(c, 0, 7)]
        meta.append(jnp.where(inside & (pattern[grid_row, grid_col, t] == 1), n, 0))
    for b in range(n_blocks):
        meta.append(jnp.where(blocks[0, 0, b] == 1, 1, 0))
    meta.append(counts[grid_row, grid_col])

    def packed(k, src, at, size):
        return pltpu.make_async_copy(
            src.at[pl.ds(0, size)], xp.at[pl.ds(pl.multiple_of(at, PACK), size)], pack_sems.at[k]
        )

    packs = []
    block_at = []
    total = jnp.int32(0)
    for b in range(n_blocks):
        block_at.append(total)
        flag = meta[NEAR + b]

        src = summ.at[pl.ds(b * SBLK, SBLK)]
        packs.append((flag == 1, packed(NEAR + b, src, total, SBLK)))
        total = total + SBLK * flag
    summ_end = total
    tile_at = []
    for t in range(NEAR):
        tile_at.append(total)
        n = meta[t]

        size = pl.multiple_of(((n + (PACK - 1)) // PACK) * PACK, PACK)
        packs.append((n > 0, packed(t, near.at[t], total, size)))
        total = total + size
    for live, copy in packs:
        pl.when(live)(copy.start)
    xp[pl.ds(pl.multiple_of(total, PACK), CHUNK), :] = jnp.zeros((CHUNK, width), BF16)
    chunks = (total + (CHUNK - 1)) // CHUNK

    place = lax.broadcasted_iota(jnp.int32, bias.shape, 1)
    live = place < summ_end
    for t in range(NEAR):
        live = live | ((place >= tile_at[t]) & (place < tile_at[t] + meta[t]))
    bias[...] = jnp.where(live, 0.0, -1e30)

    own_ready.wait()
    for copy in w_ready[:2]:
        copy.wait()
    own = own_v[...]
    valid = lax.broadcasted_iota(jnp.int32, (rows, width), 0) < meta[NEAR + n_blocks]
    masked = jnp.where(valid, cot[...].astype(F32), 0.0).astype(BF16)
    q_all[...] = (dot(own, w[0], 1, 0).astype(BF16).astype(F32) * factor).astype(BF16)
    g_all[...] = dot(masked, w[3], 1, 1).astype(BF16)

    for copy in w_ready[2:]:
        copy.wait()
    for live, copy in packs:
        pl.when(live)(copy.wait)

    def sweep(body):
        def pair(c, carry):
            body(pl.multiple_of(c * (2 * CHUNK), 2 * CHUNK), 2 * CHUNK)
            return carry

        def four(c, carry):
            body(pl.multiple_of(c * (4 * CHUNK), 4 * CHUNK), 4 * CHUNK)
            return carry

        lax.fori_loop(0, chunks // 4, four, 0)
        lax.fori_loop(chunks // 4 * 2, chunks // 2, pair, 0)

        @pl.when(lax.rem(chunks, 2) == 1)
        def _():
            body(pl.multiple_of((chunks - 1) * CHUNK, CHUNK), CHUNK)

    def project(start, size):
        at = pl.ds(start, size)
        x = xp[at, :]
        kp[at, :] = dot(x, w[1], 1, 0).astype(BF16)
        vp[at, :] = dot(x, w[2], 1, 0).astype(BF16)

    sweep(project)

    lane_head = lax.broadcasted_iota(jnp.int32, (rows, CHUNK), 1) // head_size

    def lanes(values):
        return [values[:, k : k + 128] for k in range(0, values.shape[1], 128)]


    def stack_up(j):
        q_part = q_all[:, j * CHUNK : (j + 1) * CHUNK].astype(F32)
        g_part = g_all[:, j * CHUNK : (j + 1) * CHUNK].astype(F32)
        for i in range(QUAD):
            here = slice(i * rows, (i + 1) * rows)
            qs[j % 2, here, :] = jnp.where(lane_head == i, q_part, 0.0).astype(BF16)
            gs[j % 2, here, :] = jnp.where(lane_head == i, g_part, 0.0).astype(BF16)
        m_ref[...] = jnp.full(m_ref.shape, -3e38, F32)

    def score(j, start, size):
        at = pl.ds(start, size)
        s = dot(qs[j % 2], kp[at, j * CHUNK : (j + 1) * CHUNK], 1, 1) + bias[0:1, at]
        scores[:, at] = s
        most = m_ref[...]
        for part in lanes(s):
            most = jnp.maximum(most, part)
        m_ref[...] = most

    stack_up(0)
    sweep(functools.partial(score, 0))
    for j in range(quads):
        cols = slice(j * CHUNK, (j + 1) * CHUNK)
        q_now, g_now = qs.at[j % 2], gs.at[j % 2]
        m_ref[...] = jnp.broadcast_to(jnp.max(m_ref[...], axis=1, keepdims=True), m_ref.shape)
        l_ref[...] = jnp.zeros(l_ref.shape, F32)
        acc[...] = jnp.zeros(acc.shape, F32)

        def mix(start, size):
            at = pl.ds(start, size)
            m = m_ref[...]
            e = [jnp.exp(part - m) for part in lanes(scores[:, at])]
            total = l_ref[...]
            for part in e:
                total = total + part
            l_ref[...] = total
            e = jnp.concatenate(e, axis=1).astype(BF16)
            probs[:, at] = e
            acc[...] += dot(e, vp[at, cols], 1, 0)

        sweep(mix)
        inv = 1.0 / jnp.sum(l_ref[...], axis=1, keepdims=True)
        out = acc[...] * inv
        d_ref[...] = jnp.broadcast_to(
            jnp.sum(out * g_now[...].astype(F32), axis=1, keepdims=True), d_ref.shape
        )
        picked = jnp.zeros((rows, CHUNK), F32)
        for i in range(QUAD):
            here = slice(i * rows, (i + 1) * rows)
            picked = jnp.where(lane_head == i, out[here], picked)
        o_all[:, cols] = picked.astype(BF16)
        qst[...] = (q_now[...].astype(F32) * inv).astype(BF16).T
        gst[...] = (g_now[...].astype(F32) * inv).astype(BF16).T
        l_ref[...] = jnp.broadcast_to(inv, l_ref.shape)
        acc[...] = jnp.zeros(acc.shape, F32)
        if j + 1 < quads:
            stack_up(j + 1)

        def back(start, size):
            at = pl.ds(start, size)
            e = probs[:, at]
            d = d_ref[...]
            dp = dot(g_now[...], vp[at, cols], 1, 1)
            delta = jnp.concatenate([part - d for part in lanes(dp)], axis=1)
            ds = (e.astype(F32) * delta).astype(BF16)
            acc[...] += dot(ds, kp[at, cols], 1, 0)
            dkt[cols, at] = dot(qst[...], ds, 1, 0).astype(BF16)
            dvt[cols, at] = dot(gst[...], e, 1, 0).astype(BF16)
            if j + 1 < quads:
                score(j + 1, start, size)

        sweep(back)
        inv2 = l_ref[...] * factor
        dq = acc[...] * jnp.concatenate([inv2, inv2], axis=1)
        picked = jnp.zeros((rows, CHUNK), F32)
        for i in range(QUAD):
            here = slice(i * rows, (i + 1) * rows)
            picked = jnp.where(lane_head == i, dq[here], picked)
        dq_all[:, cols] = picked.astype(BF16)

    w_part[0] = dot(own, dq_all[...], 0, 0).astype(BF16)
    w_part[3] = dot(o_all[...], masked, 0, 0).astype(BF16)

    def send_part(k):
        half = width // 2
        for q in range(2):
            src = w_part.at[k, :, q * half : (q + 1) * half]
            sent.append(load.copy(src, w_out.at[q, pl.ds(k * width, width)]))

    sent = []
    send_part(0)
    send_part(3)
    mixed = dot(o_all[...], w[3], 1, 0)
    updated[...] = (tok[...].astype(F32) + jnp.where(valid, mixed, 0.0)).astype(BF16)

    zk[...] = jnp.zeros(zk.shape, F32)
    zv[...] = jnp.zeros(zv.shape, F32)
    own_part = dot(dq_all[...], w[0], 1, 1)
    gain_part[...] = jnp.sum(
        (own_part * own.astype(F32)).reshape(rows // 8, 8, width), axis=0
    )

    def finish(start, size):
        at = pl.ds(start, size)
        x = xp[at, :]
        dk = dkt[:, at]
        dv = dvt[:, at]
        zk[...] += dot(dk, x, 1, 0)
        zv[...] += dot(dv, x, 1, 0)
        yt = dot(w[1], dk, 1, 0) + dot(w[2], dv, 1, 0)
        y = yt.astype(BF16).T
        yp[at, :] = y
        gain_part[...] += jnp.sum(
            (y.astype(F32) * x.astype(F32)).reshape(size // 8, 8, width), axis=0
        )

    sweep(finish)

    w_part[1] = zk[...].astype(BF16).T
    send_part(1)
    w_part[2] = zv[...].astype(BF16).T
    send_part(2)

    row_at = lax.broadcasted_iota(jnp.int32, (rows, width), 0)
    for t in range(NEAR):
        y = yp[pl.ds(pl.multiple_of(tile_at[t], PACK), rows), :].astype(F32)
        y = jnp.where(row_at < meta[t], y, 0.0)
        if t == NEAR // 2:
            own_grad[...] = y + own_part
            sent.append(load.copy(own_grad, own_out))
        else:
            near_grad[t] = y.astype(BF16)
            sent.append(load.copy(near_grad.at[t], near_out.at[t]))
    for b in range(n_blocks):
        y = yp[pl.ds(pl.multiple_of(block_at[b], SBLK), SBLK), :].astype(F32)
        keep = jnp.zeros((SBLK, width), jnp.int32) + meta[NEAR + b]
        sum_grad[b * SBLK : (b + 1) * SBLK, :] = jnp.where(keep == 1, y, 0.0).astype(BF16)
    sent.append(load.copy(sum_grad, sum_out))
    for copy in sent:
        copy.wait()


def layer(counts, pattern, blocks, near, summ, w, tok, cot):
    rows, width = tok.shape
    most = (NEAR * rows + summ.shape[0] + CHUNK - 1) // CHUNK * CHUNK
    stack = QUAD * rows
    vm = pl.BlockSpec(memory_space=pltpu.VMEM)
    sm = pl.BlockSpec(memory_space=pltpu.SMEM)
    far = pl.BlockSpec(memory_space=pl.ANY)
    n_blocks = summ.shape[0] // SBLK
    return pl.pallas_call(
        layer_kernel,
        out_shape=(
            jax.ShapeDtypeStruct((rows, width), BF16),
            jax.ShapeDtypeStruct((NEAR, rows, width), BF16),
            jax.ShapeDtypeStruct((rows, width), F32),
            jax.ShapeDtypeStruct(summ.shape, BF16),
            jax.ShapeDtypeStruct((2, 4 * width, width // 2), BF16),
            jax.ShapeDtypeStruct((8, width), F32),
        ),
        in_specs=[sm] * 3 + [far] * 3 + [vm] * 2,
        out_specs=(vm, far, far, far, far, vm),
        scratch_shapes=[
            pltpu.VMEM((4, width, width), BF16),
            pltpu.VMEM((rows, width), BF16),
            pltpu.VMEM((NEAR, rows, width), BF16),
            pltpu.VMEM((rows, width), F32),
            pltpu.VMEM(summ.shape, BF16),
            pltpu.VMEM((4, width, width), BF16),
            pltpu.SemaphoreType.DMA((NEAR + n_blocks,)),
            pltpu.SemaphoreType.DMA((5 + 8 + NEAR + 2,)),
            pltpu.VMEM((most + CHUNK, width), BF16),
            pltpu.VMEM((most + CHUNK, width), BF16),
            pltpu.VMEM((most, width), BF16),
            pltpu.VMEM((width, most), BF16),
            pltpu.VMEM((width, most), BF16),
            pltpu.VMEM((stack, most), F32),
            pltpu.VMEM((stack, most), BF16),
            pltpu.VMEM((8, most), F32),
            pltpu.VMEM((2, stack, CHUNK), BF16),
            pltpu.VMEM((2, stack, CHUNK), BF16),
            pltpu.VMEM((CHUNK, stack), BF16),
            pltpu.VMEM((CHUNK, stack), BF16),
            pltpu.VMEM((stack, CHUNK), F32),
            pltpu.VMEM((stack, 128), F32),
            pltpu.VMEM((stack, 128), F32),
            pltpu.VMEM((stack, 128), F32),
            pltpu.VMEM((rows, width), BF16),
            pltpu.VMEM((rows, width), BF16),
            pltpu.VMEM((rows, width), BF16),
            pltpu.VMEM((rows, width), BF16),
        ],
        compiler_params=pltpu.CompilerParams(vmem_limit_bytes=63 * 1024 * 1024),
        name="layer",
    )(counts, pattern, blocks, near, summ, w, tok, cot)


def local(
    tokens, summary, counts, tile_pattern, summary_pattern, norm_gain, projections, cotangent
):
    rows, width = tokens.shape[2:]
    token_rows = tokens[0, 0]
    grads_in = cotangent[0, 0]
    near, every = gather(token_rows, summary, norm_gain)
    updated, near_grad, own_grad, sum_grad, w_part, gain_part = layer(
        counts, tile_pattern, summary_pattern, near, every, projections, token_rows, grads_in
    )
    grad_proj, grad_tokens, grad_summary, grad_gain = exchange(
        near_grad, own_grad, sum_grad, w_part, gain_part, token_rows, summary, norm_gain, grads_in
    )
    return (
        updated.reshape(tokens.shape),
        grad_tokens.reshape(tokens.shape),
        grad_summary,
        grad_proj.reshape(projections.shape),
        grad_gain,
    )


def solution(mesh):
    finer = Mesh(
        mesh.devices.reshape(2, 4, 4, 2, mesh.shape["slide"]),
        ("ty_0", "ty_1", "tx_0", "tx_1", "slide"),
    )
    return jax.shard_map(
        local,
        mesh=finer,
        in_specs=(
            P(SLIDE_TY, TX, None, None),
            P(SLIDE_TY_TX, None),
            P("slide", None),
            P("slide", None, None),
            P(SLIDE_TY, TX, None),
            P(),
            P(),
            P(SLIDE_TY, TX, None, None),
        ),
        out_specs=(
            P(SLIDE_TY, TX, None, None),
            P(SLIDE_TY, TX, None, None),
            P(SLIDE_TY_TX, None),
            P("slide", None, None),
            P("slide"),
        ),
        check_vma=False,
    )
```

```python
import functools
import math

import jax
import jax.numpy as jnp
from jax import lax
from jax.experimental import pallas as pl
from jax.experimental.pallas import tpu as pltpu
from jax.sharding import Mesh
from jax.sharding import PartitionSpec as P

HEADS = 12
SBLK = 128
QUAD = 4
CHUNK = 256
PACK = 16
NEAR = 9
TX = ("tx_0", "tx_1")
SLIDE_TY = ("slide", "ty_0", "ty_1")
SLIDE_TY_TX = ("slide", "ty_0", "ty_1", "tx_0", "tx_1")
F32 = jnp.float32
BF16 = jnp.bfloat16
MESH = pl.DeviceIdType.MESH

epsilon = 1e-05


def places():
    return (
        2 * lax.axis_index("tx_1") + lax.axis_index("ty_0"),
        lax.axis_index("ty_1"),
        lax.axis_index("tx_0"),
    )


def peer(axis, at, by):
    there = lax.rem(at[axis] + (by + 4), 4)
    if axis == 0:
        return {"tx_1": there // 2, "ty_0": lax.rem(there, 2)}
    return {"ty_1": there} if axis == 1 else {"tx_0": there}


def row_peer(at, by):
    there = lax.rem(lax.axis_index("ty_0") * 4 + at[1] + (by + 8), 8)
    return {"ty_0": there // 4, "ty_1": lax.rem(there, 4)}


def greet(at):
    barrier = pltpu.get_barrier_semaphore()
    others = [peer(axis, at, by) for axis in range(3) for by in (1, 2, 3)]
    others += [row_peer(at, 1), row_peer(at, -1)]
    for other in others:
        pl.semaphore_signal(barrier, inc=1, device_id=other, device_id_type=MESH)
    return lambda: pl.semaphore_wait(barrier, len(others))


class Loader:
    def __init__(self, sems):
        self.sems, self.count = sems, 0

    def copy(self, src, dst):
        copy = pltpu.make_async_copy(src, dst, self.sems.at[self.count])
        self.count += 1
        copy.start()
        return copy


class Sender:
    def __init__(self, send_sems, recv_sems):
        self.send_sems, self.recv_sems = send_sems, recv_sems
        self.copies = []

    def send(self, src, dst, device):
        k = len(self.copies)
        copy = pltpu.make_async_remote_copy(
            src_ref=src,
            dst_ref=dst,
            send_sem=self.send_sems.at[k],
            recv_sem=self.recv_sems.at[k],
            device_id=device,
            device_id_type=MESH,
        )
        copy.start()
        self.copies.append(copy)
        return copy

    def drain(self):
        for copy in self.copies:
            copy.wait_send()


def take_turns(tasks):
    tasks = list(tasks)
    while tasks:
        tasks = [task for task in tasks if next(task, "end") != "end"]


def send_across(link, at, src, relay, slots):
    wide = src.shape[1] // 2
    halves = [slice(0, wide), slice(wide, 2 * wide)]
    ways = [peer(0, at, 1), peer(0, at, -1)]
    first = [link.send(src.at[:, halves[k]], relay.at[k], ways[k]) for k in range(2)]
    yield
    second = []
    for k in range(2):
        first[k].wait_recv()
        second.append(link.send(relay.at[k], slots[k].at[:, halves[k]], ways[k]))
    yield
    for copy in second:
        copy.wait_recv()


def added(*refs):
    total = refs[0][...].astype(F32)
    for ref in refs[1:]:
        total = total + ref[...].astype(F32)
    return total


def scatter_ring(link, axis, at, piece, held, ready, relay, direct, out):
    c = at[axis]
    right, left, across = [lax.rem(c + k, 4) for k in (1, 3, 2)]
    to_right, to_left = peer(axis, at, 1), peer(axis, at, -1)
    far_a = link.send(piece(across, 0), relay.at[0, 0], to_right)
    far_b = link.send(piece(across, 1), relay.at[0, 1], to_left)
    near_b = link.send(piece(right, 1), direct.at[0, 1], to_right)
    near_a = link.send(piece(left, 0), direct.at[1, 0], to_left)
    yield
    for copy in ready:
        copy.wait()
    far_a.wait_recv()
    relay[1, 0] = added(relay.at[0, 0], held.at[0]).astype(BF16)
    sum_a = link.send(relay.at[1, 0], direct.at[0, 0], to_right)
    far_b.wait_recv()
    relay[1, 1] = added(relay.at[0, 1], held.at[1]).astype(BF16)
    sum_b = link.send(relay.at[1, 1], direct.at[1, 1], to_left)
    yield
    for copy in (near_b, near_a, sum_a, sum_b):
        copy.wait_recv()
    for half in range(2):
        out[half] = added(held.at[2 + half], direct.at[0, half], direct.at[1, half]).astype(BF16)


def scatter_direct(link, axis, at, piece, slots, out):
    copies = [
        link.send(piece(lax.rem(at[axis] + k, 4)), slots.at[k - 1], peer(axis, at, k))
        for k in (1, 3, 2)
    ]
    yield
    for copy in copies:
        copy.wait_recv()
    total = added(piece(at[axis]), slots.at[0], slots.at[1], slots.at[2])
    out[...] = total.astype(out.dtype)


def gather_direct(link, axis, at, place):
    mine = place(at[axis])
    copies = [link.send(mine, mine, peer(axis, at, k)) for k in (1, 3, 2)]
    yield
    for copy in copies:
        copy.wait_recv()


def gather_ring(link, axis, at, place, half_place):
    c = at[axis]
    right, left = lax.rem(c + 1, 4), lax.rem(c + 3, 4)
    to_right, to_left = peer(axis, at, 1), peer(axis, at, -1)
    mine = place(c)
    one = link.send(mine, mine, to_right)
    two = link.send(mine, mine, to_left)
    yield
    one.wait_recv()
    half = half_place(left, 0)
    three = link.send(half, half, to_right)
    two.wait_recv()
    half = half_place(right, 1)
    four = link.send(half, half, to_left)
    yield
    three.wait_recv()
    four.wait_recv()


def gather_kernel(
    tokens, summary, gain, near, every, hidden, summ, relay, local_sems, send_sems, recv_sems
):
    at = places()
    x, y, z = at
    x_hi, x_lo = lax.axis_index("tx_1"), lax.axis_index("ty_0")
    met = greet(at)
    summ[...] = normalize(summary[...], gain[...].reshape(1, -1))[0]
    hidden[...] = normalize(tokens[...], gain[...].reshape(1, -1))[0]
    load = Loader(local_sems)
    own = every.at[x_lo, y, z, x_hi]
    kept = [load.copy(summ, own), load.copy(hidden, near.at[1, 1])]
    met()
    link = Sender(send_sems, recv_sems)
    from_x, from_z = 2 - 2 * x_hi, 2 * x_hi

    def halo():
        slots = [near.at[1, 2 - 2 * (lax.rem(x + by, 4) // 2)] for by in (1, 3)]
        beside = send_across(link, at, hidden, relay, slots)
        next(beside)
        rows = [
            link.send(hidden, near.at[0, 1], row_peer(at, 1)),
            link.send(hidden, near.at[2, 1], row_peer(at, -1)),
        ]
        yield
        next(beside)
        yield
        for _ in beside:
            pass
        there = {"tx_0": lax.rem(z + (5 - 2 * x_hi), 4)}
        beyond = link.send(near.at[1, from_x], near.at[1, from_z], there)
        rows.append(link.send(near.at[1, from_x], near.at[0, from_x], row_peer(at, 1)))
        rows.append(link.send(near.at[1, from_x], near.at[2, from_x], row_peer(at, -1)))
        yield
        beyond.wait_recv()
        rows.append(link.send(near.at[1, from_z], near.at[0, from_z], row_peer(at, 1)))
        rows.append(link.send(near.at[1, from_z], near.at[2, from_z], row_peer(at, -1)))
        yield
        yield
        yield
        for copy in rows:
            copy.wait_recv()

    def summaries():
        copies = [link.send(summ, own, peer(1, at, k)) for k in (1, 3, 2)]
        yield
        kept[0].wait()
        for copy in copies:
            copy.wait_recv()
        yield from gather_direct(
            link, 0, at, lambda d: every.at[lax.rem(d, 2), :, z, d // 2]
        )
        yield from gather_ring(
            link, 2, at, lambda d: every.at[:, :, d], lambda d, half: every.at[half, :, d]
        )

    take_turns([halo(), summaries()])
    kept[1].wait()
    link.drain()


def gather(tokens, summary, gain):
    rows, width = tokens.shape
    block = summary.shape[0]
    vm = pl.BlockSpec(memory_space=pltpu.VMEM)
    sends = 4 + 6 + 1 + 3 + 3 + 4
    near, every = pl.pallas_call(
        gather_kernel,
        out_shape=(
            jax.ShapeDtypeStruct((3, 3, rows, width), BF16),
            jax.ShapeDtypeStruct((2, 4, 4, 2, block, width), BF16),
        ),
        in_specs=[vm] * 3,
        out_specs=(pl.BlockSpec(memory_space=pltpu.HBM),) * 2,
        scratch_shapes=[
            pltpu.VMEM((rows, width), BF16),
            pltpu.VMEM((block, width), BF16),
            pltpu.VMEM((2, rows, width // 2), BF16),
            pltpu.SemaphoreType.DMA((2,)),
            pltpu.SemaphoreType.DMA((sends,)),
            pltpu.SemaphoreType.DMA((sends,)),
        ],
        compiler_params=pltpu.CompilerParams(
            collective_id=0, has_side_effects=True, vmem_limit_bytes=60 * 1024 * 1024
        ),
        name="gather",
    )(tokens, summary, gain)
    return near.reshape(NEAR, rows, width), every.reshape(-1, width)


def exchange_kernel(
    near, own, sums, w_in, gain_in, tokens, summary, gain, cot,
    grad_tokens, grad_summary, grad_gain, w_out,
    own_v, mid, tok_v, sum_v, cot_v, s_loc, w_loc,
    beside, row_sum, z_slot, x_slot, x_relay, message,
    s_relay, s_direct, s_one, s_slots_x, s_two, s_slots_y, s_sum,
    w_relay, w_direct, w_one, w_slots_two, w_two, w_slots_three, w_three,
    gain_sum, gain_slots, local_sems, send_sems, recv_sems,
):
    at = places()
    x, y, z = at
    x_hi = lax.axis_index("tx_1")
    met = greet(at)
    load = Loader(local_sems)
    part = w_in.shape[1] // 3
    size = [part // 4, part // 16, part // 64]
    s_half = sums.shape[0] // 2

    def rows_of(ref, start, count, q):
        return ref.at[q, pl.ds(pl.multiple_of(start, PACK), count)]

    def s_piece(d, h):
        return sums.at[pl.ds(h * s_half, s_half), d]

    def w_piece(p, q):
        half = size[0] // 2
        return lambda d, h: rows_of(w_in, p * part + d * size[0] + h * half, half, q)

    def own_pieces(piece, axis, slots):
        c = at[axis]
        right, left = lax.rem(c + 1, 4), lax.rem(c + 3, 4)
        wanted = ((right, 0), (left, 1), (c, 0), (c, 1))
        return [load.copy(piece(*wanted[k]), slots.at[k]) for k in range(4)]

    w_ready = {
        (p, q): own_pieces(w_piece(p, q), p, w_loc.at[p, q]) for q in range(2) for p in range(3)
    }
    s_ready = own_pieces(s_piece, 2, s_loc)
    mid_ready = load.copy(near.at[1], mid)
    gain_ready = load.copy(gain_in, gain_sum.at[0])
    rest_ready = [
        load.copy(own, own_v), load.copy(tokens, tok_v), load.copy(summary, sum_v),
        load.copy(cot, cot_v),
    ]
    met()
    link = Sender(send_sems, recv_sems)

    def halo():
        rows = []
        for j in (0, 2, 1):
            up = link.send(near.at[2, j], beside.at[0, j], row_peer(at, 1))
            down = link.send(near.at[0, j], beside.at[1, j], row_peer(at, -1))
            rows.append((j, up, down))
        yield
        mid_ready.wait()
        for j, up, down in rows[:2]:
            up.wait_recv()
            down.wait_recv()
            row_sum[j // 2] = added(mid.at[j], beside.at[0, j], beside.at[1, j]).astype(BF16)
        there = {"tx_0": lax.rem(z + (3 + 2 * x_hi), 4)}
        far = link.send(row_sum.at[x_hi], z_slot, there)
        yield
        far.wait_recv()
        message[...] = added(row_sum.at[1 - x_hi], z_slot).astype(BF16)
        last = send_across(link, at, message, x_relay, (x_slot, x_slot))
        next(last)
        yield
        next(last)
        _, up, down = rows[2]
        up.wait_recv()
        down.wait_recv()
        for copy in rest_ready:
            copy.wait()
        own_v[...] += added(beside.at[0, 1], beside.at[1, 1])
        yield
        for _ in last:
            pass
        hidden_grad = own_v[...] + x_slot[...].astype(F32)
        scale = row_scale(tok_v[...])
        back = norm_back(tok_v[...], scale, gain[...].reshape(1, -1), hidden_grad)
        grad_tokens[...] = (cot_v[...].astype(F32) + back).astype(BF16)

    def summaries():
        yield from scatter_ring(
            link, 2, at, s_piece, s_loc, s_ready, s_relay, s_direct, s_one
        )
        block = summary.shape[0]
        yield from scatter_direct(
            link, 0, at,
            lambda d: s_one.at[lax.rem(d, 2), :, pl.ds((d // 2) * block, block)],
            s_slots_x, s_two,
        )
        yield from scatter_direct(link, 1, at, lambda d: s_two.at[d], s_slots_y, s_sum)
        scale = row_scale(sum_v[...])
        back = norm_back(sum_v[...], scale, gain[...].reshape(1, -1), s_sum[...])
        grad_summary[...] = back.astype(BF16)

    def weights(p, q):
        a, b, c = p, (p + 1) % 3, (p + 2) % 3
        first = p * part
        yield from scatter_ring(
            link, a, at, w_piece(p, q), w_loc.at[p, q], w_ready[p, q],
            w_relay.at[p, q], w_direct.at[p, q], w_one.at[p, q],
        )
        yield from scatter_direct(
            link, b, at,
            lambda d: w_one.at[p, q, d // 2, pl.ds(lax.rem(d, 2) * size[1], size[1])],
            w_slots_two.at[p, q], w_two.at[p, q],
        )
        base = first + at[a] * size[0]
        inner = base + at[b] * size[1]
        yield from scatter_direct(
            link, c, at,
            lambda d: w_two.at[p, q, pl.ds(pl.multiple_of(d * size[2], PACK), size[2])],
            w_slots_three.at[p, q],
            w_three.at[p, q],
        )
        mine = rows_of(w_out, inner + at[c] * size[2], size[2], q)
        copies = [link.send(w_three.at[p, q], mine, peer(c, at, k)) for k in (1, 3, 2)]
        kept = load.copy(w_three.at[p, q], mine)
        yield
        kept.wait()
        for copy in copies:
            copy.wait_recv()
        yield from gather_direct(
            link, b, at, lambda d: rows_of(w_out, base + d * size[1], size[1], q)
        )
        yield from gather_ring(
            link, a, at,
            lambda d: rows_of(w_out, first + d * size[0], size[0], q),
            lambda d, h: rows_of(
                w_out, first + d * size[0] + h * (size[0] // 2), size[0] // 2, q
            ),
        )

    def gains():
        gain_ready.wait()
        for k in range(3):
            yield from scatter_direct(
                link, k, at, lambda d, k=k: gain_sum.at[k], gain_slots.at[k], gain_sum.at[k + 1]
            )
        total = jnp.sum(gain_sum[3], axis=0, keepdims=True)
        grad_gain[...] = total / gain[...].reshape(1, -1)

    first_half = [weights(p, 0) for p in range(3)]
    second_half = [weights(p, 1) for p in range(3)]
    take_turns(
        [halo(), summaries(), *first_half, *second_half, gains()]
    )
    link.drain()


def exchange(
    near_grad, own_grad, sum_grad, w_part, gain_part, tokens, summary, norm_gain, cot
):
    rows, width = own_grad.shape
    block = summary.shape[0]
    vm = pl.BlockSpec(memory_space=pltpu.VMEM)
    far = pl.BlockSpec(memory_space=pltpu.HBM)
    total = w_part.shape[1]
    part = total // 3
    wide = width // 2
    sends = 6 + 5 + 6 + 3 + 3 + 6 * (6 + 3 + 3 + 3 + 3 + 4) + 9
    loads = 24 + 4 + 2 + 4 + 6
    sums = sum_grad.reshape(8, 4, 2 * block, width)
    grad_tokens, grad_summary, gain, w_all = pl.pallas_call(
        exchange_kernel,
        out_shape=(
            jax.ShapeDtypeStruct((rows, width), BF16),
            jax.ShapeDtypeStruct((block, width), BF16),
            jax.ShapeDtypeStruct((1, width), F32),
            jax.ShapeDtypeStruct((2, total, wide), BF16),
        ),
        in_specs=[far] * 7 + [vm, far],
        out_specs=(vm, vm, vm, far),
        scratch_shapes=[
            pltpu.VMEM((rows, width), F32),
            pltpu.VMEM((3, rows, width), BF16),
            pltpu.VMEM((rows, width), BF16),
            pltpu.VMEM((block, width), BF16),
            pltpu.VMEM((rows, width), BF16),
            pltpu.VMEM((4, 4, 2 * block, width), BF16),
            pltpu.VMEM((3, 2, 4, part // 8, wide), BF16),
            pltpu.VMEM((2, 3, rows, width), BF16),
            pltpu.VMEM((2, rows, width), BF16),
            pltpu.VMEM((rows, width), BF16),
            pltpu.VMEM((rows, width), BF16),
            pltpu.VMEM((2, rows, wide), BF16),
            pltpu.VMEM((rows, width), BF16),
            pltpu.VMEM((2, 2, 4, 2 * block, width), BF16),
            pltpu.VMEM((2, 2, 4, 2 * block, width), BF16),
            pltpu.VMEM((2, 4, 2 * block, width), BF16),
            pltpu.VMEM((3, 4, block, width), BF16),
            pltpu.VMEM((4, block, width), BF16),
            pltpu.VMEM((3, block, width), BF16),
            pltpu.VMEM((block, width), F32),
            pltpu.VMEM((3, 2, 2, 2, part // 8, wide), BF16),
            pltpu.VMEM((3, 2, 2, 2, part // 8, wide), BF16),
            pltpu.VMEM((3, 2, 2, part // 8, wide), BF16),
            pltpu.VMEM((3, 2, 3, part // 16, wide), BF16),
            pltpu.VMEM((3, 2, part // 16, wide), BF16),
            pltpu.VMEM((3, 2, 3, part // 64, wide), BF16),
            pltpu.VMEM((3, 2, part // 64, wide), BF16),
            pltpu.VMEM((4, 8, width), F32),
            pltpu.VMEM((3, 3, 8, width), F32),
            pltpu.SemaphoreType.DMA((loads,)),
            pltpu.SemaphoreType.DMA((sends,)),
            pltpu.SemaphoreType.DMA((sends,)),
        ],
        compiler_params=pltpu.CompilerParams(
            collective_id=1, has_side_effects=True, vmem_limit_bytes=60 * 1024 * 1024
        ),
        name="exchange",
    )(
        near_grad.reshape(3, 3, rows, width), own_grad, sums, w_part,
        gain_part, tokens, summary, norm_gain, cot,
    )
    return widen(w_all, grad_tokens, grad_summary, gain)


def widen_kernel(
    narrow, tok_in, sum_in, gain_in, wide, tok_out, sum_out, gain_out,
    held, stage, tok_v, sum_v, in_sems, out_sems, pass_sems,
):
    taken = [
        pltpu.make_async_copy(tok_in, tok_v, pass_sems.at[0]),
        pltpu.make_async_copy(sum_in, sum_v, pass_sems.at[1]),
    ]
    passed = [
        pltpu.make_async_copy(tok_v, tok_out, pass_sems.at[2]),
        pltpu.make_async_copy(sum_v, sum_out, pass_sems.at[3]),
    ]
    for copy in taken:
        copy.start()
    rows = stage.shape[1]
    count = narrow.shape[1] // rows
    reads, writes = [], []
    for k in range(count):
        here = pl.ds(k * rows, rows)
        reads.append(pltpu.make_async_copy(narrow.at[:, here], held.at[k], in_sems.at[k]))
        reads[k].start()
    gain_out[...] = gain_in[...].reshape(gain_out.shape)
    for k in range(count):
        if k >= 3:
            writes[k - 3].wait()
        reads[k].wait()
        half = held.shape[3]
        stage[k % 3, :, :half] = held[k, 0].astype(F32)
        stage[k % 3, :, half:] = held[k, 1].astype(F32)
        here = pl.ds(k * rows, rows)
        writes.append(pltpu.make_async_copy(stage.at[k % 3], wide.at[here], out_sems.at[k % 3]))
        writes[k].start()
        if k == 2:
            for taking, passing in zip(taken, passed):
                taking.wait()
                passing.start()
    for copy in writes[-3:] + passed:
        copy.wait()


def widen(narrow, grad_tokens, grad_summary, gain):
    total, width = narrow.shape[1], 2 * narrow.shape[2]
    count = 12
    vm = pl.BlockSpec(memory_space=pltpu.VMEM)
    far = pl.BlockSpec(memory_space=pltpu.HBM)
    return pl.pallas_call(
        widen_kernel,
        out_shape=(
            jax.ShapeDtypeStruct((total, width), F32),
            jax.ShapeDtypeStruct(grad_tokens.shape, BF16),
            jax.ShapeDtypeStruct(grad_summary.shape, BF16),
            jax.ShapeDtypeStruct((width,), F32),
        ),
        in_specs=[far, far, far, vm],
        out_specs=(far, far, far, vm),
        scratch_shapes=[
            pltpu.VMEM((count, 2, total // count, width // 2), BF16),
            pltpu.VMEM((3, total // count, width), F32),
            pltpu.VMEM(grad_tokens.shape, BF16),
            pltpu.VMEM(grad_summary.shape, BF16),
            pltpu.SemaphoreType.DMA((count,)),
            pltpu.SemaphoreType.DMA((3,)),
            pltpu.SemaphoreType.DMA((4,)),
        ],
        compiler_params=pltpu.CompilerParams(vmem_limit_bytes=60 * 1024 * 1024),
        name="widen",
    )(narrow, grad_tokens, grad_summary, gain)


def row_scale(rows):
    values = rows.astype(F32)
    return lax.rsqrt(jnp.mean(values * values, axis=-1, keepdims=True) + epsilon)


def normalize(rows, gain):
    scale = row_scale(rows)
    return ((rows.astype(F32) * scale * gain).astype(BF16), scale)


def norm_back(rows, scale, gain, grad_norm):
    values = rows.astype(F32)
    scaled = gain * grad_norm
    return scale * scaled - values * scale**3 * jnp.mean(values * scaled, axis=-1, keepdims=True)


def dot(a, b, ca, cb):
    return lax.dot_general(a, b, (((ca,), (cb,)), ((), ())), preferred_element_type=F32)


def layer_kernel(
    counts, pattern, blocks, near, summ, w_in, tok, cot,
    updated, near_out, own_out, sum_out, w_out, gain_part,
    w, own_v, near_grad, own_grad, sum_grad, w_part, pack_sems, local_sems,
    xp, kp, vp, dkt, dvt, scores, probs, bias, qs, gs, qst, gst, acc, m_ref, l_ref, d_ref,
    q_all, g_all, o_all, dq_all,
):
    rows = tok.shape[0]
    width = tok.shape[1]
    quads = width // CHUNK
    head_size = width // HEADS
    stack = QUAD * rows
    factor = 1.0 / math.sqrt(head_size)
    n_blocks = summ.shape[0] // SBLK
    yp = kp
    zk = scores.at[:, 0:width]
    zv = scores.at[:, width : 2 * width]

    load = Loader(local_sems)
    own_ready = load.copy(near.at[NEAR // 2], own_v)
    w_ready = [load.copy(w_in.at[k], w.at[k]) for k in (0, 3, 1, 2)]

    grid_row = 4 * lax.axis_index("ty_0") + lax.axis_index("ty_1")
    grid_col = 2 * lax.axis_index("tx_0") + lax.axis_index("tx_1")
    meta = []
    for t in range(NEAR):
        r, c = grid_row + (t // 3 - 1), grid_col + (t % 3 - 1)
        inside = (r >= 0) & (r < 8) & (c >= 0) & (c < 8)
        n = counts[jnp.clip(r, 0, 7), jnp.clip(c, 0, 7)]
        meta.append(jnp.where(inside & (pattern[grid_row, grid_col, t] == 1), n, 0))
    for b in range(n_blocks):
        meta.append(jnp.where(blocks[0, 0, b] == 1, 1, 0))
    meta.append(counts[grid_row, grid_col])

    def packed(k, src, at, size):
        return pltpu.make_async_copy(
            src.at[pl.ds(0, size)], xp.at[pl.ds(pl.multiple_of(at, PACK), size)], pack_sems.at[k]
        )

    packs = []
    block_at = []
    total = jnp.int32(0)
    for b in range(n_blocks):
        block_at.append(total)
        flag = meta[NEAR + b]

        src = summ.at[pl.ds(b * SBLK, SBLK)]
        packs.append((flag == 1, packed(NEAR + b, src, total, SBLK)))
        total = total + SBLK * flag
    summ_end = total
    tile_at = []
    for t in range(NEAR):
        tile_at.append(total)
        n = meta[t]

        size = pl.multiple_of(((n + (PACK - 1)) // PACK) * PACK, PACK)
        packs.append((n > 0, packed(t, near.at[t], total, size)))
        total = total + size
    for live, copy in packs:
        pl.when(live)(copy.start)
    xp[pl.ds(pl.multiple_of(total, PACK), CHUNK), :] = jnp.zeros((CHUNK, width), BF16)
    chunks = (total + (CHUNK - 1)) // CHUNK

    place = lax.broadcasted_iota(jnp.int32, bias.shape, 1)
    live = place < summ_end
    for t in range(NEAR):
        live = live | ((place >= tile_at[t]) & (place < tile_at[t] + meta[t]))
    bias[...] = jnp.where(live, 0.0, -1e30)

    own_ready.wait()
    for copy in w_ready[:2]:
        copy.wait()
    own = own_v[...]
    valid = lax.broadcasted_iota(jnp.int32, (rows, width), 0) < meta[NEAR + n_blocks]
    masked = jnp.where(valid, cot[...].astype(F32), 0.0).astype(BF16)
    q_all[...] = (dot(own, w[0], 1, 0).astype(BF16).astype(F32) * factor).astype(BF16)
    g_all[...] = dot(masked, w[3], 1, 1).astype(BF16)

    for copy in w_ready[2:]:
        copy.wait()
    for live, copy in packs:
        pl.when(live)(copy.wait)

    def sweep(body):
        def pair(c, carry):
            body(pl.multiple_of(c * (2 * CHUNK), 2 * CHUNK), 2 * CHUNK)
            return carry

        def four(c, carry):
            body(pl.multiple_of(c * (4 * CHUNK), 4 * CHUNK), 4 * CHUNK)
            return carry

        lax.fori_loop(0, chunks // 4, four, 0)
        lax.fori_loop(chunks // 4 * 2, chunks // 2, pair, 0)

        @pl.when(lax.rem(chunks, 2) == 1)
        def _():
            body(pl.multiple_of((chunks - 1) * CHUNK, CHUNK), CHUNK)

    def project(start, size):
        at = pl.ds(start, size)
        x = xp[at, :]
        kp[at, :] = dot(x, w[1], 1, 0).astype(BF16)
        vp[at, :] = dot(x, w[2], 1, 0).astype(BF16)

    sweep(project)

    lane_head = lax.broadcasted_iota(jnp.int32, (rows, CHUNK), 1) // head_size

    def lanes(values):
        return [values[:, k : k + 128] for k in range(0, values.shape[1], 128)]


    def stack_up(j):
        q_part = q_all[:, j * CHUNK : (j + 1) * CHUNK].astype(F32)
        g_part = g_all[:, j * CHUNK : (j + 1) * CHUNK].astype(F32)
        for i in range(QUAD):
            here = slice(i * rows, (i + 1) * rows)
            qs[j % 2, here, :] = jnp.where(lane_head == i, q_part, 0.0).astype(BF16)
            gs[j % 2, here, :] = jnp.where(lane_head == i, g_part, 0.0).astype(BF16)
        m_ref[...] = jnp.full(m_ref.shape, -3e38, F32)

    def score(j, start, size):
        at = pl.ds(start, size)
        s = dot(qs[j % 2], kp[at, j * CHUNK : (j + 1) * CHUNK], 1, 1) + bias[0:1, at]
        scores[:, at] = s
        most = m_ref[...]
        for part in lanes(s):
            most = jnp.maximum(most, part)
        m_ref[...] = most

    stack_up(0)
    sweep(functools.partial(score, 0))
    for j in range(quads):
        cols = slice(j * CHUNK, (j + 1) * CHUNK)
        q_now, g_now = qs.at[j % 2], gs.at[j % 2]
        m_ref[...] = jnp.broadcast_to(jnp.max(m_ref[...], axis=1, keepdims=True), m_ref.shape)
        l_ref[...] = jnp.zeros(l_ref.shape, F32)
        acc[...] = jnp.zeros(acc.shape, F32)

        def mix(start, size):
            at = pl.ds(start, size)
            m = m_ref[...]
            e = [jnp.exp(part - m) for part in lanes(scores[:, at])]
            total = l_ref[...]
            for part in e:
                total = total + part
            l_ref[...] = total
            e = jnp.concatenate(e, axis=1).astype(BF16)
            probs[:, at] = e
            acc[...] += dot(e, vp[at, cols], 1, 0)

        sweep(mix)
        inv = 1.0 / jnp.sum(l_ref[...], axis=1, keepdims=True)
        out = acc[...] * inv
        d_ref[...] = jnp.broadcast_to(
            jnp.sum(out * g_now[...].astype(F32), axis=1, keepdims=True), d_ref.shape
        )
        picked = jnp.zeros((rows, CHUNK), F32)
        for i in range(QUAD):
            here = slice(i * rows, (i + 1) * rows)
            picked = jnp.where(lane_head == i, out[here], picked)
        o_all[:, cols] = picked.astype(BF16)
        qst[...] = (q_now[...].astype(F32) * inv).astype(BF16).T
        gst[...] = (g_now[...].astype(F32) * inv).astype(BF16).T
        l_ref[...] = jnp.broadcast_to(inv, l_ref.shape)
        acc[...] = jnp.zeros(acc.shape, F32)
        if j + 1 < quads:
            stack_up(j + 1)

        def back(start, size):
            at = pl.ds(start, size)
            e = probs[:, at]
            d = d_ref[...]
            dp = dot(g_now[...], vp[at, cols], 1, 1)
            delta = jnp.concatenate([part - d for part in lanes(dp)], axis=1)
            ds = (e.astype(F32) * delta).astype(BF16)
            acc[...] += dot(ds, kp[at, cols], 1, 0)
            dkt[cols, at] = dot(qst[...], ds, 1, 0).astype(BF16)
            dvt[cols, at] = dot(gst[...], e, 1, 0).astype(BF16)
            if j + 1 < quads:
                score(j + 1, start, size)

        sweep(back)
        inv2 = l_ref[...] * factor
        dq = acc[...] * jnp.concatenate([inv2, inv2], axis=1)
        picked = jnp.zeros((rows, CHUNK), F32)
        for i in range(QUAD):
            here = slice(i * rows, (i + 1) * rows)
            picked = jnp.where(lane_head == i, dq[here], picked)
        dq_all[:, cols] = picked.astype(BF16)

    w_part[0] = dot(own, dq_all[...], 0, 0).astype(BF16)
    w_part[3] = dot(o_all[...], masked, 0, 0).astype(BF16)

    def send_part(k):
        half = width // 2
        for q in range(2):
            src = w_part.at[k, :, q * half : (q + 1) * half]
            sent.append(load.copy(src, w_out.at[q, pl.ds(k * width, width)]))

    sent = []
    send_part(0)
    send_part(3)
    mixed = dot(o_all[...], w[3], 1, 0)
    updated[...] = (tok[...].astype(F32) + jnp.where(valid, mixed, 0.0)).astype(BF16)

    zk[...] = jnp.zeros(zk.shape, F32)
    zv[...] = jnp.zeros(zv.shape, F32)
    own_part = dot(dq_all[...], w[0], 1, 1)
    gain_part[...] = jnp.sum(
        (own_part * own.astype(F32)).reshape(rows // 8, 8, width), axis=0
    )

    def finish(start, size):
        at = pl.ds(start, size)
        x = xp[at, :]
        dk = dkt[:, at]
        dv = dvt[:, at]
        zk[...] += dot(dk, x, 1, 0)
        zv[...] += dot(dv, x, 1, 0)
        yt = dot(w[1], dk, 1, 0) + dot(w[2], dv, 1, 0)
        y = yt.astype(BF16).T
        yp[at, :] = y
        gain_part[...] += jnp.sum(
            (y.astype(F32) * x.astype(F32)).reshape(size // 8, 8, width), axis=0
        )

    sweep(finish)

    w_part[1] = zk[...].astype(BF16).T
    send_part(1)
    w_part[2] = zv[...].astype(BF16).T
    send_part(2)

    row_at = lax.broadcasted_iota(jnp.int32, (rows, width), 0)
    for t in range(NEAR):
        y = yp[pl.ds(pl.multiple_of(tile_at[t], PACK), rows), :].astype(F32)
        y = jnp.where(row_at < meta[t], y, 0.0)
        if t == NEAR // 2:
            own_grad[...] = y + own_part
            sent.append(load.copy(own_grad, own_out))
        else:
            near_grad[t] = y.astype(BF16)
            sent.append(load.copy(near_grad.at[t], near_out.at[t]))
    for b in range(n_blocks):
        y = yp[pl.ds(pl.multiple_of(block_at[b], SBLK), SBLK), :].astype(F32)
        keep = jnp.zeros((SBLK, width), jnp.int32) + meta[NEAR + b]
        sum_grad[b * SBLK : (b + 1) * SBLK, :] = jnp.where(keep == 1, y, 0.0).astype(BF16)
    sent.append(load.copy(sum_grad, sum_out))
    for copy in sent:
        copy.wait()


def layer(counts, pattern, blocks, near, summ, w, tok, cot):
    rows, width = tok.shape
    most = (NEAR * rows + summ.shape[0] + CHUNK - 1) // CHUNK * CHUNK
    stack = QUAD * rows
    vm = pl.BlockSpec(memory_space=pltpu.VMEM)
    sm = pl.BlockSpec(memory_space=pltpu.SMEM)
    far = pl.BlockSpec(memory_space=pl.ANY)
    n_blocks = summ.shape[0] // SBLK
    return pl.pallas_call(
        layer_kernel,
        out_shape=(
            jax.ShapeDtypeStruct((rows, width), BF16),
            jax.ShapeDtypeStruct((NEAR, rows, width), BF16),
            jax.ShapeDtypeStruct((rows, width), F32),
            jax.ShapeDtypeStruct(summ.shape, BF16),
            jax.ShapeDtypeStruct((2, 4 * width, width // 2), BF16),
            jax.ShapeDtypeStruct((8, width), F32),
        ),
        in_specs=[sm] * 3 + [far] * 3 + [vm] * 2,
        out_specs=(vm, far, far, far, far, vm),
        scratch_shapes=[
            pltpu.VMEM((4, width, width), BF16),
            pltpu.VMEM((rows, width), BF16),
            pltpu.VMEM((NEAR, rows, width), BF16),
            pltpu.VMEM((rows, width), F32),
            pltpu.VMEM(summ.shape, BF16),
            pltpu.VMEM((4, width, width), BF16),
            pltpu.SemaphoreType.DMA((NEAR + n_blocks,)),
            pltpu.SemaphoreType.DMA((5 + 8 + NEAR + 2,)),
            pltpu.VMEM((most + CHUNK, width), BF16),
            pltpu.VMEM((most + CHUNK, width), BF16),
            pltpu.VMEM((most, width), BF16),
            pltpu.VMEM((width, most), BF16),
            pltpu.VMEM((width, most), BF16),
            pltpu.VMEM((stack, most), F32),
            pltpu.VMEM((stack, most), BF16),
            pltpu.VMEM((8, most), F32),
            pltpu.VMEM((2, stack, CHUNK), BF16),
            pltpu.VMEM((2, stack, CHUNK), BF16),
            pltpu.VMEM((CHUNK, stack), BF16),
            pltpu.VMEM((CHUNK, stack), BF16),
            pltpu.VMEM((stack, CHUNK), F32),
            pltpu.VMEM((stack, 128), F32),
            pltpu.VMEM((stack, 128), F32),
            pltpu.VMEM((stack, 128), F32),
            pltpu.VMEM((rows, width), BF16),
            pltpu.VMEM((rows, width), BF16),
            pltpu.VMEM((rows, width), BF16),
            pltpu.VMEM((rows, width), BF16),
        ],
        compiler_params=pltpu.CompilerParams(vmem_limit_bytes=63 * 1024 * 1024),
        name="layer",
    )(counts, pattern, blocks, near, summ, w, tok, cot)


def local(
    tokens, summary, counts, tile_pattern, summary_pattern, norm_gain, projections, cotangent
):
    rows, width = tokens.shape[2:]
    token_rows = tokens[0, 0]
    grads_in = cotangent[0, 0]
    near, every = gather(token_rows, summary, norm_gain)
    updated, near_grad, own_grad, sum_grad, w_part, gain_part = layer(
        counts, tile_pattern, summary_pattern, near, every, projections, token_rows, grads_in
    )
    grad_proj, grad_tokens, grad_summary, grad_gain = exchange(
        near_grad, own_grad, sum_grad, w_part, gain_part, token_rows, summary, norm_gain, grads_in
    )
    return (
        updated.reshape(tokens.shape),
        grad_tokens.reshape(tokens.shape),
        grad_summary,
        grad_proj.reshape(projections.shape),
        grad_gain,
    )


def solution(mesh):
    finer = Mesh(
        mesh.devices.reshape(2, 4, 4, 2, mesh.shape["slide"]),
        ("ty_0", "ty_1", "tx_0", "tx_1", "slide"),
    )
    return jax.shard_map(
        local,
        mesh=finer,
        in_specs=(
            P(SLIDE_TY, TX, None, None),
            P(SLIDE_TY_TX, None),
            P("slide", None),
            P("slide", None, None),
            P(SLIDE_TY, TX, None),
            P(),
            P(),
            P(SLIDE_TY, TX, None, None),
        ),
        out_specs=(
            P(SLIDE_TY, TX, None, None),
            P(SLIDE_TY, TX, None, None),
            P(SLIDE_TY_TX, None),
            P("slide", None, None),
            P("slide"),
        ),
        check_vma=False,
    )
```

```python
import functools
import math

import jax
import jax.numpy as jnp
from jax import lax
from jax.experimental import pallas as pl
from jax.experimental.pallas import tpu as pltpu
from jax.sharding import Mesh
from jax.sharding import PartitionSpec as P

HEADS = 12
SBLK = 128
QUAD = 4
CHUNK = 256
PACK = 16
NEAR = 9
TX = ("tx_0", "tx_1")
SLIDE_TY = ("slide", "ty_0", "ty_1")
SLIDE_TY_TX = ("slide", "ty_0", "ty_1", "tx_0", "tx_1")
F32 = jnp.float32
LOG2E = math.log2(math.e)
BF16 = jnp.bfloat16
MESH = pl.DeviceIdType.MESH

epsilon = 1e-05


def places():
    return (
        2 * lax.axis_index("tx_1") + lax.axis_index("ty_0"),
        lax.axis_index("ty_1"),
        lax.axis_index("tx_0"),
    )


def peer(axis, at, by):
    there = lax.rem(at[axis] + (by + 4), 4)
    if axis == 0:
        return {"tx_1": there // 2, "ty_0": lax.rem(there, 2)}
    return {"ty_1": there} if axis == 1 else {"tx_0": there}


def row_peer(at, by):
    there = lax.rem(lax.axis_index("ty_0") * 4 + at[1] + (by + 8), 8)
    return {"ty_0": there // 4, "ty_1": lax.rem(there, 4)}


def greet(at):
    barrier = pltpu.get_barrier_semaphore()
    others = [peer(axis, at, by) for axis in range(3) for by in (1, 2, 3)]
    others += [row_peer(at, 1), row_peer(at, -1)]
    for other in others:
        pl.semaphore_signal(barrier, inc=1, device_id=other, device_id_type=MESH)
    return lambda: pl.semaphore_wait(barrier, len(others))


class Loader:
    def __init__(self, sems):
        self.sems, self.count = sems, 0

    def copy(self, src, dst):
        copy = pltpu.make_async_copy(src, dst, self.sems.at[self.count])
        self.count += 1
        copy.start()
        return copy


class Sender:
    def __init__(self, send_sems, recv_sems):
        self.send_sems, self.recv_sems = send_sems, recv_sems
        self.copies = []

    def send(self, src, dst, device):
        k = len(self.copies)
        copy = pltpu.make_async_remote_copy(
            src_ref=src,
            dst_ref=dst,
            send_sem=self.send_sems.at[k],
            recv_sem=self.recv_sems.at[k],
            device_id=device,
            device_id_type=MESH,
        )
        copy.start()
        self.copies.append(copy)
        return copy

    def drain(self):
        for copy in self.copies:
            copy.wait_send()


def take_turns(tasks):
    tasks = list(tasks)
    while tasks:
        tasks = [task for task in tasks if next(task, "end") != "end"]


def send_across(link, at, src, relay, slots):
    wide = src.shape[1] // 2
    halves = [slice(0, wide), slice(wide, 2 * wide)]
    ways = [peer(0, at, 1), peer(0, at, -1)]
    first = [link.send(src.at[:, halves[k]], relay.at[k], ways[k]) for k in range(2)]
    yield
    second = []
    for k in range(2):
        first[k].wait_recv()
        second.append(link.send(relay.at[k], slots[k].at[:, halves[k]], ways[k]))
    yield
    for copy in second:
        copy.wait_recv()


def added(*refs):
    total = refs[0][...].astype(F32)
    for ref in refs[1:]:
        total = total + ref[...].astype(F32)
    return total


def scatter_ring(link, axis, at, piece, held, ready, relay, direct, out):
    c = at[axis]
    right, left, across = [lax.rem(c + k, 4) for k in (1, 3, 2)]
    to_right, to_left = peer(axis, at, 1), peer(axis, at, -1)
    far_a = link.send(piece(across, 0), relay.at[0, 0], to_right)
    far_b = link.send(piece(across, 1), relay.at[0, 1], to_left)
    near_b = link.send(piece(right, 1), direct.at[0, 1], to_right)
    near_a = link.send(piece(left, 0), direct.at[1, 0], to_left)
    yield
    for copy in ready:
        copy.wait()
    far_a.wait_recv()
    relay[1, 0] = added(relay.at[0, 0], held.at[0]).astype(BF16)
    sum_a = link.send(relay.at[1, 0], direct.at[0, 0], to_right)
    far_b.wait_recv()
    relay[1, 1] = added(relay.at[0, 1], held.at[1]).astype(BF16)
    sum_b = link.send(relay.at[1, 1], direct.at[1, 1], to_left)
    yield
    for copy in (near_b, near_a, sum_a, sum_b):
        copy.wait_recv()
    for half in range(2):
        out[half] = added(held.at[2 + half], direct.at[0, half], direct.at[1, half]).astype(BF16)


def scatter_direct(link, axis, at, piece, slots, out):
    copies = [
        link.send(piece(lax.rem(at[axis] + k, 4)), slots.at[k - 1], peer(axis, at, k))
        for k in (1, 3, 2)
    ]
    yield
    for copy in copies:
        copy.wait_recv()
    total = added(piece(at[axis]), slots.at[0], slots.at[1], slots.at[2])
    out[...] = total.astype(out.dtype)


def gather_direct(link, axis, at, place):
    mine = place(at[axis])
    copies = [link.send(mine, mine, peer(axis, at, k)) for k in (1, 3, 2)]
    yield
    for copy in copies:
        copy.wait_recv()


def gather_ring(link, axis, at, place, half_place):
    c = at[axis]
    right, left = lax.rem(c + 1, 4), lax.rem(c + 3, 4)
    to_right, to_left = peer(axis, at, 1), peer(axis, at, -1)
    mine = place(c)
    one = link.send(mine, mine, to_right)
    two = link.send(mine, mine, to_left)
    yield
    one.wait_recv()
    half = half_place(left, 0)
    three = link.send(half, half, to_right)
    two.wait_recv()
    half = half_place(right, 1)
    four = link.send(half, half, to_left)
    yield
    three.wait_recv()
    four.wait_recv()


def gather_kernel(
    tokens, summary, gain, near, every, hidden, summ, relay, local_sems, send_sems, recv_sems
):
    at = places()
    x, y, z = at
    x_hi, x_lo = lax.axis_index("tx_1"), lax.axis_index("ty_0")
    met = greet(at)
    summ[...] = normalize(summary[...], gain[...].reshape(1, -1))[0]
    hidden[...] = normalize(tokens[...], gain[...].reshape(1, -1))[0]
    load = Loader(local_sems)
    own = every.at[x_lo, y, z, x_hi]
    kept = [load.copy(summ, own), load.copy(hidden, near.at[1, 1])]
    met()
    link = Sender(send_sems, recv_sems)
    from_x, from_z = 2 - 2 * x_hi, 2 * x_hi

    def halo():
        slots = [near.at[1, 2 - 2 * (lax.rem(x + by, 4) // 2)] for by in (1, 3)]
        beside = send_across(link, at, hidden, relay, slots)
        next(beside)
        rows = [
            link.send(hidden, near.at[0, 1], row_peer(at, 1)),
            link.send(hidden, near.at[2, 1], row_peer(at, -1)),
        ]
        yield
        next(beside)
        yield
        for _ in beside:
            pass
        there = {"tx_0": lax.rem(z + (5 - 2 * x_hi), 4)}
        beyond = link.send(near.at[1, from_x], near.at[1, from_z], there)
        rows.append(link.send(near.at[1, from_x], near.at[0, from_x], row_peer(at, 1)))
        rows.append(link.send(near.at[1, from_x], near.at[2, from_x], row_peer(at, -1)))
        yield
        beyond.wait_recv()
        rows.append(link.send(near.at[1, from_z], near.at[0, from_z], row_peer(at, 1)))
        rows.append(link.send(near.at[1, from_z], near.at[2, from_z], row_peer(at, -1)))
        yield
        yield
        yield
        for copy in rows:
            copy.wait_recv()

    def summaries():
        copies = [link.send(summ, own, peer(1, at, k)) for k in (1, 3, 2)]
        yield
        kept[0].wait()
        for copy in copies:
            copy.wait_recv()
        yield from gather_direct(
            link, 0, at, lambda d: every.at[lax.rem(d, 2), :, z, d // 2]
        )
        yield from gather_ring(
            link, 2, at, lambda d: every.at[:, :, d], lambda d, half: every.at[half, :, d]
        )

    take_turns([halo(), summaries()])
    kept[1].wait()
    link.drain()


def gather(tokens, summary, gain):
    rows, width = tokens.shape
    block = summary.shape[0]
    vm = pl.BlockSpec(memory_space=pltpu.VMEM)
    sends = 4 + 6 + 1 + 3 + 3 + 4
    near, every = pl.pallas_call(
        gather_kernel,
        out_shape=(
            jax.ShapeDtypeStruct((3, 3, rows, width), BF16),
            jax.ShapeDtypeStruct((2, 4, 4, 2, block, width), BF16),
        ),
        in_specs=[vm] * 3,
        out_specs=(pl.BlockSpec(memory_space=pltpu.HBM),) * 2,
        scratch_shapes=[
            pltpu.VMEM((rows, width), BF16),
            pltpu.VMEM((block, width), BF16),
            pltpu.VMEM((2, rows, width // 2), BF16),
            pltpu.SemaphoreType.DMA((2,)),
            pltpu.SemaphoreType.DMA((sends,)),
            pltpu.SemaphoreType.DMA((sends,)),
        ],
        compiler_params=pltpu.CompilerParams(
            collective_id=0, has_side_effects=True, vmem_limit_bytes=60 * 1024 * 1024
        ),
        name="gather",
    )(tokens, summary, gain)
    return near.reshape(NEAR, rows, width), every.reshape(-1, width)


def exchange_kernel(
    near, own, sums, w_in, gain_in, tokens, summary, gain, cot,
    grad_tokens, grad_summary, grad_gain, w_out,
    own_v, mid, tok_v, sum_v, cot_v, s_loc, w_loc,
    beside, row_sum, z_slot, x_slot, x_relay, message,
    s_relay, s_direct, s_one, s_slots_x, s_two, s_slots_y, s_sum,
    w_relay, w_direct, w_one, w_slots_two, w_two, w_slots_three, w_three,
    gain_sum, gain_slots, local_sems, send_sems, recv_sems,
):
    at = places()
    x, y, z = at
    x_hi = lax.axis_index("tx_1")
    met = greet(at)
    load = Loader(local_sems)
    part = w_in.shape[1] // 3
    size = [part // 4, part // 16, part // 64]
    s_half = sums.shape[0] // 2

    def rows_of(ref, start, count, q):
        return ref.at[q, pl.ds(pl.multiple_of(start, PACK), count)]

    def s_piece(d, h):
        return sums.at[pl.ds(h * s_half, s_half), d]

    def w_piece(p, q):
        half = size[0] // 2
        return lambda d, h: rows_of(w_in, p * part + d * size[0] + h * half, half, q)

    def own_pieces(piece, axis, slots):
        c = at[axis]
        right, left = lax.rem(c + 1, 4), lax.rem(c + 3, 4)
        wanted = ((right, 0), (left, 1), (c, 0), (c, 1))
        return [load.copy(piece(*wanted[k]), slots.at[k]) for k in range(4)]

    w_ready = {
        (p, q): own_pieces(w_piece(p, q), p, w_loc.at[p, q]) for q in range(2) for p in range(3)
    }
    s_ready = own_pieces(s_piece, 2, s_loc)
    mid_ready = load.copy(near.at[1], mid)
    gain_ready = load.copy(gain_in, gain_sum.at[0])
    rest_ready = [
        load.copy(own, own_v), load.copy(tokens, tok_v), load.copy(summary, sum_v),
        load.copy(cot, cot_v),
    ]
    met()
    link = Sender(send_sems, recv_sems)

    def halo():
        rows = []
        for j in (0, 2, 1):
            up = link.send(near.at[2, j], beside.at[0, j], row_peer(at, 1))
            down = link.send(near.at[0, j], beside.at[1, j], row_peer(at, -1))
            rows.append((j, up, down))
        yield
        mid_ready.wait()
        for j, up, down in rows[:2]:
            up.wait_recv()
            down.wait_recv()
            row_sum[j // 2] = added(mid.at[j], beside.at[0, j], beside.at[1, j]).astype(BF16)
        there = {"tx_0": lax.rem(z + (3 + 2 * x_hi), 4)}
        far = link.send(row_sum.at[x_hi], z_slot, there)
        yield
        far.wait_recv()
        message[...] = added(row_sum.at[1 - x_hi], z_slot).astype(BF16)
        last = send_across(link, at, message, x_relay, (x_slot, x_slot))
        next(last)
        yield
        next(last)
        _, up, down = rows[2]
        up.wait_recv()
        down.wait_recv()
        for copy in rest_ready:
            copy.wait()
        own_v[...] += added(beside.at[0, 1], beside.at[1, 1])
        yield
        for _ in last:
            pass
        hidden_grad = own_v[...] + x_slot[...].astype(F32)
        scale = row_scale(tok_v[...])
        back = norm_back(tok_v[...], scale, gain[...].reshape(1, -1), hidden_grad)
        grad_tokens[...] = (cot_v[...].astype(F32) + back).astype(BF16)

    def summaries():
        yield from scatter_ring(
            link, 2, at, s_piece, s_loc, s_ready, s_relay, s_direct, s_one
        )
        block = summary.shape[0]
        yield from scatter_direct(
            link, 0, at,
            lambda d: s_one.at[lax.rem(d, 2), :, pl.ds((d // 2) * block, block)],
            s_slots_x, s_two,
        )
        yield from scatter_direct(link, 1, at, lambda d: s_two.at[d], s_slots_y, s_sum)
        scale = row_scale(sum_v[...])
        back = norm_back(sum_v[...], scale, gain[...].reshape(1, -1), s_sum[...])
        grad_summary[...] = back.astype(BF16)

    def weights(p, q):
        a, b, c = p, (p + 1) % 3, (p + 2) % 3
        first = p * part
        yield from scatter_ring(
            link, a, at, w_piece(p, q), w_loc.at[p, q], w_ready[p, q],
            w_relay.at[p, q], w_direct.at[p, q], w_one.at[p, q],
        )
        yield from scatter_direct(
            link, b, at,
            lambda d: w_one.at[p, q, d // 2, pl.ds(lax.rem(d, 2) * size[1], size[1])],
            w_slots_two.at[p, q], w_two.at[p, q],
        )
        base = first + at[a] * size[0]
        inner = base + at[b] * size[1]
        yield from scatter_direct(
            link, c, at,
            lambda d: w_two.at[p, q, pl.ds(pl.multiple_of(d * size[2], PACK), size[2])],
            w_slots_three.at[p, q],
            w_three.at[p, q],
        )
        mine = rows_of(w_out, inner + at[c] * size[2], size[2], q)
        copies = [link.send(w_three.at[p, q], mine, peer(c, at, k)) for k in (1, 3, 2)]
        kept = load.copy(w_three.at[p, q], mine)
        yield
        kept.wait()
        for copy in copies:
            copy.wait_recv()
        yield from gather_direct(
            link, b, at, lambda d: rows_of(w_out, base + d * size[1], size[1], q)
        )
        yield from gather_ring(
            link, a, at,
            lambda d: rows_of(w_out, first + d * size[0], size[0], q),
            lambda d, h: rows_of(
                w_out, first + d * size[0] + h * (size[0] // 2), size[0] // 2, q
            ),
        )

    def gains():
        gain_ready.wait()
        for k in range(3):
            yield from scatter_direct(
                link, k, at, lambda d, k=k: gain_sum.at[k], gain_slots.at[k], gain_sum.at[k + 1]
            )
        total = jnp.sum(gain_sum[3], axis=0, keepdims=True)
        grad_gain[...] = total / gain[...].reshape(1, -1)

    first_half = [weights(p, 0) for p in range(3)]
    second_half = [weights(p, 1) for p in range(3)]
    take_turns(
        [halo(), summaries(), *first_half, *second_half, gains()]
    )
    link.drain()


def exchange(
    near_grad, own_grad, sum_grad, w_part, gain_part, tokens, summary, norm_gain, cot
):
    rows, width = own_grad.shape
    block = summary.shape[0]
    vm = pl.BlockSpec(memory_space=pltpu.VMEM)
    far = pl.BlockSpec(memory_space=pltpu.HBM)
    total = w_part.shape[1]
    part = total // 3
    wide = width // 2
    sends = 6 + 5 + 6 + 3 + 3 + 6 * (6 + 3 + 3 + 3 + 3 + 4) + 9
    loads = 24 + 4 + 2 + 4 + 6
    sums = sum_grad.reshape(8, 4, 2 * block, width)
    grad_tokens, grad_summary, gain, w_all = pl.pallas_call(
        exchange_kernel,
        out_shape=(
            jax.ShapeDtypeStruct((rows, width), BF16),
            jax.ShapeDtypeStruct((block, width), BF16),
            jax.ShapeDtypeStruct((1, width), F32),
            jax.ShapeDtypeStruct((2, total, wide), BF16),
        ),
        in_specs=[far] * 7 + [vm, far],
        out_specs=(vm, vm, vm, far),
        scratch_shapes=[
            pltpu.VMEM((rows, width), F32),
            pltpu.VMEM((3, rows, width), BF16),
            pltpu.VMEM((rows, width), BF16),
            pltpu.VMEM((block, width), BF16),
            pltpu.VMEM((rows, width), BF16),
            pltpu.VMEM((4, 4, 2 * block, width), BF16),
            pltpu.VMEM((3, 2, 4, part // 8, wide), BF16),
            pltpu.VMEM((2, 3, rows, width), BF16),
            pltpu.VMEM((2, rows, width), BF16),
            pltpu.VMEM((rows, width), BF16),
            pltpu.VMEM((rows, width), BF16),
            pltpu.VMEM((2, rows, wide), BF16),
            pltpu.VMEM((rows, width), BF16),
            pltpu.VMEM((2, 2, 4, 2 * block, width), BF16),
            pltpu.VMEM((2, 2, 4, 2 * block, width), BF16),
            pltpu.VMEM((2, 4, 2 * block, width), BF16),
            pltpu.VMEM((3, 4, block, width), BF16),
            pltpu.VMEM((4, block, width), BF16),
            pltpu.VMEM((3, block, width), BF16),
            pltpu.VMEM((block, width), F32),
            pltpu.VMEM((3, 2, 2, 2, part // 8, wide), BF16),
            pltpu.VMEM((3, 2, 2, 2, part // 8, wide), BF16),
            pltpu.VMEM((3, 2, 2, part // 8, wide), BF16),
            pltpu.VMEM((3, 2, 3, part // 16, wide), BF16),
            pltpu.VMEM((3, 2, part // 16, wide), BF16),
            pltpu.VMEM((3, 2, 3, part // 64, wide), BF16),
            pltpu.VMEM((3, 2, part // 64, wide), BF16),
            pltpu.VMEM((4, 8, width), F32),
            pltpu.VMEM((3, 3, 8, width), F32),
            pltpu.SemaphoreType.DMA((loads,)),
            pltpu.SemaphoreType.DMA((sends,)),
            pltpu.SemaphoreType.DMA((sends,)),
        ],
        compiler_params=pltpu.CompilerParams(
            collective_id=1, has_side_effects=True, vmem_limit_bytes=60 * 1024 * 1024
        ),
        name="exchange",
    )(
        near_grad.reshape(3, 3, rows, width), own_grad, sums, w_part,
        gain_part, tokens, summary, norm_gain, cot,
    )
    return widen(w_all, grad_tokens, grad_summary, gain)


def widen_kernel(
    narrow, tok_in, sum_in, gain_in, wide, tok_out, sum_out, gain_out,
    held, stage, tok_v, sum_v, gain_v, gain_w, in_sems, out_sems, pass_sems,
):
    taken = [
        pltpu.make_async_copy(tok_in, tok_v, pass_sems.at[0]),
        pltpu.make_async_copy(sum_in, sum_v, pass_sems.at[1]),
        pltpu.make_async_copy(gain_in, gain_v, pass_sems.at[4]),
    ]
    passed = [
        pltpu.make_async_copy(tok_v, tok_out, pass_sems.at[2]),
        pltpu.make_async_copy(sum_v, sum_out, pass_sems.at[3]),
        pltpu.make_async_copy(gain_w, gain_out, pass_sems.at[5]),
    ]
    for copy in taken:
        copy.start()
    rows = stage.shape[1]
    count = narrow.shape[1] // rows
    reads, writes = [], []
    for k in range(count):
        here = pl.ds(k * rows, rows)
        reads.append(pltpu.make_async_copy(narrow.at[:, here], held.at[k], in_sems.at[k]))
        reads[k].start()
    for k in range(count):
        if k >= 3:
            writes[k - 3].wait()
        reads[k].wait()
        half = held.shape[3]
        stage[k % 3, :, :half] = held[k, 0].astype(F32)
        stage[k % 3, :, half:] = held[k, 1].astype(F32)
        here = pl.ds(k * rows, rows)
        writes.append(pltpu.make_async_copy(stage.at[k % 3], wide.at[here], out_sems.at[k % 3]))
        writes[k].start()
        if k == 2:
            for copy in taken:
                copy.wait()
            gain_w[...] = gain_v[...].reshape(gain_w.shape)
            for copy in passed:
                copy.start()
    for copy in writes[-3:] + passed:
        copy.wait()


def widen(narrow, grad_tokens, grad_summary, gain):
    total, width = narrow.shape[1], 2 * narrow.shape[2]
    count = 12
    far = pl.BlockSpec(memory_space=pltpu.HBM)
    return pl.pallas_call(
        widen_kernel,
        out_shape=(
            jax.ShapeDtypeStruct((total, width), F32),
            jax.ShapeDtypeStruct(grad_tokens.shape, BF16),
            jax.ShapeDtypeStruct(grad_summary.shape, BF16),
            jax.ShapeDtypeStruct((width,), F32),
        ),
        in_specs=[far] * 4,
        out_specs=(far,) * 4,
        scratch_shapes=[
            pltpu.VMEM((count, 2, total // count, width // 2), BF16),
            pltpu.VMEM((3, total // count, width), F32),
            pltpu.VMEM(grad_tokens.shape, BF16),
            pltpu.VMEM(grad_summary.shape, BF16),
            pltpu.VMEM((1, width), F32),
            pltpu.VMEM((width,), F32),
            pltpu.SemaphoreType.DMA((count,)),
            pltpu.SemaphoreType.DMA((3,)),
            pltpu.SemaphoreType.DMA((6,)),
        ],
        compiler_params=pltpu.CompilerParams(vmem_limit_bytes=60 * 1024 * 1024),
        name="widen",
    )(narrow, grad_tokens, grad_summary, gain)


def row_scale(rows):
    values = rows.astype(F32)
    return lax.rsqrt(jnp.mean(values * values, axis=-1, keepdims=True) + epsilon)


def normalize(rows, gain):
    scale = row_scale(rows)
    return ((rows.astype(F32) * scale * gain).astype(BF16), scale)


def norm_back(rows, scale, gain, grad_norm):
    values = rows.astype(F32)
    scaled = gain * grad_norm
    return scale * scaled - values * scale**3 * jnp.mean(values * scaled, axis=-1, keepdims=True)


def dot(a, b, ca, cb):
    return lax.dot_general(a, b, (((ca,), (cb,)), ((), ())), preferred_element_type=F32)


def layer_kernel(
    counts, pattern, blocks, near, summ, w_in, tok, cot,
    updated, near_out, own_out, sum_out, w_out, gain_part,
    w, own_v, near_grad, own_grad, sum_grad, w_part, pack_sems, local_sems,
    xp, kp, vp, dkt, dvt, scores, probs, bias, qs, gs, qst, gst, acc, m_ref, l_ref, d_ref,
    q_all, g_all, o_all, dq_all,
):
    rows = tok.shape[0]
    width = tok.shape[1]
    quads = width // CHUNK
    head_size = width // HEADS
    stack = QUAD * rows
    factor = 1.0 / math.sqrt(head_size)
    n_blocks = summ.shape[0] // SBLK
    yp = kp
    zk = scores.at[:, 0:width]
    zv = scores.at[:, width : 2 * width]

    load = Loader(local_sems)
    own_ready = load.copy(near.at[NEAR // 2], own_v)
    w_ready = [load.copy(w_in.at[k], w.at[k]) for k in (0, 3, 1, 2)]

    grid_row = 4 * lax.axis_index("ty_0") + lax.axis_index("ty_1")
    grid_col = 2 * lax.axis_index("tx_0") + lax.axis_index("tx_1")
    meta = []
    for t in range(NEAR):
        r, c = grid_row + (t // 3 - 1), grid_col + (t % 3 - 1)
        inside = (r >= 0) & (r < 8) & (c >= 0) & (c < 8)
        n = counts[jnp.clip(r, 0, 7), jnp.clip(c, 0, 7)]
        meta.append(jnp.where(inside & (pattern[grid_row, grid_col, t] == 1), n, 0))
    for b in range(n_blocks):
        meta.append(jnp.where(blocks[0, 0, b] == 1, 1, 0))
    meta.append(counts[grid_row, grid_col])

    def packed(k, src, at, size):
        return pltpu.make_async_copy(
            src.at[pl.ds(0, size)], xp.at[pl.ds(pl.multiple_of(at, PACK), size)], pack_sems.at[k]
        )

    packs = []
    block_at = []
    total = jnp.int32(0)
    for b in range(n_blocks):
        block_at.append(total)
        flag = meta[NEAR + b]

        src = summ.at[pl.ds(b * SBLK, SBLK)]
        packs.append((flag == 1, packed(NEAR + b, src, total, SBLK)))
        total = total + SBLK * flag
    summ_end = total
    tile_at = []
    for t in range(NEAR):
        tile_at.append(total)
        n = meta[t]

        size = pl.multiple_of(((n + (PACK - 1)) // PACK) * PACK, PACK)
        packs.append((n > 0, packed(t, near.at[t], total, size)))
        total = total + size
    for live, copy in packs:
        pl.when(live)(copy.start)
    xp[pl.ds(pl.multiple_of(total, PACK), CHUNK), :] = jnp.zeros((CHUNK, width), BF16)
    chunks = (total + (CHUNK - 1)) // CHUNK

    place = lax.broadcasted_iota(jnp.int32, bias.shape, 1)
    live = place < summ_end
    for t in range(NEAR):
        live = live | ((place >= tile_at[t]) & (place < tile_at[t] + meta[t]))
    bias[...] = jnp.where(live, 0.0, -1e30)

    own_ready.wait()
    for copy in w_ready[:2]:
        copy.wait()
    own = own_v[...]
    valid = lax.broadcasted_iota(jnp.int32, (rows, width), 0) < meta[NEAR + n_blocks]
    masked = jnp.where(valid, cot[...].astype(F32), 0.0).astype(BF16)
    q_all[...] = (dot(own, w[0], 1, 0) * (factor * LOG2E)).astype(BF16)
    g_all[...] = dot(masked, w[3], 1, 1).astype(BF16)

    for copy in w_ready[2:]:
        copy.wait()
    for live, copy in packs:
        pl.when(live)(copy.wait)

    def sweep(body):
        def pair(c, carry):
            body(pl.multiple_of(c * (2 * CHUNK), 2 * CHUNK), 2 * CHUNK)
            return carry

        def four(c, carry):
            body(pl.multiple_of(c * (4 * CHUNK), 4 * CHUNK), 4 * CHUNK)
            return carry

        lax.fori_loop(0, chunks // 4, four, 0)
        lax.fori_loop(chunks // 4 * 2, chunks // 2, pair, 0)

        @pl.when(lax.rem(chunks, 2) == 1)
        def _():
            body(pl.multiple_of((chunks - 1) * CHUNK, CHUNK), CHUNK)

    def project(start, size):
        at = pl.ds(start, size)
        x = xp[at, :]
        kp[at, :] = dot(x, w[1], 1, 0).astype(BF16)
        vp[at, :] = dot(x, w[2], 1, 0).astype(BF16)

    sweep(project)

    lane_head = lax.broadcasted_iota(jnp.int32, (rows, CHUNK), 1) // head_size

    def lanes(values):
        return [values[:, k : k + 128] for k in range(0, values.shape[1], 128)]


    def stack_up(j):
        q_part = q_all[:, j * CHUNK : (j + 1) * CHUNK].astype(F32)
        g_part = g_all[:, j * CHUNK : (j + 1) * CHUNK].astype(F32)
        for i in range(QUAD):
            here = slice(i * rows, (i + 1) * rows)
            qs[j % 2, here, :] = jnp.where(lane_head == i, q_part, 0.0).astype(BF16)
            gs[j % 2, here, :] = jnp.where(lane_head == i, g_part, 0.0).astype(BF16)
        m_ref[...] = jnp.full(m_ref.shape, -3e38, F32)

    def score(j, start, size):
        at = pl.ds(start, size)
        s = dot(qs[j % 2], kp[at, j * CHUNK : (j + 1) * CHUNK], 1, 1) + bias[0:1, at]
        scores[:, at] = s
        most = m_ref[...]
        for part in lanes(s):
            most = jnp.maximum(most, part)
        m_ref[...] = most

    stack_up(0)
    sweep(functools.partial(score, 0))
    for j in range(quads):
        cols = slice(j * CHUNK, (j + 1) * CHUNK)
        q_now, g_now = qs.at[j % 2], gs.at[j % 2]
        m_ref[...] = jnp.broadcast_to(jnp.max(m_ref[...], axis=1, keepdims=True), m_ref.shape)
        l_ref[...] = jnp.zeros(l_ref.shape, F32)
        acc[...] = jnp.zeros(acc.shape, F32)

        def mix(start, size):
            at = pl.ds(start, size)
            m = m_ref[...]
            e = [jnp.exp2(part - m) for part in lanes(scores[:, at])]
            total = l_ref[...]
            for part in e:
                total = total + part
            l_ref[...] = total
            e = jnp.concatenate(e, axis=1).astype(BF16)
            probs[:, at] = e
            acc[...] += dot(e, vp[at, cols], 1, 0)

        sweep(mix)
        inv = 1.0 / jnp.sum(l_ref[...], axis=1, keepdims=True)
        out = acc[...] * inv
        d_ref[...] = jnp.broadcast_to(
            jnp.sum(out * g_now[...].astype(F32), axis=1, keepdims=True), d_ref.shape
        )
        picked = jnp.zeros((rows, CHUNK), F32)
        for i in range(QUAD):
            here = slice(i * rows, (i + 1) * rows)
            picked = jnp.where(lane_head == i, out[here], picked)
        o_all[:, cols] = picked.astype(BF16)
        qst[...] = (q_now[...].astype(F32) * (inv / LOG2E)).astype(BF16).T
        gst[...] = (g_now[...].astype(F32) * inv).astype(BF16).T
        l_ref[...] = jnp.broadcast_to(inv, l_ref.shape)
        acc[...] = jnp.zeros(acc.shape, F32)
        if j + 1 < quads:
            stack_up(j + 1)

        def back(start, size):
            at = pl.ds(start, size)
            e = probs[:, at]
            d = d_ref[...]
            dp = dot(g_now[...], vp[at, cols], 1, 1)
            delta = jnp.concatenate([part - d for part in lanes(dp)], axis=1)
            ds = (e.astype(F32) * delta).astype(BF16)
            acc[...] += dot(ds, kp[at, cols], 1, 0)
            dkt[cols, at] = dot(qst[...], ds, 1, 0).astype(BF16)
            dvt[cols, at] = dot(gst[...], e, 1, 0).astype(BF16)
            if j + 1 < quads:
                score(j + 1, start, size)

        sweep(back)
        inv2 = l_ref[...] * factor
        dq = acc[...] * jnp.concatenate([inv2, inv2], axis=1)
        picked = jnp.zeros((rows, CHUNK), F32)
        for i in range(QUAD):
            here = slice(i * rows, (i + 1) * rows)
            picked = jnp.where(lane_head == i, dq[here], picked)
        dq_all[:, cols] = picked.astype(BF16)

    w_part[0] = dot(own, dq_all[...], 0, 0).astype(BF16)
    w_part[3] = dot(o_all[...], masked, 0, 0).astype(BF16)

    def send_part(k):
        half = width // 2
        for q in range(2):
            src = w_part.at[k, :, q * half : (q + 1) * half]
            sent.append(load.copy(src, w_out.at[q, pl.ds(k * width, width)]))

    sent = []
    send_part(0)
    send_part(3)
    mixed = dot(o_all[...], w[3], 1, 0)
    updated[...] = (tok[...].astype(F32) + jnp.where(valid, mixed, 0.0)).astype(BF16)

    zk[...] = jnp.zeros(zk.shape, F32)
    zv[...] = jnp.zeros(zv.shape, F32)
    own_part = dot(dq_all[...], w[0], 1, 1)
    gain_part[...] = jnp.sum(
        (own_part * own.astype(F32)).reshape(rows // 8, 8, width), axis=0
    )

    def finish(start, size):
        at = pl.ds(start, size)
        x = xp[at, :]
        dk = dkt[:, at]
        dv = dvt[:, at]
        zk[...] += dot(dk, x, 1, 0)
        zv[...] += dot(dv, x, 1, 0)
        yt = dot(w[1], dk, 1, 0) + dot(w[2], dv, 1, 0)
        y = yt.astype(BF16).T
        yp[at, :] = y
        gain_part[...] += jnp.sum(
            (y.astype(F32) * x.astype(F32)).reshape(size // 8, 8, width), axis=0
        )

    sweep(finish)

    w_part[1] = zk[...].astype(BF16).T
    send_part(1)
    w_part[2] = zv[...].astype(BF16).T
    send_part(2)

    row_at = lax.broadcasted_iota(jnp.int32, (rows, width), 0)
    for t in range(NEAR):
        y = yp[pl.ds(pl.multiple_of(tile_at[t], PACK), rows), :].astype(F32)
        y = jnp.where(row_at < meta[t], y, 0.0)
        if t == NEAR // 2:
            own_grad[...] = y + own_part
            sent.append(load.copy(own_grad, own_out))
        else:
            near_grad[t] = y.astype(BF16)
            sent.append(load.copy(near_grad.at[t], near_out.at[t]))
    for b in range(n_blocks):
        y = yp[pl.ds(pl.multiple_of(block_at[b], SBLK), SBLK), :].astype(F32)
        keep = jnp.zeros((SBLK, width), jnp.int32) + meta[NEAR + b]
        sum_grad[b * SBLK : (b + 1) * SBLK, :] = jnp.where(keep == 1, y, 0.0).astype(BF16)
    sent.append(load.copy(sum_grad, sum_out))
    for copy in sent:
        copy.wait()


def layer(counts, pattern, blocks, near, summ, w, tok, cot):
    rows, width = tok.shape
    most = (NEAR * rows + summ.shape[0] + CHUNK - 1) // CHUNK * CHUNK
    stack = QUAD * rows
    vm = pl.BlockSpec(memory_space=pltpu.VMEM)
    sm = pl.BlockSpec(memory_space=pltpu.SMEM)
    far = pl.BlockSpec(memory_space=pl.ANY)
    n_blocks = summ.shape[0] // SBLK
    return pl.pallas_call(
        layer_kernel,
        out_shape=(
            jax.ShapeDtypeStruct((rows, width), BF16),
            jax.ShapeDtypeStruct((NEAR, rows, width), BF16),
            jax.ShapeDtypeStruct((rows, width), F32),
            jax.ShapeDtypeStruct(summ.shape, BF16),
            jax.ShapeDtypeStruct((2, 4 * width, width // 2), BF16),
            jax.ShapeDtypeStruct((8, width), F32),
        ),
        in_specs=[sm] * 3 + [far] * 3 + [vm] * 2,
        out_specs=(vm, far, far, far, far, vm),
        scratch_shapes=[
            pltpu.VMEM((4, width, width), BF16),
            pltpu.VMEM((rows, width), BF16),
            pltpu.VMEM((NEAR, rows, width), BF16),
            pltpu.VMEM((rows, width), F32),
            pltpu.VMEM(summ.shape, BF16),
            pltpu.VMEM((4, width, width), BF16),
            pltpu.SemaphoreType.DMA((NEAR + n_blocks,)),
            pltpu.SemaphoreType.DMA((5 + 8 + NEAR + 2,)),
            pltpu.VMEM((most + CHUNK, width), BF16),
            pltpu.VMEM((most + CHUNK, width), BF16),
            pltpu.VMEM((most, width), BF16),
            pltpu.VMEM((width, most), BF16),
            pltpu.VMEM((width, most), BF16),
            pltpu.VMEM((stack, most), F32),
            pltpu.VMEM((stack, most), BF16),
            pltpu.VMEM((8, most), F32),
            pltpu.VMEM((2, stack, CHUNK), BF16),
            pltpu.VMEM((2, stack, CHUNK), BF16),
            pltpu.VMEM((CHUNK, stack), BF16),
            pltpu.VMEM((CHUNK, stack), BF16),
            pltpu.VMEM((stack, CHUNK), F32),
            pltpu.VMEM((stack, 128), F32),
            pltpu.VMEM((stack, 128), F32),
            pltpu.VMEM((stack, 128), F32),
            pltpu.VMEM((rows, width), BF16),
            pltpu.VMEM((rows, width), BF16),
            pltpu.VMEM((rows, width), BF16),
            pltpu.VMEM((rows, width), BF16),
        ],
        compiler_params=pltpu.CompilerParams(vmem_limit_bytes=63 * 1024 * 1024),
        name="layer",
    )(counts, pattern, blocks, near, summ, w, tok, cot)


def local(
    tokens, summary, counts, tile_pattern, summary_pattern, norm_gain, projections, cotangent
):
    rows, width = tokens.shape[2:]
    token_rows = tokens[0, 0]
    grads_in = cotangent[0, 0]
    near, every = gather(token_rows, summary, norm_gain)
    updated, near_grad, own_grad, sum_grad, w_part, gain_part = layer(
        counts, tile_pattern, summary_pattern, near, every, projections, token_rows, grads_in
    )
    grad_proj, grad_tokens, grad_summary, grad_gain = exchange(
        near_grad, own_grad, sum_grad, w_part, gain_part, token_rows, summary, norm_gain, grads_in
    )
    return (
        updated.reshape(tokens.shape),
        grad_tokens.reshape(tokens.shape),
        grad_summary,
        grad_proj.reshape(projections.shape),
        grad_gain,
    )


def solution(mesh):
    finer = Mesh(
        mesh.devices.reshape(2, 4, 4, 2, mesh.shape["slide"]),
        ("ty_0", "ty_1", "tx_0", "tx_1", "slide"),
    )
    return jax.shard_map(
        local,
        mesh=finer,
        in_specs=(
            P(SLIDE_TY, TX, None, None),
            P(SLIDE_TY_TX, None),
            P("slide", None),
            P("slide", None, None),
            P(SLIDE_TY, TX, None),
            P(),
            P(),
            P(SLIDE_TY, TX, None, None),
        ),
        out_specs=(
            P(SLIDE_TY, TX, None, None),
            P(SLIDE_TY, TX, None, None),
            P(SLIDE_TY_TX, None),
            P("slide", None, None),
            P("slide"),
        ),
        check_vma=False,
    )
```

```python
import functools
import math

import jax
import jax.numpy as jnp
from jax import lax
from jax.experimental import pallas as pl
from jax.experimental.pallas import tpu as pltpu
from jax.sharding import Mesh
from jax.sharding import PartitionSpec as P

HEADS = 12
SBLK = 128
QUAD = 4
CHUNK = 256
PACK = 16
NEAR = 9
TX = ("tx_0", "tx_1")
SLIDE_TY = ("slide", "ty_0", "ty_1")
SLIDE_TY_TX = ("slide", "ty_0", "ty_1", "tx_0", "tx_1")
F32 = jnp.float32
BF16 = jnp.bfloat16
MESH = pl.DeviceIdType.MESH

epsilon = 1e-05


def places():
    return (
        2 * lax.axis_index("tx_1") + lax.axis_index("ty_0"),
        lax.axis_index("ty_1"),
        lax.axis_index("tx_0"),
    )


def peer(axis, at, by):
    there = lax.rem(at[axis] + (by + 4), 4)
    if axis == 0:
        return {"tx_1": there // 2, "ty_0": lax.rem(there, 2)}
    return {"ty_1": there} if axis == 1 else {"tx_0": there}


def row_peer(at, by):
    there = lax.rem(lax.axis_index("ty_0") * 4 + at[1] + (by + 8), 8)
    return {"ty_0": there // 4, "ty_1": lax.rem(there, 4)}


def greet(at):
    barrier = pltpu.get_barrier_semaphore()
    others = [peer(axis, at, by) for axis in range(3) for by in (1, 2, 3)]
    others += [row_peer(at, 1), row_peer(at, -1)]
    for other in others:
        pl.semaphore_signal(barrier, inc=1, device_id=other, device_id_type=MESH)
    return lambda: pl.semaphore_wait(barrier, len(others))


class Loader:
    def __init__(self, sems):
        self.sems, self.count = sems, 0

    def copy(self, src, dst):
        copy = pltpu.make_async_copy(src, dst, self.sems.at[self.count])
        self.count += 1
        copy.start()
        return copy


class Sender:
    def __init__(self, send_sems, recv_sems):
        self.send_sems, self.recv_sems = send_sems, recv_sems
        self.copies = []

    def send(self, src, dst, device):
        k = len(self.copies)
        copy = pltpu.make_async_remote_copy(
            src_ref=src,
            dst_ref=dst,
            send_sem=self.send_sems.at[k],
            recv_sem=self.recv_sems.at[k],
            device_id=device,
            device_id_type=MESH,
        )
        copy.start()
        self.copies.append(copy)
        return copy

    def drain(self):
        for copy in self.copies:
            copy.wait_send()


def take_turns(tasks):
    tasks = list(tasks)
    while tasks:
        tasks = [task for task in tasks if next(task, "end") != "end"]


def send_across(link, at, src, relay, slots):
    wide = src.shape[1] // 2
    halves = [slice(0, wide), slice(wide, 2 * wide)]
    ways = [peer(0, at, 1), peer(0, at, -1)]
    first = [link.send(src.at[:, halves[k]], relay.at[k], ways[k]) for k in range(2)]
    yield
    second = []
    for k in range(2):
        first[k].wait_recv()
        second.append(link.send(relay.at[k], slots[k].at[:, halves[k]], ways[k]))
    yield
    for copy in second:
        copy.wait_recv()


def added(*refs):
    total = refs[0][...].astype(F32)
    for ref in refs[1:]:
        total = total + ref[...].astype(F32)
    return total


def scatter_ring(link, axis, at, piece, held, ready, relay, direct, out):
    c = at[axis]
    right, left, across = [lax.rem(c + k, 4) for k in (1, 3, 2)]
    to_right, to_left = peer(axis, at, 1), peer(axis, at, -1)
    far_a = link.send(piece(across, 0), relay.at[0, 0], to_right)
    far_b = link.send(piece(across, 1), relay.at[0, 1], to_left)
    near_b = link.send(piece(right, 1), direct.at[0, 1], to_right)
    near_a = link.send(piece(left, 0), direct.at[1, 0], to_left)
    yield
    for copy in ready:
        copy.wait()
    far_a.wait_recv()
    relay[1, 0] = added(relay.at[0, 0], held.at[0]).astype(BF16)
    sum_a = link.send(relay.at[1, 0], direct.at[0, 0], to_right)
    far_b.wait_recv()
    relay[1, 1] = added(relay.at[0, 1], held.at[1]).astype(BF16)
    sum_b = link.send(relay.at[1, 1], direct.at[1, 1], to_left)
    yield
    for copy in (near_b, near_a, sum_a, sum_b):
        copy.wait_recv()
    for half in range(2):
        out[half] = added(held.at[2 + half], direct.at[0, half], direct.at[1, half]).astype(BF16)


def scatter_direct(link, axis, at, piece, slots, out):
    copies = [
        link.send(piece(lax.rem(at[axis] + k, 4)), slots.at[k - 1], peer(axis, at, k))
        for k in (1, 3, 2)
    ]
    yield
    for copy in copies:
        copy.wait_recv()
    total = added(piece(at[axis]), slots.at[0], slots.at[1], slots.at[2])
    out[...] = total.astype(out.dtype)


def gather_direct(link, axis, at, place):
    mine = place(at[axis])
    copies = [link.send(mine, mine, peer(axis, at, k)) for k in (1, 3, 2)]
    yield
    for copy in copies:
        copy.wait_recv()


def gather_ring(link, axis, at, place, half_place):
    c = at[axis]
    right, left = lax.rem(c + 1, 4), lax.rem(c + 3, 4)
    to_right, to_left = peer(axis, at, 1), peer(axis, at, -1)
    mine = place(c)
    one = link.send(mine, mine, to_right)
    two = link.send(mine, mine, to_left)
    yield
    one.wait_recv()
    half = half_place(left, 0)
    three = link.send(half, half, to_right)
    two.wait_recv()
    half = half_place(right, 1)
    four = link.send(half, half, to_left)
    yield
    three.wait_recv()
    four.wait_recv()


def gather_kernel(
    tokens, summary, gain, near, every, hidden, summ, relay, local_sems, send_sems, recv_sems
):
    at = places()
    x, y, z = at
    x_hi, x_lo = lax.axis_index("tx_1"), lax.axis_index("ty_0")
    met = greet(at)
    summ[...] = normalize(summary[...], gain[...].reshape(1, -1))[0]
    hidden[...] = normalize(tokens[...], gain[...].reshape(1, -1))[0]
    load = Loader(local_sems)
    own = every.at[x_lo, y, z, x_hi]
    kept = [load.copy(summ, own), load.copy(hidden, near.at[1, 1])]
    met()
    link = Sender(send_sems, recv_sems)
    from_x, from_z = 2 - 2 * x_hi, 2 * x_hi

    def halo():
        slots = [near.at[1, 2 - 2 * (lax.rem(x + by, 4) // 2)] for by in (1, 3)]
        beside = send_across(link, at, hidden, relay, slots)
        next(beside)
        rows = [
            link.send(hidden, near.at[0, 1], row_peer(at, 1)),
            link.send(hidden, near.at[2, 1], row_peer(at, -1)),
        ]
        yield
        next(beside)
        yield
        for _ in beside:
            pass
        there = {"tx_0": lax.rem(z + (5 - 2 * x_hi), 4)}
        beyond = link.send(near.at[1, from_x], near.at[1, from_z], there)
        rows.append(link.send(near.at[1, from_x], near.at[0, from_x], row_peer(at, 1)))
        rows.append(link.send(near.at[1, from_x], near.at[2, from_x], row_peer(at, -1)))
        yield
        beyond.wait_recv()
        rows.append(link.send(near.at[1, from_z], near.at[0, from_z], row_peer(at, 1)))
        rows.append(link.send(near.at[1, from_z], near.at[2, from_z], row_peer(at, -1)))
        yield
        yield
        yield
        for copy in rows:
            copy.wait_recv()

    def summaries():
        copies = [link.send(summ, own, peer(1, at, k)) for k in (1, 3, 2)]
        yield
        kept[0].wait()
        for copy in copies:
            copy.wait_recv()
        yield from gather_direct(
            link, 0, at, lambda d: every.at[lax.rem(d, 2), :, z, d // 2]
        )
        yield from gather_ring(
            link, 2, at, lambda d: every.at[:, :, d], lambda d, half: every.at[half, :, d]
        )

    take_turns([halo(), summaries()])
    kept[1].wait()
    link.drain()


def gather(tokens, summary, gain):
    rows, width = tokens.shape
    block = summary.shape[0]
    vm = pl.BlockSpec(memory_space=pltpu.VMEM)
    sends = 4 + 6 + 1 + 3 + 3 + 4
    near, every = pl.pallas_call(
        gather_kernel,
        out_shape=(
            jax.ShapeDtypeStruct((3, 3, rows, width), BF16),
            jax.ShapeDtypeStruct((2, 4, 4, 2, block, width), BF16),
        ),
        in_specs=[vm] * 3,
        out_specs=(pl.BlockSpec(memory_space=pltpu.HBM),) * 2,
        scratch_shapes=[
            pltpu.VMEM((rows, width), BF16),
            pltpu.VMEM((block, width), BF16),
            pltpu.VMEM((2, rows, width // 2), BF16),
            pltpu.SemaphoreType.DMA((2,)),
            pltpu.SemaphoreType.DMA((sends,)),
            pltpu.SemaphoreType.DMA((sends,)),
        ],
        compiler_params=pltpu.CompilerParams(
            collective_id=0, has_side_effects=True, vmem_limit_bytes=60 * 1024 * 1024
        ),
        name="gather",
    )(tokens, summary, gain)
    return near.reshape(NEAR, rows, width), every.reshape(-1, width)


def exchange_kernel(
    near, own, sums, w_in, gain_in, tokens, summary, gain, cot,
    grad_tokens, grad_summary, grad_gain, w_out,
    own_v, mid, tok_v, sum_v, cot_v, s_loc, w_loc,
    beside, row_sum, z_slot, x_slot, x_relay, message,
    s_relay, s_direct, s_one, s_slots_x, s_two, s_slots_y, s_sum,
    w_relay, w_direct, w_one, w_slots_two, w_two, w_slots_three, w_three,
    gain_sum, gain_slots, local_sems, send_sems, recv_sems,
):
    at = places()
    x, y, z = at
    x_hi = lax.axis_index("tx_1")
    met = greet(at)
    load = Loader(local_sems)
    part = w_in.shape[1] // 3
    size = [part // 4, part // 16, part // 64]
    s_half = sums.shape[0] // 2

    def rows_of(ref, start, count, q):
        return ref.at[q, pl.ds(pl.multiple_of(start, PACK), count)]

    def s_piece(d, h):
        return sums.at[pl.ds(h * s_half, s_half), d]

    def w_piece(p, q):
        half = size[0] // 2
        return lambda d, h: rows_of(w_in, p * part + d * size[0] + h * half, half, q)

    def own_pieces(piece, axis, slots):
        c = at[axis]
        right, left = lax.rem(c + 1, 4), lax.rem(c + 3, 4)
        wanted = ((right, 0), (left, 1), (c, 0), (c, 1))
        return [load.copy(piece(*wanted[k]), slots.at[k]) for k in range(4)]

    w_ready = {
        (p, q): own_pieces(w_piece(p, q), p, w_loc.at[p, q]) for q in range(2) for p in range(3)
    }
    s_ready = own_pieces(s_piece, 2, s_loc)
    mid_ready = load.copy(near.at[1], mid)
    gain_ready = load.copy(gain_in, gain_sum.at[0])
    rest_ready = [
        load.copy(own, own_v), load.copy(tokens, tok_v), load.copy(summary, sum_v),
        load.copy(cot, cot_v),
    ]
    met()
    link = Sender(send_sems, recv_sems)

    def halo():
        rows = []
        for j in (0, 2, 1):
            up = link.send(near.at[2, j], beside.at[0, j], row_peer(at, 1))
            down = link.send(near.at[0, j], beside.at[1, j], row_peer(at, -1))
            rows.append((j, up, down))
        yield
        mid_ready.wait()
        for j, up, down in rows[:2]:
            up.wait_recv()
            down.wait_recv()
            row_sum[j // 2] = added(mid.at[j], beside.at[0, j], beside.at[1, j]).astype(BF16)
        there = {"tx_0": lax.rem(z + (3 + 2 * x_hi), 4)}
        far = link.send(row_sum.at[x_hi], z_slot, there)
        yield
        far.wait_recv()
        message[...] = added(row_sum.at[1 - x_hi], z_slot).astype(BF16)
        last = send_across(link, at, message, x_relay, (x_slot, x_slot))
        next(last)
        yield
        next(last)
        _, up, down = rows[2]
        up.wait_recv()
        down.wait_recv()
        for copy in rest_ready:
            copy.wait()
        own_v[...] += added(beside.at[0, 1], beside.at[1, 1])
        yield
        for _ in last:
            pass
        hidden_grad = own_v[...] + x_slot[...].astype(F32)
        scale = row_scale(tok_v[...])
        back = norm_back(tok_v[...], scale, gain[...].reshape(1, -1), hidden_grad)
        grad_tokens[...] = (cot_v[...].astype(F32) + back).astype(BF16)

    def summaries():
        yield from scatter_ring(
            link, 2, at, s_piece, s_loc, s_ready, s_relay, s_direct, s_one
        )
        block = summary.shape[0]
        yield from scatter_direct(
            link, 0, at,
            lambda d: s_one.at[lax.rem(d, 2), :, pl.ds((d // 2) * block, block)],
            s_slots_x, s_two,
        )
        yield from scatter_direct(link, 1, at, lambda d: s_two.at[d], s_slots_y, s_sum)
        scale = row_scale(sum_v[...])
        back = norm_back(sum_v[...], scale, gain[...].reshape(1, -1), s_sum[...])
        grad_summary[...] = back.astype(BF16)

    def weights(p, q):
        a, b, c = p, (p + 1) % 3, (p + 2) % 3
        first = p * part
        yield from scatter_ring(
            link, a, at, w_piece(p, q), w_loc.at[p, q], w_ready[p, q],
            w_relay.at[p, q], w_direct.at[p, q], w_one.at[p, q],
        )
        yield from scatter_direct(
            link, b, at,
            lambda d: w_one.at[p, q, d // 2, pl.ds(lax.rem(d, 2) * size[1], size[1])],
            w_slots_two.at[p, q], w_two.at[p, q],
        )
        base = first + at[a] * size[0]
        inner = base + at[b] * size[1]
        yield from scatter_direct(
            link, c, at,
            lambda d: w_two.at[p, q, pl.ds(pl.multiple_of(d * size[2], PACK), size[2])],
            w_slots_three.at[p, q],
            w_three.at[p, q],
        )
        mine = rows_of(w_out, inner + at[c] * size[2], size[2], q)
        copies = [link.send(w_three.at[p, q], mine, peer(c, at, k)) for k in (1, 3, 2)]
        kept = load.copy(w_three.at[p, q], mine)
        yield
        kept.wait()
        for copy in copies:
            copy.wait_recv()
        yield from gather_direct(
            link, b, at, lambda d: rows_of(w_out, base + d * size[1], size[1], q)
        )
        yield from gather_ring(
            link, a, at,
            lambda d: rows_of(w_out, first + d * size[0], size[0], q),
            lambda d, h: rows_of(
                w_out, first + d * size[0] + h * (size[0] // 2), size[0] // 2, q
            ),
        )

    def gains():
        gain_ready.wait()
        for k in range(3):
            yield from scatter_direct(
                link, k, at, lambda d, k=k: gain_sum.at[k], gain_slots.at[k], gain_sum.at[k + 1]
            )
        total = jnp.sum(gain_sum[3], axis=0, keepdims=True)
        grad_gain[...] = total / gain[...].reshape(1, -1)

    first_half = [weights(p, 0) for p in range(3)]
    second_half = [weights(p, 1) for p in range(3)]
    take_turns(
        [halo(), summaries(), *first_half, *second_half, gains()]
    )
    link.drain()


def exchange(
    near_grad, own_grad, sum_grad, w_part, gain_part, tokens, summary, norm_gain, cot
):
    rows, width = own_grad.shape
    block = summary.shape[0]
    vm = pl.BlockSpec(memory_space=pltpu.VMEM)
    far = pl.BlockSpec(memory_space=pltpu.HBM)
    total = w_part.shape[1]
    part = total // 3
    wide = width // 2
    sends = 6 + 5 + 6 + 3 + 3 + 6 * (6 + 3 + 3 + 3 + 3 + 4) + 9
    loads = 24 + 4 + 2 + 4 + 6
    sums = sum_grad.reshape(8, 4, 2 * block, width)
    grad_tokens, grad_summary, gain, w_all = pl.pallas_call(
        exchange_kernel,
        out_shape=(
            jax.ShapeDtypeStruct((rows, width), BF16),
            jax.ShapeDtypeStruct((block, width), BF16),
            jax.ShapeDtypeStruct((1, width), F32),
            jax.ShapeDtypeStruct((2, total, wide), BF16),
        ),
        in_specs=[far] * 7 + [vm, far],
        out_specs=(vm, vm, vm, far),
        scratch_shapes=[
            pltpu.VMEM((rows, width), F32),
            pltpu.VMEM((3, rows, width), BF16),
            pltpu.VMEM((rows, width), BF16),
            pltpu.VMEM((block, width), BF16),
            pltpu.VMEM((rows, width), BF16),
            pltpu.VMEM((4, 4, 2 * block, width), BF16),
            pltpu.VMEM((3, 2, 4, part // 8, wide), BF16),
            pltpu.VMEM((2, 3, rows, width), BF16),
            pltpu.VMEM((2, rows, width), BF16),
            pltpu.VMEM((rows, width), BF16),
            pltpu.VMEM((rows, width), BF16),
            pltpu.VMEM((2, rows, wide), BF16),
            pltpu.VMEM((rows, width), BF16),
            pltpu.VMEM((2, 2, 4, 2 * block, width), BF16),
            pltpu.VMEM((2, 2, 4, 2 * block, width), BF16),
            pltpu.VMEM((2, 4, 2 * block, width), BF16),
            pltpu.VMEM((3, 4, block, width), BF16),
            pltpu.VMEM((4, block, width), BF16),
            pltpu.VMEM((3, block, width), BF16),
            pltpu.VMEM((block, width), F32),
            pltpu.VMEM((3, 2, 2, 2, part // 8, wide), BF16),
            pltpu.VMEM((3, 2, 2, 2, part // 8, wide), BF16),
            pltpu.VMEM((3, 2, 2, part // 8, wide), BF16),
            pltpu.VMEM((3, 2, 3, part // 16, wide), BF16),
            pltpu.VMEM((3, 2, part // 16, wide), BF16),
            pltpu.VMEM((3, 2, 3, part // 64, wide), BF16),
            pltpu.VMEM((3, 2, part // 64, wide), BF16),
            pltpu.VMEM((4, 8, width), F32),
            pltpu.VMEM((3, 3, 8, width), F32),
            pltpu.SemaphoreType.DMA((loads,)),
            pltpu.SemaphoreType.DMA((sends,)),
            pltpu.SemaphoreType.DMA((sends,)),
        ],
        compiler_params=pltpu.CompilerParams(
            collective_id=1, has_side_effects=True, vmem_limit_bytes=60 * 1024 * 1024
        ),
        name="exchange",
    )(
        near_grad.reshape(3, 3, rows, width), own_grad, sums, w_part,
        gain_part, tokens, summary, norm_gain, cot,
    )
    return widen(w_all, grad_tokens, grad_summary, gain)


def widen_kernel(
    narrow, tok_in, sum_in, gain_in, wide, tok_out, sum_out, gain_out,
    held, stage, tok_v, sum_v, gain_v, gain_w, in_sems, out_sems, pass_sems,
):
    taken = [
        pltpu.make_async_copy(tok_in, tok_v, pass_sems.at[0]),
        pltpu.make_async_copy(sum_in, sum_v, pass_sems.at[1]),
        pltpu.make_async_copy(gain_in, gain_v, pass_sems.at[4]),
    ]
    passed = [
        pltpu.make_async_copy(tok_v, tok_out, pass_sems.at[2]),
        pltpu.make_async_copy(sum_v, sum_out, pass_sems.at[3]),
        pltpu.make_async_copy(gain_w, gain_out, pass_sems.at[5]),
    ]
    for copy in taken:
        copy.start()
    rows = stage.shape[1]
    count = narrow.shape[1] // rows
    reads, writes = [], []
    for k in range(count):
        here = pl.ds(k * rows, rows)
        reads.append(pltpu.make_async_copy(narrow.at[:, here], held.at[k], in_sems.at[k]))
        reads[k].start()
    for k in range(count):
        if k >= 3:
            writes[k - 3].wait()
        reads[k].wait()
        half = held.shape[3]
        stage[k % 3, :, :half] = held[k, 0].astype(F32)
        stage[k % 3, :, half:] = held[k, 1].astype(F32)
        here = pl.ds(k * rows, rows)
        writes.append(pltpu.make_async_copy(stage.at[k % 3], wide.at[here], out_sems.at[k % 3]))
        writes[k].start()
        if k == 2:
            for copy in taken:
                copy.wait()
            gain_w[...] = gain_v[...].reshape(gain_w.shape)
            for copy in passed:
                copy.start()
    for copy in writes[-3:] + passed:
        copy.wait()


def widen(narrow, grad_tokens, grad_summary, gain):
    total, width = narrow.shape[1], 2 * narrow.shape[2]
    count = 12
    far = pl.BlockSpec(memory_space=pltpu.HBM)
    return pl.pallas_call(
        widen_kernel,
        out_shape=(
            jax.ShapeDtypeStruct((total, width), F32),
            jax.ShapeDtypeStruct(grad_tokens.shape, BF16),
            jax.ShapeDtypeStruct(grad_summary.shape, BF16),
            jax.ShapeDtypeStruct((width,), F32),
        ),
        in_specs=[far] * 4,
        out_specs=(far,) * 4,
        scratch_shapes=[
            pltpu.VMEM((count, 2, total // count, width // 2), BF16),
            pltpu.VMEM((3, total // count, width), F32),
            pltpu.VMEM(grad_tokens.shape, BF16),
            pltpu.VMEM(grad_summary.shape, BF16),
            pltpu.VMEM((1, width), F32),
            pltpu.VMEM((width,), F32),
            pltpu.SemaphoreType.DMA((count,)),
            pltpu.SemaphoreType.DMA((3,)),
            pltpu.SemaphoreType.DMA((6,)),
        ],
        compiler_params=pltpu.CompilerParams(vmem_limit_bytes=60 * 1024 * 1024),
        name="widen",
    )(narrow, grad_tokens, grad_summary, gain)


def row_scale(rows):
    values = rows.astype(F32)
    return lax.rsqrt(jnp.mean(values * values, axis=-1, keepdims=True) + epsilon)


def normalize(rows, gain):
    scale = row_scale(rows)
    return ((rows.astype(F32) * scale * gain).astype(BF16), scale)


def norm_back(rows, scale, gain, grad_norm):
    values = rows.astype(F32)
    scaled = gain * grad_norm
    return scale * scaled - values * scale**3 * jnp.mean(values * scaled, axis=-1, keepdims=True)


def dot(a, b, ca, cb):
    return lax.dot_general(a, b, (((ca,), (cb,)), ((), ())), preferred_element_type=F32)


def layer_kernel(
    counts, pattern, blocks, near, summ, w_in, tok, cot,
    updated, near_out, own_out, sum_out, w_out, gain_part,
    w, own_v, near_grad, own_grad, sum_grad, w_part, pack_sems, local_sems,
    xp, kp, vp, dkt, dvt, scores, probs, bias, qs, gs, qst, gst, acc, m_ref, l_ref, d_ref,
    q_all, g_all, o_all, dq_all,
):
    rows = tok.shape[0]
    width = tok.shape[1]
    quads = width // CHUNK
    head_size = width // HEADS
    stack = QUAD * rows
    factor = 1.0 / math.sqrt(head_size)
    n_blocks = summ.shape[0] // SBLK
    yp = kp
    zk = scores.at[:, 0:width]
    zv = scores.at[:, width : 2 * width]

    load = Loader(local_sems)
    own_ready = load.copy(near.at[NEAR // 2], own_v)
    w_ready = [load.copy(w_in.at[k], w.at[k]) for k in (0, 3, 1, 2)]

    grid_row = 4 * lax.axis_index("ty_0") + lax.axis_index("ty_1")
    grid_col = 2 * lax.axis_index("tx_0") + lax.axis_index("tx_1")
    meta = []
    for t in range(NEAR):
        r, c = grid_row + (t // 3 - 1), grid_col + (t % 3 - 1)
        inside = (r >= 0) & (r < 8) & (c >= 0) & (c < 8)
        n = counts[jnp.clip(r, 0, 7), jnp.clip(c, 0, 7)]
        meta.append(jnp.where(inside & (pattern[grid_row, grid_col, t] == 1), n, 0))
    for b in range(n_blocks):
        meta.append(jnp.where(blocks[0, 0, b] == 1, 1, 0))
    meta.append(counts[grid_row, grid_col])

    def packed(k, src, at, size):
        return pltpu.make_async_copy(
            src.at[pl.ds(0, size)], xp.at[pl.ds(pl.multiple_of(at, PACK), size)], pack_sems.at[k]
        )

    packs = []
    block_at = []
    total = jnp.int32(0)
    for b in range(n_blocks):
        block_at.append(total)
        flag = meta[NEAR + b]

        src = summ.at[pl.ds(b * SBLK, SBLK)]
        packs.append((flag == 1, packed(NEAR + b, src, total, SBLK)))
        total = total + SBLK * flag
    summ_end = total
    tile_at = []
    for t in range(NEAR):
        tile_at.append(total)
        n = meta[t]

        size = pl.multiple_of(((n + (PACK - 1)) // PACK) * PACK, PACK)
        packs.append((n > 0, packed(t, near.at[t], total, size)))
        total = total + size
    for live, copy in packs:
        pl.when(live)(copy.start)
    xp[pl.ds(pl.multiple_of(total, PACK), CHUNK), :] = jnp.zeros((CHUNK, width), BF16)
    chunks = (total + (CHUNK - 1)) // CHUNK

    place = lax.broadcasted_iota(jnp.int32, bias.shape, 1)
    live = place < summ_end
    for t in range(NEAR):
        live = live | ((place >= tile_at[t]) & (place < tile_at[t] + meta[t]))
    bias[...] = jnp.where(live, 0.0, -1e30)

    own_ready.wait()
    for copy in w_ready[:2]:
        copy.wait()
    own = own_v[...]
    valid = lax.broadcasted_iota(jnp.int32, (rows, width), 0) < meta[NEAR + n_blocks]
    masked = jnp.where(valid, cot[...].astype(F32), 0.0).astype(BF16)
    q_all[...] = (dot(own, w[0], 1, 0).astype(BF16).astype(F32) * factor).astype(BF16)
    g_all[...] = dot(masked, w[3], 1, 1).astype(BF16)

    for copy in w_ready[2:]:
        copy.wait()
    for live, copy in packs:
        pl.when(live)(copy.wait)

    def sweep(body):
        def pair(c, carry):
            body(pl.multiple_of(c * (2 * CHUNK), 2 * CHUNK), 2 * CHUNK)
            return carry

        def four(c, carry):
            body(pl.multiple_of(c * (4 * CHUNK), 4 * CHUNK), 4 * CHUNK)
            return carry

        lax.fori_loop(0, chunks // 4, four, 0)
        lax.fori_loop(chunks // 4 * 2, chunks // 2, pair, 0)

        @pl.when(lax.rem(chunks, 2) == 1)
        def _():
            body(pl.multiple_of((chunks - 1) * CHUNK, CHUNK), CHUNK)

    def project(start, size):
        at = pl.ds(start, size)
        x = xp[at, :]
        kp[at, :] = dot(x, w[1], 1, 0).astype(BF16)
        vp[at, :] = dot(x, w[2], 1, 0).astype(BF16)

    sweep(project)

    lane_head = lax.broadcasted_iota(jnp.int32, (rows, CHUNK), 1) // head_size

    def lanes(values):
        return [values[:, k : k + 128] for k in range(0, values.shape[1], 128)]


    def stack_up(j):
        q_part = q_all[:, j * CHUNK : (j + 1) * CHUNK].astype(F32)
        g_part = g_all[:, j * CHUNK : (j + 1) * CHUNK].astype(F32)
        for i in range(QUAD):
            here = slice(i * rows, (i + 1) * rows)
            qs[j % 2, here, :] = jnp.where(lane_head == i, q_part, 0.0).astype(BF16)
            gs[j % 2, here, :] = jnp.where(lane_head == i, g_part, 0.0).astype(BF16)
        m_ref[...] = jnp.full(m_ref.shape, -3e38, F32)

    def score(j, start, size):
        at = pl.ds(start, size)
        s = dot(qs[j % 2], kp[at, j * CHUNK : (j + 1) * CHUNK], 1, 1) + bias[0:1, at]
        scores[:, at] = s
        most = m_ref[...]
        for part in lanes(s):
            most = jnp.maximum(most, part)
        m_ref[...] = most

    stack_up(0)
    sweep(functools.partial(score, 0))
    for j in range(quads):
        cols = slice(j * CHUNK, (j + 1) * CHUNK)
        q_now, g_now = qs.at[j % 2], gs.at[j % 2]
        m_ref[...] = jnp.broadcast_to(jnp.max(m_ref[...], axis=1, keepdims=True), m_ref.shape)
        l_ref[...] = jnp.zeros(l_ref.shape, F32)
        acc[...] = jnp.zeros(acc.shape, F32)

        def mix(start, size):
            at = pl.ds(start, size)
            m = m_ref[...]
            e = [jnp.exp(part - m) for part in lanes(scores[:, at])]
            total = l_ref[...]
            for part in e:
                total = total + part
            l_ref[...] = total
            e = jnp.concatenate(e, axis=1).astype(BF16)
            probs[:, at] = e
            acc[...] += dot(e, vp[at, cols], 1, 0)

        sweep(mix)
        inv = 1.0 / jnp.sum(l_ref[...], axis=1, keepdims=True)
        out = acc[...] * inv
        d_ref[...] = jnp.broadcast_to(
            jnp.sum(out * g_now[...].astype(F32), axis=1, keepdims=True), d_ref.shape
        )
        picked = jnp.zeros((rows, CHUNK), F32)
        for i in range(QUAD):
            here = slice(i * rows, (i + 1) * rows)
            picked = jnp.where(lane_head == i, out[here], picked)
        o_all[:, cols] = picked.astype(BF16)
        qst[...] = (q_now[...].astype(F32) * inv).astype(BF16).T
        gst[...] = (g_now[...].astype(F32) * inv).astype(BF16).T
        l_ref[...] = jnp.broadcast_to(inv, l_ref.shape)
        acc[...] = jnp.zeros(acc.shape, F32)
        if j + 1 < quads:
            stack_up(j + 1)

        def back(start, size):
            at = pl.ds(start, size)
            e = probs[:, at]
            d = d_ref[...]
            dp = dot(g_now[...], vp[at, cols], 1, 1)
            delta = jnp.concatenate([part - d for part in lanes(dp)], axis=1)
            ds = (e.astype(F32) * delta).astype(BF16)
            acc[...] += dot(ds, kp[at, cols], 1, 0)
            dkt[cols, at] = dot(qst[...], ds, 1, 0).astype(BF16)
            dvt[cols, at] = dot(gst[...], e, 1, 0).astype(BF16)
            if j + 1 < quads:
                score(j + 1, start, size)

        sweep(back)
        inv2 = l_ref[...] * factor
        dq = acc[...] * jnp.concatenate([inv2, inv2], axis=1)
        picked = jnp.zeros((rows, CHUNK), F32)
        for i in range(QUAD):
            here = slice(i * rows, (i + 1) * rows)
            picked = jnp.where(lane_head == i, dq[here], picked)
        dq_all[:, cols] = picked.astype(BF16)

    w_part[0] = dot(own, dq_all[...], 0, 0).astype(BF16)
    w_part[3] = dot(o_all[...], masked, 0, 0).astype(BF16)

    def send_part(k):
        half = width // 2
        for q in range(2):
            src = w_part.at[k, :, q * half : (q + 1) * half]
            sent.append(load.copy(src, w_out.at[q, pl.ds(k * width, width)]))

    sent = []
    send_part(0)
    send_part(3)
    mixed = dot(o_all[...], w[3], 1, 0)
    updated[...] = (tok[...].astype(F32) + jnp.where(valid, mixed, 0.0)).astype(BF16)

    zk[...] = jnp.zeros(zk.shape, F32)
    zv[...] = jnp.zeros(zv.shape, F32)
    own_part = dot(dq_all[...], w[0], 1, 1)
    gain_part[...] = jnp.sum(
        (own_part * own.astype(F32)).reshape(rows // 8, 8, width), axis=0
    )

    def finish(start, size):
        at = pl.ds(start, size)
        x = xp[at, :]
        dk = dkt[:, at]
        dv = dvt[:, at]
        zk[...] += dot(dk, x, 1, 0)
        zv[...] += dot(dv, x, 1, 0)
        yt = dot(w[1], dk, 1, 0) + dot(w[2], dv, 1, 0)
        y = yt.astype(BF16).T
        yp[at, :] = y
        gain_part[...] += jnp.sum(
            (y.astype(F32) * x.astype(F32)).reshape(size // 8, 8, width), axis=0
        )

    sweep(finish)

    w_part[1] = zk[...].astype(BF16).T
    send_part(1)
    w_part[2] = zv[...].astype(BF16).T
    send_part(2)

    row_at = lax.broadcasted_iota(jnp.int32, (rows, width), 0)
    for t in range(NEAR):
        y = yp[pl.ds(pl.multiple_of(tile_at[t], PACK), rows), :].astype(F32)
        y = jnp.where(row_at < meta[t], y, 0.0)
        if t == NEAR // 2:
            own_grad[...] = y + own_part
            sent.append(load.copy(own_grad, own_out))
        else:
            near_grad[t] = y.astype(BF16)
            sent.append(load.copy(near_grad.at[t], near_out.at[t]))
    for b in range(n_blocks):
        y = yp[pl.ds(pl.multiple_of(block_at[b], SBLK), SBLK), :].astype(F32)
        keep = jnp.zeros((SBLK, width), jnp.int32) + meta[NEAR + b]
        sum_grad[b * SBLK : (b + 1) * SBLK, :] = jnp.where(keep == 1, y, 0.0).astype(BF16)
    sent.append(load.copy(sum_grad, sum_out))
    for copy in sent:
        copy.wait()


def layer(counts, pattern, blocks, near, summ, w, tok, cot):
    rows, width = tok.shape
    most = (NEAR * rows + summ.shape[0] + CHUNK - 1) // CHUNK * CHUNK
    stack = QUAD * rows
    vm = pl.BlockSpec(memory_space=pltpu.VMEM)
    sm = pl.BlockSpec(memory_space=pltpu.SMEM)
    far = pl.BlockSpec(memory_space=pl.ANY)
    n_blocks = summ.shape[0] // SBLK
    return pl.pallas_call(
        layer_kernel,
        out_shape=(
            jax.ShapeDtypeStruct((rows, width), BF16),
            jax.ShapeDtypeStruct((NEAR, rows, width), BF16),
            jax.ShapeDtypeStruct((rows, width), F32),
            jax.ShapeDtypeStruct(summ.shape, BF16),
            jax.ShapeDtypeStruct((2, 4 * width, width // 2), BF16),
            jax.ShapeDtypeStruct((8, width), F32),
        ),
        in_specs=[sm] * 3 + [far] * 3 + [vm] * 2,
        out_specs=(vm, far, far, far, far, vm),
        scratch_shapes=[
            pltpu.VMEM((4, width, width), BF16),
            pltpu.VMEM((rows, width), BF16),
            pltpu.VMEM((NEAR, rows, width), BF16),
            pltpu.VMEM((rows, width), F32),
            pltpu.VMEM(summ.shape, BF16),
            pltpu.VMEM((4, width, width), BF16),
            pltpu.SemaphoreType.DMA((NEAR + n_blocks,)),
            pltpu.SemaphoreType.DMA((5 + 8 + NEAR + 2,)),
            pltpu.VMEM((most + CHUNK, width), BF16),
            pltpu.VMEM((most + CHUNK, width), BF16),
            pltpu.VMEM((most, width), BF16),
            pltpu.VMEM((width, most), BF16),
            pltpu.VMEM((width, most), BF16),
            pltpu.VMEM((stack, most), F32),
            pltpu.VMEM((stack, most), BF16),
            pltpu.VMEM((8, most), F32),
            pltpu.VMEM((2, stack, CHUNK), BF16),
            pltpu.VMEM((2, stack, CHUNK), BF16),
            pltpu.VMEM((CHUNK, stack), BF16),
            pltpu.VMEM((CHUNK, stack), BF16),
            pltpu.VMEM((stack, CHUNK), F32),
            pltpu.VMEM((stack, 128), F32),
            pltpu.VMEM((stack, 128), F32),
            pltpu.VMEM((stack, 128), F32),
            pltpu.VMEM((rows, width), BF16),
            pltpu.VMEM((rows, width), BF16),
            pltpu.VMEM((rows, width), BF16),
            pltpu.VMEM((rows, width), BF16),
        ],
        compiler_params=pltpu.CompilerParams(vmem_limit_bytes=63 * 1024 * 1024),
        name="layer",
    )(counts, pattern, blocks, near, summ, w, tok, cot)


def local(
    tokens, summary, counts, tile_pattern, summary_pattern, norm_gain, projections, cotangent
):
    rows, width = tokens.shape[2:]
    token_rows = tokens[0, 0]
    grads_in = cotangent[0, 0]
    near, every = gather(token_rows, summary, norm_gain)
    updated, near_grad, own_grad, sum_grad, w_part, gain_part = layer(
        counts, tile_pattern, summary_pattern, near, every, projections, token_rows, grads_in
    )
    grad_proj, grad_tokens, grad_summary, grad_gain = exchange(
        near_grad, own_grad, sum_grad, w_part, gain_part, token_rows, summary, norm_gain, grads_in
    )
    return (
        updated.reshape(tokens.shape),
        grad_tokens.reshape(tokens.shape),
        grad_summary,
        grad_proj.reshape(projections.shape),
        grad_gain,
    )


def solution(mesh):
    finer = Mesh(
        mesh.devices.reshape(2, 4, 4, 2, mesh.shape["slide"]),
        ("ty_0", "ty_1", "tx_0", "tx_1", "slide"),
    )
    return jax.shard_map(
        local,
        mesh=finer,
        in_specs=(
            P(SLIDE_TY, TX, None, None),
            P(SLIDE_TY_TX, None),
            P("slide", None),
            P("slide", None, None),
            P(SLIDE_TY, TX, None),
            P(),
            P(),
            P(SLIDE_TY, TX, None, None),
        ),
        out_specs=(
            P(SLIDE_TY, TX, None, None),
            P(SLIDE_TY, TX, None, None),
            P(SLIDE_TY_TX, None),
            P("slide", None, None),
            P("slide"),
        ),
        check_vma=False,
    )
```
